32 devices in a mesh: seq: 4 (over x, core), expert: 8 (over z, y).
Axes of the slice: x: 2, y: 2, z: 4, core: 2. Of those that a mesh axis runs over, the one named last changes fastest.
Arguments:
- tokens: bfloat16 [8, 512, 2048], P('expert', 'seq'), may hold values from -6 to 6
- lengths: int32 [8, 4], P('expert'), may hold values from 1 to 512, as said below
- routes: int32 [8, 512, 8], P('expert', 'seq'), may hold values from 0 to 15, all different within a row; in each aligned block of 128 rows (0 to 127, 128 to 255, ..., all dimensions but the last counted through in order) at most 64 rows name the same one
- gain_attn: float32 [2048], replicated, may hold values from 0.5 to 1.5
- w_query: bfloat16 [2048, 2048], P(('seq', 'expert')), may hold values from -0.125 to 0.125
- w_key: bfloat16 [2048, 2048], P(('seq', 'expert')), may hold values from -0.125 to 0.125
- w_value: bfloat16 [2048, 2048], P(('seq', 'expert')), may hold values from -0.125 to 0.125
- gain_query: float32 [2048], replicated, may hold values from 0.5 to 1.5
- gain_key: float32 [2048], replicated, may hold values from 0.5 to 1.5
- w_out: bfloat16 [2048, 2048], P(('seq', 'expert')), may hold values from -0.75 to 0.75
- gain_mlp: float32 [2048], replicated, may hold values from 0.5 to 1.5
- router: bfloat16 [2048, 16], replicated, may hold values from -0.0625 to 0.0625
- w_gate: bfloat16 [16, 2048, 1024], P('expert'), may hold values from -0.125 to 0.125
- w_up: bfloat16 [16, 2048, 1024], P('expert'), may hold values from -0.125 to 0.125
- w_down: bfloat16 [16, 1024, 2048], P('expert'), may hold values from -3 to 3
- cotangent: bfloat16 [8, 512, 2048], P('expert', 'seq'), may hold values from -6 to 6
Outputs:
- mixed: bfloat16 [8, 512, 2048], P('expert', 'seq')
- d_tokens: float32 [8, 512, 2048], P('expert', 'seq')
- d_gain_attn: float32 [2048], replicated
- d_w_query: float32 [2048, 2048], P(('seq', 'expert'))
- d_w_key: float32 [2048, 2048], P(('seq', 'expert'))
- d_w_value: float32 [2048, 2048], P(('seq', 'expert'))
- d_gain_query: float32 [2048], replicated
- d_gain_key: float32 [2048], replicated
- d_w_out: float32 [2048, 2048], P(('seq', 'expert'))
- d_gain_mlp: float32 [2048], replicated
- d_router: float32 [2048, 16], replicated
- d_w_gate: float32 [16, 2048, 1024], P('expert', 'seq')
- d_w_up: float32 [16, 2048, 1024], P('expert', 'seq')
- d_w_down: float32 [16, 1024, 2048], P('expert', 'seq')
The draws below stay inside these ranges and needn't reach their ends.
Inputs may be any that keep to these rules, and one draw needn't show every extreme that they name: `routes`: in the tokens of one device no expert is named by more than 64 of them. Each pack's 4 document lengths are positive and add up to 512.
All inputs are finite; a program needn't handle non-finite values.
Results may differ from the reference program's by a relative error of at most 0.02.
Values may be sent and summed in bfloat16 or wider, within the bound.
A program may use at most 320 MiB of HBM per device.

```python
import math
import jax
import jax.numpy as jnp
import numpy as np
from jax import lax

D = 2048
HEADS = 16
HD = 128
FF = 1024
TOP = 8
MOST = 64
DOCS = 4
TOK_DEV = 128
EXPERTS = 16
LENGTH = 512
PACKS = 8
TOKENS = 4096
N_SEQ = 4
N_EXPERT = 8


def draw_lengths(key, part):
    key = jax.random.fold_in(key, 11)
    small_key, pick_key = jax.random.split(key)
    smaller = jax.random.randint(small_key, (PACKS, DOCS), 1, TOK_DEV // DOCS + 1, dtype=jnp.int32)
    picked = jax.random.randint(pick_key, (PACKS, 1), 0, DOCS, dtype=jnp.int32)
    places = jnp.arange(DOCS, dtype=jnp.int32)[None, :]
    larger = (places == picked).astype(jnp.int32)
    single = (places == (picked + 1) % DOCS).astype(jnp.int32)
    smaller = smaller * (1 - single) + single
    others = smaller * (1 - larger)
    return others + larger * (LENGTH - jnp.sum(others, axis=1, keepdims=True))


def block_scale(rng, shape, cuts, low, high):
    def one(axis_at, parts):
        heights = jax.random.uniform(jax.random.fold_in(jax.random.fold_in(rng, 6), axis_at), (parts,), jnp.float32, low / len(cuts), high / len(cuts))
        return jnp.repeat(jnp.exp(heights), shape[axis_at] // parts).reshape((-1,) + (1,) * (len(shape) - axis_at - 1))

    factor_of = one(*cuts[0])
    for cut in cuts[1:]:
        factor_of = factor_of * one(*cut)
    return factor_of


def shared_out(key, own, number, rows, amount, top, reach, skew):
    order = jax.random.permutation(key, amount)
    crowded, common = load_shares(amount, rows * top, reach, skew, True), load_shares(amount, rows * top, reach, skew, False)
    places = jnp.arange(amount)

    def named(sizes, turn):
        used = int((sizes > 0).sum())
        fixed = max(1, used // 4)
        moved = fixed + (places - fixed + turn * (used - fixed)) % max(1, amount - fixed)
        return jnp.zeros((amount,), jnp.int32).at[order[jnp.where(places < fixed, places, moved)]].set(jnp.asarray(sizes, jnp.int32))

    sizes = jnp.where(number % 4 == 0, named(crowded, number // 4), named(common, number - number // 4 - 1))
    mixed = jax.random.permutation(jax.random.fold_in(own, 3), amount)
    donor, taker = mixed[0:amount // 2 * 2:2], mixed[1:amount // 2 * 2:2]
    margin = jnp.minimum(sizes[donor] - 1, reach - sizes[taker]) // 2
    margin = jnp.where((donor == order[0]) | (taker == order[0]) | (sizes[taker] == 0), 0, jnp.maximum(margin, 0))
    moved = jax.random.randint(jax.random.fold_in(own, 4), (amount // 2,), 0, 1 << 20) % (margin + 1)
    sizes = sizes.at[donor].add(-moved).at[taker].add(moved)
    items = jnp.searchsorted(jnp.cumsum(sizes), jnp.arange(rows * top), side="right").astype(jnp.int32)
    listing = items.reshape(top, rows).T
    listing = listing[jax.random.permutation(jax.random.fold_in(own, 1), rows)]
    turn = jax.random.randint(jax.random.fold_in(own, 2), (rows, 1), 0, top)
    return jnp.take_along_axis(listing, (jnp.arange(top)[None, :] + turn) % top, axis=1)


def load_shares(amount, total, bound, skew, full):
    loads = [(1 << 20) // math.isqrt(standing ** skew) + 1 for standing in range(1, amount + 1)]
    largest = bound if full else min(bound, max(-(-total // amount), total * loads[0] // sum(loads)))
    least = 1 if total - largest >= amount - 1 else 0
    holding, surplus = [largest] + [least] * (amount - 1), total - largest - least * (amount - 1)
    while surplus > 0:
        free = [i for i in range(1, amount) if holding[i] < largest] or [i for i in range(1, amount) if holding[i] < bound]
        mass, left = sum([loads[i] for i in free]), surplus
        for i in free:
            more = min(bound - holding[i], max(1, left * loads[i] // mass), surplus)
            holding[i] = holding[i] + more
            surplus = surplus - more
    return np.array(holding)


def centred(own_key, dims, deviation, limit, cuts=(), held_as=jnp.bfloat16):
    factor_of = block_scale(own_key, dims, cuts, -0.22, 0.18) if cuts else 1.0
    values = jax.random.normal(own_key, dims, jnp.float32) * deviation * factor_of
    return jnp.minimum(jnp.maximum(values, -limit), limit).astype(held_as)


def setup_inputs(seed: int = 0) -> dict:
    keys = jax.random.split(jax.random.key(seed), 17)
    tokens = centred(keys[0], (PACKS, LENGTH, D), 1.0, 6.0, ((0, 8), (1, 4)))
    lengths = draw_lengths(jax.random.fold_in(keys[16], 71), 0)
    routes_keys = jax.random.split(jax.random.fold_in(keys[2], 1), PACKS * LENGTH // TOK_DEV)
    routes_turns = jax.random.permutation(jax.random.fold_in(keys[2], 3), PACKS * LENGTH // TOK_DEV)
    routes = jax.vmap(lambda own, number: shared_out(jax.random.fold_in(keys[2], 2), own, number, TOK_DEV, EXPERTS, TOP, MOST, 3))(routes_keys, routes_turns).reshape((PACKS, LENGTH, TOP))
    gain_attn = jnp.clip(1.0 + 0.1 * jax.random.normal(keys[3], (D,), jnp.float32), 0.5, 1.5)
    w_query = centred(keys[4], (D, D), D ** -0.5, 0.125, ((0, 32),))
    w_key = centred(keys[5], (D, D), D ** -0.5, 0.125, ((0, 32),))
    w_value = centred(keys[6], (D, D), D ** -0.5, 0.125, ((0, 32),))
    gain_query = jnp.clip(1.0 + 0.1 * jax.random.normal(keys[7], (D,), jnp.float32), 0.5, 1.5)
    gain_key = jnp.clip(1.0 + 0.1 * jax.random.normal(keys[8], (D,), jnp.float32), 0.5, 1.5)
    w_out = centred(keys[9], (D, D), (max(D // 32, 1)) ** -0.5, 0.75, ((0, 32),))
    gain_mlp = jnp.clip(1.0 + 0.1 * jax.random.normal(keys[10], (D,), jnp.float32), 0.5, 1.5)
    router = centred(keys[11], (D, EXPERTS), (4 * D) ** -0.5, 0.0625)
    w_gate = centred(keys[12], (EXPERTS, D, FF), D ** -0.5, 0.125, ((0, 8),))
    w_up = centred(keys[13], (EXPERTS, D, FF), D ** -0.5, 0.125, ((0, 8),))
    w_down = centred(keys[14], (EXPERTS, FF, D), (max(FF // 256, 1)) ** -0.5, 3.0, ((0, 8),))
    cotangent = centred(keys[15], (PACKS, LENGTH, D), 1.0, 6.0, ((0, 8), (1, 4)))
    return dict(tokens=tokens, lengths=lengths, routes=routes, gain_attn=gain_attn, w_query=w_query, w_key=w_key, w_value=w_value, gain_query=gain_query, gain_key=gain_key, w_out=w_out, gain_mlp=gain_mlp, router=router, w_gate=w_gate, w_up=w_up, w_down=w_down, cotangent=cotangent)


@jax.custom_vjp
def low(v):
    return lax.optimization_barrier(v.astype(jnp.bfloat16)).astype(jnp.float32)

@jax.custom_vjp
def low_back(v):
    return v

def low_keep(v):
    return (low(v), None)

def low_pass(kept, grad):
    return (grad,)

def back_keep(v):
    return (v, None)

def back_low(kept, grad):
    return (low(grad),)
low.defvjp(low_keep, low_pass)
low_back.defvjp(back_keep, back_low)
norm_eps = 1e-05
masked_score = -1e+30

def product(left_matrix, right_matrix):
    return jnp.dot(left_matrix, right_matrix, precision=lax.Precision.HIGHEST, preferred_element_type=jnp.float32)

def rms_norm(values, norm_gain):
    return values * lax.rsqrt(lax.optimization_barrier(jnp.mean(values * values, axis=-1, keepdims=True)) + norm_eps) * norm_gain

def rotate(values, offsets):
    half_dim = values.shape[-1] // 2
    inverse = 10000.0 ** (-jnp.arange(half_dim, dtype=jnp.float32) / half_dim)
    angles = offsets.astype(jnp.float32)[:, None] * inverse[None, :]
    cosine = jnp.cos(angles)[:, None, :]
    sine_table = jnp.sin(angles)[:, None, :]
    first_half = values[..., :half_dim]
    second = values[..., half_dim:]
    return jnp.concatenate([first_half * cosine - second * sine_table, second * cosine + first_half * sine_table], axis=-1)

def doc_tables(lengths_row, places):
    doc_ends = jnp.cumsum(lengths_row)
    passed = (places[:, None] >= doc_ends[None, :]).astype(jnp.int32)
    return (lax.optimization_barrier(jnp.sum(passed, axis=1)), places - lax.optimization_barrier(jnp.sum(passed * lengths_row[None, :], axis=1)))

def reference(tokens, lengths, routes, gain_attn, w_query, w_key, w_value, gain_query, gain_key, w_out, gain_mlp, router, w_gate, w_up, w_down, cotangent):
    places = jnp.arange(LENGTH, dtype=jnp.int32)
    doc_index, offsets = jax.vmap(lambda lengths_row: doc_tables(lengths_row, places))(lengths)
    allowed = (doc_index[:, :, None] == doc_index[:, None, :]) & (places[None, None, :] <= places[None, :, None])
    flat_routes = routes.reshape(TOKENS, TOP)
    chosen_int = lax.optimization_barrier(jnp.sum((flat_routes[:, :, None] == jnp.arange(EXPERTS, dtype=jnp.int32)[None, None, :]).astype(jnp.int32), axis=1))
    chosen = chosen_int.astype(jnp.float32)
    capacity = min(TOKENS, MOST * N_SEQ * N_EXPERT)
    score_scale = HD ** (-0.5)

    def forward(inputs, attn_gain, query_w, key_w, value_w, query_gain, key_gain, out_w, mlp_gain, router_w, gate_w, up_w, down_w):

        def attend(packed):
            pack_rows, offset_row, allowed_block = packed
            normed = low(rms_norm(pack_rows, attn_gain))
            queries = low_back(product(normed, query_w))
            key_rows = low_back(product(normed, key_w))
            value_heads = low_back(low(product(normed, value_w))).reshape(LENGTH, HEADS, HD)
            queries = low(rotate(rms_norm(queries, query_gain).reshape(LENGTH, HEADS, HD), offset_row))
            key_heads = low(rotate(rms_norm(key_rows, key_gain).reshape(LENGTH, HEADS, HD), offset_row))
            scores = low_back(jnp.einsum('qhd,khd->hqk', queries, key_heads, precision=lax.Precision.HIGHEST) * score_scale)
            scores = jnp.where(allowed_block[None], scores, masked_score)
            attn_probs = low(jax.nn.softmax(scores, axis=-1))
            attended = jnp.einsum('hqk,khd->qhd', attn_probs, value_heads, precision=lax.Precision.HIGHEST).reshape(LENGTH, D)
            attended = low_back(low(attended))
            return pack_rows + low_back(product(attended, out_w))
        hidden = lax.map(jax.checkpoint(attend), (inputs, offsets, allowed))
        flat_hidden = hidden.reshape(TOKENS, D)
        normed2 = low(rms_norm(flat_hidden, mlp_gain))
        router_probs = jax.nn.softmax(low_back(product(normed2, router_w)), axis=-1)
        weights = router_probs * chosen

        def expert_step(summed, packed):
            gate_e, up_e, down_e, column, picked = packed
            picked_rows = jnp.argsort(1 - picked, stable=True)[:capacity].astype(jnp.int32)
            routed = low_back(normed2[picked_rows])
            gate_pre = low_back(product(routed, gate_e))
            up_pre = low_back(product(routed, up_e))
            active = low(jax.nn.silu(gate_pre) * up_pre)
            result = low_back(low(product(active, down_e)))
            return (summed.at[picked_rows].add(column[picked_rows][:, None] * result), None)
        summed, unused = lax.scan(jax.checkpoint(expert_step), jnp.zeros((TOKENS, D), jnp.float32), (gate_w, up_w, down_w, weights.T, chosen_int.T))
        return (flat_hidden + summed).reshape(PACKS, LENGTH, D)
    floats = [argument.astype(jnp.float32) for argument in (tokens, gain_attn, w_query, w_key, w_value, gain_query, gain_key, w_out, gain_mlp, router, w_gate, w_up, w_down)]
    output, pullback = jax.vjp(forward, *floats)
    gradients = pullback(cotangent.astype(jnp.float32))
    return (output.astype(jnp.bfloat16), gradients[0], gradients[1], gradients[2], gradients[3], gradients[4], gradients[5], gradients[6], gradients[7], gradients[8], gradients[9], gradients[10], gradients[11], gradients[12])
```

```python
from functools import partial

import jax
import jax.numpy as jnp
from jax import lax
from jax.sharding import PartitionSpec as P

HEADS = 16
MOST = 64
BF = jnp.bfloat16
F32 = jnp.float32

norm_eps = 1e-05
masked_score = -1e30


def product(left, right):
    return jnp.dot(left, right, preferred_element_type=F32)


def rms_norm(values, norm_gain):
    return (
        values * lax.rsqrt(jnp.mean(values * values, axis=-1, keepdims=True) + norm_eps) * norm_gain
    )


def swap(value, axis):
    n = lax.axis_size(axis)
    return lax.ppermute(value, axis, [(i, i ^ 1) for i in range(n)])


def shift(value, axis):
    n = lax.axis_size(axis)
    return lax.ppermute(value, axis, [(i, (i + 2) % n) for i in range(n)])


def flip(value, axis, delta):
    n = lax.axis_size(axis)
    return lax.ppermute(value, axis, [(i, i ^ delta) for i in range(n)])


def owners(axis):
    n = lax.axis_size(axis)
    me = lax.axis_index(axis)
    outer, inner = me // 2, me % 2
    return [((outer - i) % (n // 2)) * 2 + (inner ^ b) for i in range(n // 2) for b in range(2)]


def gather_blocks(value, axis):
    blocks = []
    current = value
    for i in range(lax.axis_size(axis) // 2):
        if i:
            current = shift(current, axis)
        blocks += [current, swap(current, axis)]
    return blocks


def add_low(left, right):
    return (left.astype(F32) + right.astype(F32)).astype(BF)


def scatter_sum(blocks, axis):
    outer_count = lax.axis_size(axis) // 2
    pairs = {}
    for t in list(range(1, outer_count)) + [0]:
        arrived = swap(blocks[2 * t + 1], axis)
        pairs[t] = blocks[2 * t].astype(F32) + arrived.astype(F32)
    total = pairs[1 % outer_count]
    for t in range(1, outer_count):
        arrived = shift(total.astype(BF), axis)
        total = arrived.astype(F32) + pairs[(t + 1) % outer_count]
    return total


def all_sum(value, axes):
    for axis in axes:
        delta = 1
        while delta < lax.axis_size(axis):
            value = value + flip(value, axis, delta)
            delta *= 2
    return value


def exchange(parts, axis):
    n = lax.axis_size(axis)
    me = lax.axis_index(axis)
    out = parts
    for delta in range(1, n):
        other = me ^ delta
        got = flip(lax.dynamic_index_in_dim(parts, other, 0, keepdims=False), axis, delta)
        out = lax.dynamic_update_index_in_dim(out, got, other, 0)
    return out


def after(value, *others):
    return lax.optimization_barrier((value,) + others)[0]


def local(
    tokens,
    lengths,
    routes,
    gain_attn,
    w_query,
    w_key,
    w_value,
    gain_query,
    gain_key,
    w_out,
    gain_mlp,
    router,
    w_gate,
    w_up,
    w_down,
    cotangent,
):
    seq_count = lax.axis_size("seq")
    group_count = lax.axis_size("expert")
    seq_me = lax.axis_index("seq")
    group_me = lax.axis_index("expert")
    tok_rows, width = tokens.shape[1], tokens.shape[2]
    head_dim = width // HEADS
    heads = HEADS // seq_count
    cols = width // seq_count
    wrows = w_query.shape[0]
    length = tok_rows * seq_count
    experts_local = w_gate.shape[0]
    total_experts = experts_local * group_count
    slots = MOST
    score_scale = head_dim ** (-0.5)
    inputs = tokens[0].astype(F32)

    seq_owners = jnp.stack(owners("seq"))
    places = (seq_owners[:, None] * tok_rows + jnp.arange(tok_rows)[None, :]).reshape(length)
    doc_ends = jnp.cumsum(lengths[0])
    passed = (places[:, None] >= doc_ends[None, :]).astype(jnp.int32)
    docs = jnp.sum(passed, axis=1)
    offsets = places - jnp.sum(passed * lengths[0][None, :], axis=1)
    allowed = (docs[:, None] == docs[None, :]) & (places[None, :] <= places[:, None])
    half = head_dim // 2
    inverse = 10000.0 ** (-jnp.arange(half, dtype=F32) / half)
    angles = offsets.astype(F32)[:, None] * inverse[None, :]
    cosine = jnp.cos(angles)[:, None, :]
    sine = jnp.sin(angles)[:, None, :]

    def turn(values, sine_table):
        first, second = values[..., :half], values[..., half:]
        return jnp.concatenate(
            [first * cosine - second * sine_table, second * cosine + first * sine_table], axis=-1
        )

    w_three = jnp.stack([w_query, w_key, w_value], axis=1)
    w_parts = w_three.reshape(wrows, 3, seq_count, cols).transpose(2, 0, 1, 3)
    w_mine = exchange(w_parts.reshape(seq_count, wrows, 3 * cols), "seq")
    group_owners = owners("expert")
    w_blocks = gather_blocks(w_mine, "expert")
    w_cols = jnp.zeros((seq_count, group_count, wrows, 3 * cols), BF)
    for owner, block in zip(group_owners, w_blocks):
        w_cols = lax.dynamic_update_slice(w_cols, block[:, None], (0, owner, 0, 0))
    w_cols = w_cols.reshape(width, 3 * cols)
    out_blocks = gather_blocks(after(w_out, w_blocks[-1]), "expert")
    w_rows = jnp.zeros((group_count, wrows, width), BF)
    for owner, block in zip(group_owners, out_blocks):
        w_rows = lax.dynamic_update_slice(w_rows, block[None], (owner, 0, 0))
    w_rows = w_rows.reshape(cols, width)

    normed, attn_norm_back = jax.vjp(rms_norm, inputs, gain_attn)
    normed_all = jnp.concatenate(gather_blocks(normed.astype(BF), "seq"), axis=0)
    raw = product(normed_all, w_cols)
    query_raw, key_raw = raw[:, :cols], raw[:, cols : 2 * cols]
    value_low = raw[:, 2 * cols :].astype(BF).reshape(length, heads, head_dim)

    def row_sums(left, right):
        sums = jnp.stack([jnp.sum(left, axis=1), jnp.sum(right, axis=1)])
        sums = sums.reshape(2, seq_count, tok_rows)
        ordered = jnp.zeros_like(sums).at[:, seq_owners].set(sums)
        return lax.psum(ordered, "seq")[:, seq_owners].reshape(2, length) / width

    inv_rms = lax.rsqrt(row_sums(query_raw**2, key_raw**2) + norm_eps)
    gain_q = lax.dynamic_slice_in_dim(gain_query, seq_me * cols, cols)
    gain_k = lax.dynamic_slice_in_dim(gain_key, seq_me * cols, cols)
    query_unit = query_raw * inv_rms[0][:, None]
    key_unit = key_raw * inv_rms[1][:, None]
    query_low = turn((query_unit * gain_q).reshape(length, heads, head_dim), sine).astype(BF)
    key_low = turn((key_unit * gain_k).reshape(length, heads, head_dim), sine).astype(BF)
    scores = jnp.einsum("qhd,khd->hqk", query_low, key_low, preferred_element_type=F32)
    scores = jnp.where(allowed[None], scores * score_scale, masked_score)
    top_score = jnp.max(scores, axis=-1, keepdims=True)
    weights = jnp.exp(scores - top_score)
    probs = weights / jnp.sum(weights, axis=-1, keepdims=True)
    probs_low = probs.astype(BF)
    attended = jnp.einsum("hqk,khd->qhd", probs_low, value_low, preferred_element_type=F32)
    attended_low = attended.reshape(length, cols).astype(BF)
    hidden_parts = product(attended_low, w_rows).astype(BF).reshape(seq_count, tok_rows, width)
    hidden = inputs + scatter_sum([hidden_parts[i] for i in range(seq_count)], "seq")

    normed2, mlp_norm_back = jax.vjp(rms_norm, hidden, gain_mlp)
    normed2_low = normed2.astype(BF)

    order = jnp.stack(group_owners)
    picks = lax.all_gather(routes[0], "expert", axis=0)[order]
    first_expert = group_me * experts_local
    local_ids = first_expert + jnp.arange(experts_local, dtype=jnp.int32)
    hit = jnp.any(picks[:, None, :, :] == local_ids[None, :, None, None], axis=-1)
    before = (jnp.arange(tok_rows)[:, None] < jnp.arange(tok_rows)[None, :]).astype(BF)
    rank = jnp.einsum("ejt,tu->eju", hit.astype(BF), before, preferred_element_type=F32)
    slot_ids = jnp.arange(slots, dtype=jnp.int32)
    chosen = hit[:, :, None, :] & (rank.astype(jnp.int32)[:, :, None, :] == slot_ids[None, None, :, None])
    chosen_low = chosen.astype(BF)

    normed2_all = jnp.stack(gather_blocks(normed2_low, "expert"))
    cot_all = jnp.stack(gather_blocks(after(cotangent[0], out_blocks[-1]), "expert"))
    logits_all = jnp.einsum("etd,dn->etn", normed2_all, router, preferred_element_type=F32)
    probs_all = jax.nn.softmax(logits_all, axis=-1)
    mine = lax.dynamic_slice_in_dim(probs_all, first_expert, experts_local, axis=2)
    gate_rows = jnp.einsum(
        "ejmt,etj->jem", chosen.astype(F32), mine, precision=lax.Precision.HIGHEST
    )[..., None]

    def pick_rows(values):
        return jnp.einsum("ejmt,etd->jemd", chosen_low, values, preferred_element_type=F32).astype(BF)

    def place_rows(values):
        return jnp.einsum("ejmt,jemd->etd", chosen_low, values, preferred_element_type=F32).astype(BF)

    routed = pick_rows(normed2_all)
    cot_rows = pick_rows(cot_all)

    def each(left, right, how):
        return jnp.einsum(how, left, right, preferred_element_type=F32)

    gate_pre = each(routed, w_gate, "jemd,jdf->jemf")
    up_pre = each(routed, w_up, "jemd,jdf->jemf")
    sigmoid_gate = jax.nn.sigmoid(gate_pre)
    silu_gate = gate_pre * sigmoid_gate
    active = silu_gate * up_pre
    active_low = active.astype(BF)
    grad_unit = each(cot_rows, w_down, "jemd,jfd->jemf")
    grad_gate_rows = jnp.sum(grad_unit * active_low.astype(F32), axis=-1)
    grad_active = grad_unit * gate_rows
    grad_gate_low = (
        grad_active * up_pre * sigmoid_gate * (1.0 + gate_pre * (1.0 - sigmoid_gate))
    ).astype(BF)
    grad_up_low = (grad_active * silu_gate).astype(BF)
    grad_routed = each(grad_gate_low, w_gate, "jemf,jdf->jemd")
    grad_routed = (grad_routed + each(grad_up_low, w_up, "jemf,jdf->jemd")).astype(BF)
    grad_parts = place_rows(grad_routed)
    grad_normed2 = scatter_sum([grad_parts[i] for i in range(group_count)], "expert")
    grad_probs_parts = jnp.einsum(
        "ejmt,jem->etj", chosen.astype(F32), grad_gate_rows, precision=lax.Precision.HIGHEST
    )
    to_owner = jnp.zeros_like(grad_probs_parts).at[order].set(grad_probs_parts)
    grad_probs = lax.all_to_all(to_owner, "expert", split_axis=0, concat_axis=0, tiled=True)
    grad_probs = grad_probs.transpose(1, 0, 2).reshape(tok_rows, total_experts)

    expert_out = each(active_low, w_down, "jemf,jfd->jemd") * gate_rows
    out_parts = place_rows(expert_out.astype(BF))
    out_parts = after(out_parts, grad_normed2)
    mixed = hidden + scatter_sum([out_parts[i] for i in range(group_count)], "expert")

    active_scaled = (active_low.astype(F32) * gate_rows).astype(BF)

    def expert_grad(left, right):
        grad = jnp.einsum("jemd,jemf->jdf", left, right, preferred_element_type=F32).astype(BF)
        rows = grad.shape[1] // seq_count
        grad = grad.reshape(experts_local, seq_count, rows, grad.shape[2])
        return scatter_sum(
            [lax.dynamic_index_in_dim(grad, o, 1, keepdims=False) for o in owners("seq")], "seq"
        )

    d_w_gate = expert_grad(routed, grad_gate_low)
    d_w_up = expert_grad(routed, grad_up_low)
    d_w_down = expert_grad(active_scaled, cot_rows)

    router_probs, softmax_back = jax.vjp(
        partial(jax.nn.softmax, axis=-1), product(normed2_low, router)
    )
    (grad_logits,) = softmax_back(grad_probs)
    grad_logits_low = grad_logits.astype(BF)
    grad_router = jnp.einsum("td,te->ed", normed2_low, grad_logits_low, preferred_element_type=F32)
    grad_normed2 = grad_normed2 + jnp.einsum(
        "te,de->td", grad_logits_low, router, preferred_element_type=F32
    )
    grad_hidden_part, grad_gain_mlp = mlp_norm_back(grad_normed2)
    grad_hidden = cotangent[0].astype(F32) + grad_hidden_part

    grad_hidden_all = jnp.concatenate(gather_blocks(grad_hidden.astype(BF), "seq"), axis=0)
    grad_attended = jnp.einsum(
        "te,de->td", grad_hidden_all, w_rows, preferred_element_type=F32
    ).astype(BF)
    grad_attended = grad_attended.reshape(length, heads, head_dim)
    grad_w_out = jnp.einsum(
        "td,te->de", attended_low, grad_hidden_all, preferred_element_type=F32
    ).astype(BF).reshape(group_count, wrows, width)
    grad_probs_attn = jnp.einsum(
        "qhd,khd->hqk", grad_attended, value_low, preferred_element_type=F32
    )
    row_dot = jnp.sum(probs * grad_probs_attn, axis=-1, keepdims=True)
    grad_scores = (probs * (grad_probs_attn - row_dot)).astype(BF)
    grad_query = jnp.einsum("hqk,khd->qhd", grad_scores, key_low, preferred_element_type=F32)
    grad_key = jnp.einsum("hqk,qhd->khd", grad_scores, query_low, preferred_element_type=F32)
    grad_value = jnp.einsum("hqk,qhd->khd", probs_low, grad_attended, preferred_element_type=F32)
    grad_query = turn(grad_query * score_scale, -sine).reshape(length, cols)
    grad_key = turn(grad_key * score_scale, -sine).reshape(length, cols)
    grad_gain_query = jnp.sum(grad_query * query_unit, axis=0)
    grad_gain_key = jnp.sum(grad_key * key_unit, axis=0)
    grad_query_g, grad_key_g = grad_query * gain_q, grad_key * gain_k
    means = row_sums(grad_query_g * query_unit, grad_key_g * key_unit)
    grad_query_low = (
        inv_rms[0][:, None] * (grad_query_g - query_unit * means[0][:, None])
    ).astype(BF)
    grad_key_low = (inv_rms[1][:, None] * (grad_key_g - key_unit * means[1][:, None])).astype(BF)
    grad_value_low = grad_value.reshape(length, cols).astype(BF)
    grad_three = jnp.concatenate([grad_query_low, grad_key_low, grad_value_low], axis=1)
    grad_normed_parts = jnp.einsum(
        "te,de->td", grad_three, w_cols, preferred_element_type=F32
    ).astype(BF).reshape(seq_count, tok_rows, width)
    grad_normed = scatter_sum([grad_normed_parts[i] for i in range(seq_count)], "seq")
    grad_inputs_part, grad_gain_attn = attn_norm_back(grad_normed)
    d_tokens = grad_hidden + grad_inputs_part

    grad_w_three = jnp.einsum(
        "td,te->de", normed_all, grad_three, preferred_element_type=F32
    ).astype(BF).reshape(seq_count, group_count, wrows, 3 * cols)
    d_w_out = scatter_sum(
        [lax.dynamic_index_in_dim(grad_w_out, o, 0, keepdims=False) for o in group_owners], "expert"
    )
    d_three = scatter_sum(
        [lax.dynamic_index_in_dim(grad_w_three, o, 1, keepdims=False) for o in group_owners],
        "expert",
    )
    d_three = exchange(d_three.astype(BF), "seq")
    d_three = d_three.reshape(seq_count, wrows, 3, cols).transpose(2, 1, 0, 3)
    d_three = d_three.reshape(3, wrows, width).astype(F32)

    def full(value):
        return lax.dynamic_update_slice(jnp.zeros((width,), F32), value, (seq_me * cols,))

    axes = ("seq", "expert")
    early = all_sum(jnp.concatenate([grad_router, grad_gain_mlp[None]]), axes)
    late = all_sum(jnp.stack([full(grad_gain_query), full(grad_gain_key), grad_gain_attn]), axes)
    return (
        mixed.astype(BF)[None],
        d_tokens[None],
        late[2],
        d_three[0],
        d_three[1],
        d_three[2],
        late[0],
        late[1],
        d_w_out,
        early[total_experts],
        early[:total_experts].T,
        d_w_gate,
        d_w_up,
        d_w_down,
    )


def solution(mesh):
    return jax.shard_map(
        local,
        mesh=mesh,
        in_specs=(
            P("expert", "seq", None),
            P("expert", None),
            P("expert", "seq", None),
            P(),
            P(("seq", "expert"), None),
            P(("seq", "expert"), None),
            P(("seq", "expert"), None),
            P(),
            P(),
            P(("seq", "expert"), None),
            P(),
            P(),
            P("expert", None, None),
            P("expert", None, None),
            P("expert", None, None),
            P("expert", "seq", None),
        ),
        out_specs=(
            P("expert", "seq", None),
            P("expert", "seq", None),
            P(),
            P(("seq", "expert"), None),
            P(("seq", "expert"), None),
            P(("seq", "expert"), None),
            P(),
            P(),
            P(("seq", "expert"), None),
            P(),
            P(),
            P("expert", "seq", None),
            P("expert", "seq", None),
            P("expert", "seq", None),
        ),
        check_vma=False,
    )
```

```python
from functools import partial

import jax
import jax.numpy as jnp
from jax import lax
from jax.experimental import pallas as pl
from jax.experimental.pallas import tpu as pltpu
from jax.sharding import PartitionSpec as P

HEADS = 16
MOST = 64
BF = jnp.bfloat16
F32 = jnp.float32

norm_eps = 1e-05
masked_score = -1e30


MESH = pl.DeviceIdType.MESH
ANY = pl.BlockSpec(memory_space=pl.ANY)
IN_VMEM = pl.BlockSpec(memory_space=pltpu.VMEM)
VMEM_BYTES = 63 << 20


def product(left, right):
    return jnp.dot(left, right, preferred_element_type=F32)


def rms_norm(values, norm_gain):
    return (
        values * lax.rsqrt(jnp.mean(values * values, axis=-1, keepdims=True) + norm_eps) * norm_gain
    )


def swap(value, axis):
    n = lax.axis_size(axis)
    return lax.ppermute(value, axis, [(i, i ^ 1) for i in range(n)])


def shift(value, axis):
    n = lax.axis_size(axis)
    return lax.ppermute(value, axis, [(i, (i + 2) % n) for i in range(n)])


def flip(value, axis, delta):
    n = lax.axis_size(axis)
    return lax.ppermute(value, axis, [(i, i ^ delta) for i in range(n)])


def owners(axis):
    n = lax.axis_size(axis)
    me = lax.axis_index(axis)
    outer, inner = me // 2, me % 2
    return [((outer - i) % (n // 2)) * 2 + (inner ^ b) for i in range(n // 2) for b in range(2)]


def gather_blocks(value, axis):
    blocks = []
    current = value
    for i in range(lax.axis_size(axis) // 2):
        if i:
            current = shift(current, axis)
        blocks += [current, swap(current, axis)]
    return blocks


def add_low(left, right):
    return (left.astype(F32) + right.astype(F32)).astype(BF)


def scatter_sum(blocks, axis):
    outer_count = lax.axis_size(axis) // 2
    pairs = {}
    for t in list(range(1, outer_count)) + [0]:
        arrived = swap(blocks[2 * t + 1], axis)
        pairs[t] = blocks[2 * t].astype(F32) + arrived.astype(F32)
    total = pairs[1 % outer_count]
    for t in range(1, outer_count):
        arrived = shift(total.astype(BF), axis)
        total = arrived.astype(F32) + pairs[(t + 1) % outer_count]
    return total


def all_sum(value, axes):
    for axis in axes:
        delta = 1
        while delta < lax.axis_size(axis):
            value = value + flip(value, axis, delta)
            delta *= 2
    return value


def exchange(parts, axis):
    n = lax.axis_size(axis)
    me = lax.axis_index(axis)
    out = parts
    for delta in range(1, n):
        other = me ^ delta
        got = flip(lax.dynamic_index_in_dim(parts, other, 0, keepdims=False), axis, delta)
        out = lax.dynamic_update_index_in_dim(out, got, other, 0)
    return out


def after(value, *others):
    return lax.optimization_barrier((value,) + others)[0]


def remote(src, dst, send_sem, recv_sem, device):
    return pltpu.make_async_remote_copy(
        src_ref=src,
        dst_ref=dst,
        send_sem=send_sem,
        recv_sem=recv_sem,
        device_id=device,
        device_id_type=MESH,
    )


def greet(devices):
    barrier = pltpu.get_barrier_semaphore()
    for device in devices:
        pl.semaphore_signal(barrier, inc=1, device_id=device, device_id_type=MESH)
    pl.semaphore_wait(barrier, len(devices))


class Ring:
    def __init__(self, axis):
        self.axis = axis
        self.size = lax.axis_size(axis)
        self.outer_count = self.size // 2
        self.me = lax.axis_index(axis)
        self.outer, self.inner = self.me // 2, self.me % 2
        self.pair = {axis: self.outer * 2 + (1 - self.inner)}
        self.next = {axis: self.at(-1) * 2 + self.inner}
        self.last = {axis: self.at(1) * 2 + self.inner}

    def at(self, back):
        return lax.rem(self.outer - back + self.outer_count, self.outer_count)

    def partners(self):
        if self.outer_count == 1:
            return [self.pair]
        if self.outer_count == 2:
            return [self.pair, self.next]
        return [self.pair, self.next, self.last]


class Gather:
    def __init__(self, ring, place, send_sems, recv_sems):
        self.ring, self.place = ring, place
        self.send_sems, self.recv_sems = send_sems, recv_sems
        self.copies = []

    def block(self, back):
        return self.place(self.ring.at(back) * 2 + self.ring.inner)

    def _send(self, back, src):
        ring = self.ring
        if back < ring.outer_count - 1:
            copy = remote(src, self.block(back), self.send_sems.at[back, 0],
                          self.recv_sems.at[back + 1, 0], ring.next)
            copy.start()
            self.copies.append(copy)
        copy = remote(src, self.block(back), self.send_sems.at[back, 1],
                      self.recv_sems.at[back, 1], ring.pair)
        copy.start()
        self.copies.append(copy)

    def start(self, src):
        self._send(0, src)

    def relay(self, back):
        dst = self.block(back)
        remote(dst, dst, self.send_sems.at[back - 1, 0], self.recv_sems.at[back, 0],
               self.ring.next).wait_recv()
        self._send(back, dst)

    def finish(self):
        ring = self.ring
        for back in range(ring.outer_count):
            dst = self.place(ring.at(back) * 2 + 1 - ring.inner)
            remote(dst, dst, self.send_sems.at[back, 1], self.recv_sems.at[back, 1],
                   ring.pair).wait_recv()
        for copy in self.copies:
            copy.wait_send()


def gather_sems(ring, chunks):
    shape = (chunks, ring.outer_count, 2)
    return [pltpu.SemaphoreType.DMA(shape), pltpu.SemaphoreType.DMA(shape)]


class Scatter:
    def __init__(self, ring, x_ref, chunks, own, land, ringbuf, out, own_sems, sems):
        self.ring, self.x_ref, self.chunks = ring, x_ref, chunks
        self.own, self.land, self.ringbuf, self.out = own, land, ringbuf, out
        self.own_sems, self.sems = own_sems, sems
        self.order = list(range(1, ring.outer_count)) + [0]
        self.rows = x_ref.shape[1] // chunks

    def cut(self, c):
        return pl.ds(c * self.rows, self.rows)

    def pair_copy(self, t, c):
        ring = self.ring
        src = self.x_ref.at[ring.at(t) * 2 + 1 - ring.inner, self.cut(c)]
        return remote(src, self.land.at[t, self.cut(c)], self.sems.at[0, t, c],
                      self.sems.at[1, t, c], ring.pair)

    def slot(self, t):
        return (t - 2) % self.ring.outer_count

    def own_copy(self, t):
        src = self.x_ref.at[self.ring.at(t) * 2 + self.ring.inner]
        return pltpu.make_async_copy(src, self.own.at[t], self.own_sems.at[t])

    def ring_copy(self, t, c):
        to = (t + 1) % self.ring.outer_count
        return remote(self.out.at[t - 1, self.cut(c)], self.ringbuf.at[self.slot(to), self.cut(c)],
                      self.sems.at[2, t, c], self.sems.at[3, to, c], self.ring.next)

    def start_place(self, t):
        self.own_copy(t).start()
        for c in range(self.chunks):
            self.pair_copy(t, c).start()

    def start(self):
        for t in self.order:
            self.start_place(t)

    def mine(self, t, c):
        return self.own[t, self.cut(c)]

    def arrive(self, t, c):
        if c == 0:
            self.own_copy(t).wait()
        self.pair_copy(t, c).wait_recv()

    def step(self, t, c):
        self.arrive(t, c)
        cut = self.cut(c)
        total = self.mine(t, c).astype(F32) + self.land[t, cut].astype(F32)
        if t != self.order[0]:
            self.ring_copy((t - 1) % self.ring.outer_count, c).wait_recv()
            total = total + self.ringbuf[self.slot(t), cut].astype(F32)
        if t:
            self.out[t - 1, cut] = total.astype(BF)
            self.ring_copy(t, c).start()
        return total

    def finish(self):
        for t in self.order:
            for c in range(self.chunks):
                self.pair_copy(t, c).wait_send()
                if t:
                    self.ring_copy(t, c).wait_send()


class KeptScatter(Scatter):
    def __init__(self, ring, x_ref, chunks, own, land, ringbuf, out, sems):
        super().__init__(ring, x_ref, chunks, own, land, ringbuf, out, None, sems)

    def start_place(self, t):
        for c in range(self.chunks):
            self.pair_copy(t, c).start()

    def mine(self, t, c):
        return self.own[pl.ds(t * self.x_ref.shape[1] + c * self.rows, self.rows)]

    def arrive(self, t, c):
        self.pair_copy(t, c).wait_recv()


class PlaceScatter(Scatter):
    def __init__(self, ring, parts, chunks, land, ringbuf, sems):
        super().__init__(ring, parts, chunks, None, land, ringbuf, None, None, sems)

    def block(self, t):
        return self.ring.at(t) * 2 + self.ring.inner

    def ring_copy(self, t, c):
        to = (t + 1) % self.ring.outer_count
        return remote(self.x_ref.at[self.block(t), self.cut(c)], self.ringbuf.at[self.slot(to), self.cut(c)],
                      self.sems.at[2, t, c], self.sems.at[3, to, c], self.ring.next)

    def start_place(self, t):
        for c in range(self.chunks):
            self.pair_copy(t, c).start()

    def step(self, t, c):
        self.pair_copy(t, c).wait_recv()
        cut, mine = self.cut(c), self.block(t)
        total = self.x_ref[mine, cut].astype(F32) + self.land[t, cut].astype(F32)
        if t != self.order[0]:
            self.ring_copy((t - 1) % self.ring.outer_count, c).wait_recv()
            total = total + self.ringbuf[self.slot(t), cut].astype(F32)
        if t:
            self.x_ref[mine, cut] = total.astype(BF)
            self.ring_copy(t, c).start()
        return total


def scatter_scratch(axis, rows, columns, chunks):
    outer_count = lax.axis_size(axis) // 2
    buf = pltpu.VMEM((outer_count, rows, columns), BF)
    less = pltpu.VMEM((max(outer_count - 1, 1), rows, columns), BF)
    return [buf, buf, less, less, pltpu.SemaphoreType.DMA((outer_count,)),
            pltpu.SemaphoreType.DMA((4, outer_count, chunks))]


def kept_scratch(axis, rows, columns, chunks):
    scratch = scatter_scratch(axis, rows, columns, chunks)
    return scratch[1:4] + scratch[5:]


SCATTER_REFS = 6


def kernel_params(number):
    return pltpu.CompilerParams(
        collective_id=number, has_side_effects=True, vmem_limit_bytes=VMEM_BYTES
    )


def call(kernel, number, micros, outs, scratch, *args, specs=None, out_specs=None):
    return pl.pallas_call(
        kernel,
        out_shape=outs,
        in_specs=specs or [ANY] * len(args),
        out_specs=out_specs or jax.tree.map(lambda _: ANY, outs),
        scratch_shapes=scratch,
        compiler_params=kernel_params(number),
        cost_estimate=pl.CostEstimate(
            flops=0, bytes_accessed=micros * 3_000_000, transcendentals=0
        ),
    )(*args)


def weights_kernel(
    wq, wk, wv, normed, hits, q_out, k_out, v_out, normed_out, hits_out,
    own_sems, swap_send, swap_recv, tok_send, tok_recv, g_send, g_recv,
):
    seq, group = Ring("seq"), Ring("expert")
    others = [{"seq": seq.me ^ d} for d in range(1, seq.size)]
    greet(others + group.partners())
    wrows = wq.shape[0]
    cols = wq.shape[1] // seq.size
    rows_mine = pl.ds(group.me * wrows, wrows)
    weights = [(wq, q_out), (wk, k_out), (wv, v_out)]

    def columns_of(ref, s):
        return ref.at[:, pl.ds(pl.multiple_of(s * cols, cols), cols)]

    def swap_copy(i, d):
        src, dst = weights[i]
        return remote(columns_of(src, seq.me ^ d), dst.at[seq.me, rows_mine],
                      swap_send.at[i, d], swap_recv.at[i, d], others[d - 1])

    def token_copy(d):
        return remote(normed, normed_out.at[seq.me], tok_send.at[d], tok_recv.at[d], others[d - 1])

    own = [
        pltpu.make_async_copy(columns_of(src, seq.me), dst.at[seq.me, rows_mine], own_sems.at[i])
        for i, (src, dst) in enumerate(weights)
    ]
    own.append(pltpu.make_async_copy(normed, normed_out.at[seq.me], own_sems.at[3]))
    own.append(pltpu.make_async_copy(hits, hits_out.at[group.me], own_sems.at[4]))
    for i in range(3):
        own[i].start()
        for d in range(1, seq.size):
            swap_copy(i, d).start()
    own[3].start()
    own[4].start()
    for d in range(1, seq.size):
        token_copy(d).start()

    def placed(ref):
        return lambda e: ref.at[:, pl.ds(e * wrows, wrows)]

    gathers = [
        Gather(group, placed(dst), g_send.at[i], g_recv.at[i])
        for i, (_, dst) in enumerate(weights)
    ]
    gathers.append(Gather(group, lambda e: hits_out.at[e], g_send.at[3], g_recv.at[3]))
    gathers[3].start(hits)
    for i in range(3):
        own[i].wait()
        for d in range(1, seq.size):
            remote(weights[i][1].at[seq.me ^ d, rows_mine], weights[i][1].at[seq.me ^ d, rows_mine],
                   swap_send.at[i, d], swap_recv.at[i, d], others[d - 1]).wait_recv()
        gathers[i].start(weights[i][1].at[:, rows_mine])
    for back in range(1, group.outer_count):
        for gather in gathers:
            gather.relay(back)
    for gather in gathers:
        gather.finish()
    for d in range(1, seq.size):
        there = normed_out.at[seq.me ^ d]
        remote(there, there, tok_send.at[d], tok_recv.at[d], others[d - 1]).wait_recv()
        token_copy(d).wait_send()
        for i in range(3):
            swap_copy(i, d).wait_send()
    own[3].wait()
    own[4].wait()


def gather_weights(wq, wk, wv, normed, hits):
    seq_count, group_count = lax.axis_size("seq"), lax.axis_size("expert")
    width = wq.shape[1]
    w_shape = jax.ShapeDtypeStruct((seq_count, width // seq_count, width // seq_count), BF)
    dma = pltpu.SemaphoreType.DMA
    return call(
        weights_kernel, 1, 90,
        (w_shape, w_shape, w_shape,
         jax.ShapeDtypeStruct((seq_count,) + normed.shape, BF),
         jax.ShapeDtypeStruct((group_count,) + hits.shape, BF)),
        [dma((5,)), dma((3, seq_count)), dma((3, seq_count)), dma((seq_count,)), dma((seq_count,)),
         dma((4, group_count // 2, 2)), dma((4, group_count // 2, 2))],
        wq, wk, wv, normed, hits,
    )


HIDDEN_CHUNKS = 2


def hidden_kernel(parts, tokens, gain, hidden_out, all_out, *scratch):
    seq, group = Ring("seq"), Ring("expert")
    greet(seq.partners() + group.partners())
    scatter = Scatter(seq, parts, HIDDEN_CHUNKS, *scratch[:SCATTER_REFS])
    low, low_sems, g_send, g_recv = scratch[SCATTER_REFS:]
    scatter.start()
    for t in scatter.order[:-1]:
        for c in range(HIDDEN_CHUNKS):
            scatter.step(t, c)
    gathers, own = [], []
    for c in range(HIDDEN_CHUNKS):
        cut = scatter.cut(c)
        hidden = tokens[cut].astype(F32) + scatter.step(0, c)
        hidden_out[cut] = hidden
        scale = lax.rsqrt(jnp.mean(hidden * hidden, axis=-1, keepdims=True) + norm_eps)
        low[cut] = (hidden * scale * gain[...]).astype(BF)
        own.append(pltpu.make_async_copy(low.at[cut], all_out.at[group.me, cut], low_sems.at[c]))
        own[c].start()
        gathers.append(
            Gather(group, lambda e, cut=cut: all_out.at[e, cut], g_send.at[c], g_recv.at[c])
        )
        gathers[c].start(low.at[cut])
    for back in range(1, group.outer_count):
        for gather in gathers:
            gather.relay(back)
    for c in range(HIDDEN_CHUNKS):
        gathers[c].finish()
        own[c].wait()
    scatter.finish()


def hidden_and_rows(parts, tokens, gain):
    group_count = lax.axis_size("expert")
    rows, width = tokens.shape
    dma = pltpu.SemaphoreType.DMA
    return call(
        hidden_kernel, 2, 60,
        (jax.ShapeDtypeStruct((rows, width), F32),
         jax.ShapeDtypeStruct((group_count, rows, width), BF)),
        scatter_scratch("seq", rows, width, HIDDEN_CHUNKS)
        + [pltpu.VMEM((rows, width), BF), dma((HIDDEN_CHUNKS,)),
           dma((HIDDEN_CHUNKS, group_count // 2, 2)), dma((HIDDEN_CHUNKS, group_count // 2, 2))],
        parts, tokens, gain[None],
        specs=[ANY, IN_VMEM, IN_VMEM], out_specs=(IN_VMEM, ANY),
    )


ROW_CHUNKS = 2


def rows_kernel(parts, out, *scratch):
    group = Ring("expert")
    greet(group.partners())
    scatter = Scatter(group, parts, ROW_CHUNKS, *scratch)
    scatter.start()
    for t in scatter.order:
        for c in range(ROW_CHUNKS):
            total = scatter.step(t, c)
            if not t:
                out[scatter.cut(c)] = total
    scatter.finish()


def sum_rows(parts):
    rows, width = parts.shape[1:]
    return call(
        rows_kernel, 3, 50, jax.ShapeDtypeStruct((rows, width), F32),
        scatter_scratch("expert", rows, width, ROW_CHUNKS), parts, out_specs=IN_VMEM,
    )


def pack_kernel(rows_in, out, own_sems, g_send, g_recv):
    seq = Ring("seq")
    greet(seq.partners())
    chunks = g_send.shape[0]
    rows = rows_in.shape[0] // chunks
    gathers = []
    for c in range(chunks):
        cut = pl.ds(c * rows, rows)
        pltpu.make_async_copy(rows_in.at[cut], out.at[seq.me, cut], own_sems.at[c]).start()
        gathers.append(
            Gather(seq, lambda s, cut=cut: out.at[s, cut], g_send.at[c], g_recv.at[c])
        )
        gathers[c].start(rows_in.at[cut])
    for back in range(1, seq.outer_count):
        for gather in gathers:
            gather.relay(back)
    for c in range(chunks):
        gathers[c].finish()
        cut = pl.ds(c * rows, rows)
        pltpu.make_async_copy(rows_in.at[cut], out.at[seq.me, cut], own_sems.at[c]).wait()


def gather_pack(rows_in, chunks=2):
    seq_count = lax.axis_size("seq")
    dma = pltpu.SemaphoreType.DMA
    return call(
        pack_kernel, 4, 18, jax.ShapeDtypeStruct((seq_count,) + rows_in.shape, BF),
        [dma((chunks,)), dma((chunks, seq_count // 2, 2)), dma((chunks, seq_count // 2, 2))],
        rows_in,
    )


def dot(left, right, left_dim=1, right_dim=0):
    return lax.dot_general(
        left, right, (((left_dim,), (right_dim,)), ((), ())), preferred_element_type=F32
    )


GRAD_CHUNKS = 2
TILE = 256


def expert_kernel(
    n2, cot, sel, sel_t, gates, wg, wu, wd,
    rows_out, out_parts, d_gate, d_up, d_down,
    stage, parts, routed, cot_rows, wg_v, wu_v, wd_v, scaled, ggate, gup, gate_sums,
    land, ringbuf, in_sems, w_sems, part_sems, wide_sems, out_sems, *dw_scratch,
):
    seq, group = Ring("seq"), Ring("expert")
    greet(seq.partners() + group.partners())
    groups, toks, width = n2.shape
    experts, rows, _ = routed.shape
    slots = rows // groups
    ff = wg_v.shape[1]
    n_total = experts * groups

    def stage_copy(e):
        return pltpu.make_async_copy(n2.at[e], stage.at[e], in_sems.at[0, e])

    def cot_copy(e):
        return pltpu.make_async_copy(cot.at[e], parts.at[e, :, pl.ds(0, width)], in_sems.at[1, e])

    def weight_copy(i, j):
        src, dst = ((wg, wg_v), (wu, wu_v), (wd, wd_v))[i]
        return pltpu.make_async_copy(src.at[j], dst, w_sems.at[i])

    def each(count, body):
        lax.fori_loop(0, count, lambda i, _: (body(i), 0)[1], 0)

    each(groups, lambda e: stage_copy(e).start())
    for i in range(3):
        weight_copy(i, 0).start()
    each(groups, lambda e: cot_copy(e).start())

    def pick(copy, src, dst):
        def body(e):
            copy(e).wait()
            got = dot(sel[e], src[e, :, pl.ds(0, width)]).astype(BF)
            at = pl.ds(pl.multiple_of(e * slots, slots), slots)
            for j in range(experts):
                dst[j, at] = got[j * slots : (j + 1) * slots]
        return body

    each(groups, pick(stage_copy, stage, routed))
    each(groups, pick(cot_copy, parts, cot_rows))

    for j in range(experts):
        for i in range(3):
            weight_copy(i, j).wait()
        gate_sums[j] = jnp.zeros_like(gate_sums[j])

        def hidden_tile(f, j=j):
            at = pl.ds(pl.multiple_of(f * TILE, TILE), TILE)
            gate_pre = dot(routed[j], wg_v[:, at])
            up_pre = dot(routed[j], wu_v[:, at])
            unit = dot(cot_rows[j], wd_v[at, :], 1, 1)
            gate = gates[j][:, :1]
            sig = 1.0 / (1.0 + jnp.exp(-gate_pre))
            silu = gate_pre * sig
            active = silu * up_pre
            low = active.astype(BF).astype(F32)
            gate_sums[j] += jnp.sum(unit * low, axis=-1, keepdims=True)
            scaled[j, :, at] = (low * gate).astype(BF)
            grad_active = unit * gate
            ggate[j, :, at] = (grad_active * up_pre * sig * (1.0 + gate_pre * (1.0 - sig))).astype(BF)
            gup[j, :, at] = (grad_active * silu).astype(BF)

        each(ff // TILE, hidden_tile)
        if j + 1 < experts:
            weight_copy(2, j + 1).start()

        def row_tile(d, j=j):
            at = pl.ds(pl.multiple_of(d * TILE, TILE), TILE)
            grad = dot(ggate[j], wg_v[at, :], 1, 1) + dot(gup[j], wu_v[at, :], 1, 1)
            stage[:, j * slots : (j + 1) * slots, at] = grad.astype(BF).reshape(groups, slots, TILE)

        each(width // TILE, row_tile)
        if j + 1 < experts:
            weight_copy(0, j + 1).start()
            weight_copy(1, j + 1).start()
    weight_copy(2, 0).start()

    scatter = PlaceScatter(group, parts, GRAD_CHUNKS, land, ringbuf, part_sems)
    lanes = lax.broadcasted_iota(jnp.int32, (slots, 128), 1)

    def place(e):
        parts[e, :, pl.ds(0, width)] = dot(sel_t[e], stage[e]).astype(BF)
        at = pl.ds(pl.multiple_of(e * slots, slots), slots)
        high, low = [], []
        for j in range(experts):
            value = gate_sums[j, at]
            first = value.astype(BF)
            rest = (value - first.astype(F32)).astype(BF)
            mine = group.me * experts + j
            high.append(jnp.where(lanes == mine, first.astype(F32),
                                  jnp.where(lanes == mine + n_total, rest.astype(F32), 0.0)))
        parts[e, :, pl.ds(width, 128)] = dot(
            sel_t[e], jnp.concatenate(high, axis=0).astype(BF)
        ).astype(BF)

    for t in scatter.order:
        place(group.at(t) * 2 + 1 - group.inner)
        scatter.start_place(t)
        place(group.at(t) * 2 + group.inner)

    def grad_step(t):
        for c in range(GRAD_CHUNKS):
            total = scatter.step(t, c)
            if not t:
                rows_out[scatter.cut(c)] = total

    side, short = width // seq.size, ff // seq.size

    def wide_grad(right, s, j):
        at = pl.ds(pl.multiple_of(s * side, side), side)
        return dot(routed[j, :, at], right[j], 0, 0).astype(BF)

    def send_wide(right, out, s):
        copies = [
            pltpu.make_async_copy(
                wg_v.at[pl.ds(j * side, side)], out.at[s, pl.ds(j * side, side)], wide_sems.at[j]
            )
            for j in range(experts)
        ]
        for j in range(experts):
            wg_v[pl.ds(j * side, side)] = wide_grad(right, s, j)
            copies[j].start()
        for copy in copies:
            copy.wait()

    def send_tall(s):
        at = pl.ds(pl.multiple_of(s * short, short), short)
        per = short // toks
        copies = []
        for j in range(experts):
            value = dot(scaled[j, :, at], cot_rows[j], 0, 0).astype(BF)
            for i in range(per):
                place_at = j * per + i
                stage[place_at] = value[i * toks : (i + 1) * toks]
                copies.append(pltpu.make_async_copy(
                    stage.at[place_at], d_down.at[s, pl.ds(place_at * toks, toks)],
                    out_sems.at[place_at]))
                copies[-1].start()
        for copy in copies:
            copy.wait()

    dw = KeptScatter(seq, d_gate[0], 1, wu_v, *dw_scratch)
    for t in dw.order:
        send_wide(ggate, d_gate[0], seq.at(t) * 2 + 1 - seq.inner)
        dw.start_place(t)
    grad_step(scatter.order[0])
    for t in dw.order:
        for j in range(experts):
            wu_v[pl.ds((t * experts + j) * side, side)] = wide_grad(
                ggate, seq.at(t) * 2 + seq.inner, j
            )
        if t:
            dw.step(t, 0)
    if len(scatter.order) > 2:
        grad_step(scatter.order[1])
    each(seq.size, lambda s: send_wide(gup, d_up, s))
    for t in scatter.order[2:-1]:
        grad_step(t)
    each(seq.size, send_tall)

    for j in range(experts):
        weight_copy(2, j).wait()

        def out_tile(d, j=j):
            at = pl.ds(pl.multiple_of(d * TILE, TILE), TILE)
            value = dot(scaled[j], wd_v[:, at])
            stage[:, j * slots : (j + 1) * slots, at] = value.astype(BF).reshape(groups, slots, TILE)

        each(width // TILE, out_tile)
        if j + 1 < experts:
            weight_copy(2, j + 1).start()

    def out_copy(e):
        return pltpu.make_async_copy(stage.at[e], out_parts.at[e], out_sems.at[e])

    def out_place(e):
        stage[e] = dot(sel_t[e], stage[e]).astype(BF)
        out_copy(e).start()

    each(groups, out_place)
    grad_step(0)
    d_gate[1][...] = dw.step(0, 0)
    each(groups, lambda e: out_copy(e).wait())
    scatter.finish()
    dw.finish()


def run_experts(n2, cot, sel, sel_t, gates, wg, wu, wd):
    seq_count, group_count = lax.axis_size("seq"), lax.axis_size("expert")
    experts, width, ff = wg.shape
    toks = n2.shape[1]
    rows = gates.shape[1]
    outer_count = group_count // 2
    columns = width + 128
    dma = pltpu.SemaphoreType.DMA
    side, short = width // seq_count, ff // seq_count

    def kernel(*refs):
        ins, outs, scratch = refs[:8], refs[8:14], refs[14:]
        expert_kernel(*ins, outs[0], outs[1], (outs[2], outs[3]), outs[4], outs[5], *scratch)

    low = lambda *shape: pltpu.VMEM(shape, BF)
    return call(
        kernel, 6, 120,
        (jax.ShapeDtypeStruct((toks, columns), F32),
         jax.ShapeDtypeStruct((group_count, toks, width), BF),
         jax.ShapeDtypeStruct((seq_count, experts * side, ff), BF),
         jax.ShapeDtypeStruct((experts * side, ff), F32),
         jax.ShapeDtypeStruct((seq_count, experts * side, ff), BF),
         jax.ShapeDtypeStruct((seq_count, experts * short, width), BF)),
        [low(group_count, toks, width), low(group_count, toks, columns),
         low(experts, rows, width), low(experts, rows, width),
         low(width, ff), low(width, ff), low(ff, width),
         low(experts, rows, ff), low(experts, rows, ff), low(experts, rows, ff),
         pltpu.VMEM((experts, rows, 128), F32),
         low(outer_count, toks, columns), low(outer_count - 1, toks, columns),
         dma((2, group_count)), dma((3,)), dma((4, outer_count, GRAD_CHUNKS)), dma((experts,)),
         dma((group_count,))]
        + kept_scratch("seq", experts * side, ff, 1),
        n2, cot, sel, sel_t, gates, wg, wu, wd,
        specs=[ANY, ANY, IN_VMEM, IN_VMEM, IN_VMEM, ANY, ANY, ANY],
        out_specs=(IN_VMEM, ANY, ANY, IN_VMEM, ANY, ANY),
    )


LAST_CHUNKS = 2


def last_kernel(
    normed_parts, three_parts, out_parts, tokens, gain, grad_hidden, small, *refs, extra
):
    expert_parts, refs = refs[:extra], refs[extra:]
    d_tokens, d_three, d_out, small_out = refs[:4]
    expert_sums, scratch = refs[4 : 4 + extra], refs[4 + extra :]
    expert_scratch, scratch = scratch[: extra * SCATTER_REFS], scratch[extra * SCATTER_REFS :]
    seq, group = Ring("seq"), Ring("expert")
    others = [{"seq": seq.me ^ d} for d in range(1, seq.size)]
    steps = [{"expert": group.me ^ (1 << i)} for i in range((group.size - 1).bit_length())]
    steps += [{"seq": seq.me ^ (1 << i)} for i in range((seq.size - 1).bit_length())]
    known = [{"expert": group.me ^ (1 << i)} for i in range((group.size - 1).bit_length())]
    greet(others + known + [group.next, group.last])
    n = SCATTER_REFS
    normed = Scatter(seq, normed_parts, LAST_CHUNKS, *scratch[:n])
    outs = Scatter(group, out_parts, 1, *scratch[n : 2 * n])
    three = Scatter(group, three_parts, LAST_CHUNKS, *scratch[2 * n : 3 * n])
    three_low, sum_buf, sum_land, own_sem, swap_sems, sum_sems = scratch[3 * n :]
    experts = [
        Scatter(seq, ref, 1, *expert_scratch[i * n : (i + 1) * n])
        for i, ref in enumerate(expert_parts)
    ]
    normed.start()
    for t in three.order:
        three.start_place(t)
        outs.start_place(t)
    for scatter in experts:
        scatter.start()
    for t in normed.order[:-1]:
        for c in range(LAST_CHUNKS):
            normed.step(t, c)
    for scatter in experts:
        scatter.step(scatter.order[0], 0)
    gain_sum = jnp.zeros((1, tokens.shape[1]), F32)
    for c in range(LAST_CHUNKS):
        cut = normed.cut(c)
        grad = normed.step(0, c)
        value = tokens[cut].astype(F32)
        scale = lax.rsqrt(jnp.mean(value * value, axis=-1, keepdims=True) + norm_eps)
        unit = value * scale
        gained = grad * gain[...]
        mean = jnp.mean(gained * unit, axis=-1, keepdims=True)
        d_tokens[cut] = grad_hidden[cut] + scale * (gained - unit * mean)
        gain_sum = gain_sum + jnp.sum(grad * unit, axis=0, keepdims=True)
    sum_buf[0] = small[...]
    last_row = small.shape[0] - 1
    sum_buf[0, pl.ds(last_row, 1)] = gain_sum

    def sum_copy(i):
        return remote(sum_buf.at[i], sum_land.at[i], sum_sems.at[0, i], sum_sems.at[1, i], steps[i])

    def sum_step(i):
        sum_copy(i).wait_recv()
        total = sum_buf[i] + sum_land[i]
        if i + 1 < len(steps):
            sum_buf[i + 1] = total
            sum_copy(i + 1).start()
        else:
            small_out[...] = total

    for t in three.order[:-1]:
        for c in range(LAST_CHUNKS):
            three.step(t, c)
        outs.step(t, 0)
    for c in range(LAST_CHUNKS):
        three_low[three.cut(c)] = three.step(0, c).astype(BF)
    wrows = three_low.shape[0] // seq.size

    def swap_copy(d):
        src = three_low.at[pl.ds((seq.me ^ d) * wrows, wrows)]
        return remote(src, d_three.at[seq.me], swap_sems.at[0, d], swap_sems.at[1, d], others[d - 1])

    for d in range(1, seq.size):
        swap_copy(d).start()
    own = pltpu.make_async_copy(
        three_low.at[pl.ds(seq.me * wrows, wrows)], d_three.at[seq.me], own_sem.at[0]
    )
    own.start()
    d_out[...] = outs.step(0, 0)
    sum_copy(0).start()
    for i in range(len(steps)):
        sum_step(i)
    for scatter, out in zip(experts, expert_sums):
        for t in scatter.order[1:-1]:
            scatter.step(t, 0)
        out[...] = scatter.step(0, 0)
    for d in range(1, seq.size):
        there = d_three.at[seq.me ^ d]
        remote(there, there, swap_sems.at[0, d], swap_sems.at[1, d], others[d - 1]).wait_recv()
        swap_copy(d).wait_send()
    own.wait()
    for i in range(len(steps)):
        sum_copy(i).wait_send()
    for scatter in (normed, three, outs, *experts):
        scatter.finish()


def finish_all(normed_parts, three_parts, out_parts, tokens, gain, grad_hidden, small, *expert_parts):
    seq_count, group_count = lax.axis_size("seq"), lax.axis_size("expert")
    rows, width = tokens.shape
    rows3, cols3 = three_parts.shape[1:]
    wrows = rows3 // seq_count
    count = (seq_count - 1).bit_length() + (group_count - 1).bit_length()
    dma = pltpu.SemaphoreType.DMA
    return call(
        partial(last_kernel, extra=len(expert_parts)), 5, 110,
        (jax.ShapeDtypeStruct((rows, width), F32),
         jax.ShapeDtypeStruct((seq_count, wrows, cols3), BF),
         jax.ShapeDtypeStruct(out_parts.shape[1:], F32),
         jax.ShapeDtypeStruct(small.shape, F32))
        + tuple(jax.ShapeDtypeStruct(e.shape[1:], F32) for e in expert_parts),
        sum([scatter_scratch("seq", e.shape[1], e.shape[2], 1) for e in expert_parts], [])
        + scatter_scratch("seq", rows, width, LAST_CHUNKS)
        + scatter_scratch("expert", out_parts.shape[1], width, 1)
        + scatter_scratch("expert", rows3, cols3, LAST_CHUNKS)
        + [pltpu.VMEM((rows3, cols3), BF), pltpu.VMEM((count,) + small.shape, F32),
           pltpu.VMEM((count,) + small.shape, F32), dma((1,)), dma((2, seq_count)), dma((2, count))],
        normed_parts, three_parts, out_parts, tokens, gain[None], grad_hidden, small, *expert_parts,
        specs=[ANY, ANY, ANY, IN_VMEM, IN_VMEM, IN_VMEM, IN_VMEM] + [ANY] * len(expert_parts),
        out_specs=(IN_VMEM, ANY, IN_VMEM, IN_VMEM) + (IN_VMEM,) * len(expert_parts),
    )


def each(left, right, how):
    return jnp.einsum(how, left, right, preferred_element_type=F32)


def plain_experts(normed2_all, cot_all, chosen, gate_rows, w_gate, w_up, w_down):
    seq_count, group_count = lax.axis_size("seq"), lax.axis_size("expert")
    experts_local, tok_rows = w_gate.shape[0], chosen.shape[-1]
    total_experts = experts_local * group_count
    chosen_low = chosen.astype(BF)

    def pick_rows(values):
        return jnp.einsum("ejmt,etd->jemd", chosen_low, values, preferred_element_type=F32).astype(BF)

    def place_rows(values):
        return jnp.einsum("ejmt,jemd->etd", chosen_low, values, preferred_element_type=F32).astype(BF)

    routed = pick_rows(normed2_all)
    cot_rows = pick_rows(cot_all)

    gate_pre = each(routed, w_gate, "jemd,jdf->jemf")
    up_pre = each(routed, w_up, "jemd,jdf->jemf")
    sigmoid_gate = jax.nn.sigmoid(gate_pre)
    silu_gate = gate_pre * sigmoid_gate
    active = silu_gate * up_pre
    active_low = active.astype(BF)
    grad_unit = each(cot_rows, w_down, "jemd,jfd->jemf")
    grad_gate_rows = jnp.sum(grad_unit * active_low.astype(F32), axis=-1)
    grad_active = grad_unit * gate_rows
    grad_gate_low = (
        grad_active * up_pre * sigmoid_gate * (1.0 + gate_pre * (1.0 - sigmoid_gate))
    ).astype(BF)
    grad_up_low = (grad_active * silu_gate).astype(BF)
    grad_routed = each(grad_gate_low, w_gate, "jemf,jdf->jemd")
    grad_routed = (grad_routed + each(grad_up_low, w_up, "jemf,jdf->jemd")).astype(BF)
    grad_parts = place_rows(grad_routed)
    grad_normed2 = sum_rows(grad_parts)
    grad_probs_parts = jnp.einsum(
        "ejmt,jem->etj", chosen.astype(F32), grad_gate_rows, precision=lax.Precision.HIGHEST
    )
    grad_probs = lax.all_to_all(grad_probs_parts, "expert", split_axis=0, concat_axis=0, tiled=True)
    grad_probs = grad_probs.transpose(1, 0, 2).reshape(tok_rows, total_experts)

    expert_out = each(active_low, w_down, "jemf,jfd->jemd") * gate_rows
    out_parts = place_rows(expert_out.astype(BF))

    active_scaled = (active_low.astype(F32) * gate_rows).astype(BF)

    def expert_grad(left, right):
        grad = jnp.einsum("jemd,jemf->jdf", left, right, preferred_element_type=F32).astype(BF)
        rows = grad.shape[1] // seq_count
        grad = grad.reshape(experts_local, seq_count, rows, grad.shape[2])
        return scatter_sum(
            [lax.dynamic_index_in_dim(grad, o, 1, keepdims=False) for o in owners("seq")], "seq"
        )

    d_w_gate = expert_grad(routed, grad_gate_low)
    d_w_up = expert_grad(routed, grad_up_low)
    d_w_down = expert_grad(active_scaled, cot_rows)
    return grad_normed2, grad_probs, out_parts, d_w_gate, d_w_up, d_w_down


def local(
    tokens,
    lengths,
    routes,
    gain_attn,
    w_query,
    w_key,
    w_value,
    gain_query,
    gain_key,
    w_out,
    gain_mlp,
    router,
    w_gate,
    w_up,
    w_down,
    cotangent,
):
    seq_count = lax.axis_size("seq")
    group_count = lax.axis_size("expert")
    seq_me = lax.axis_index("seq")
    group_me = lax.axis_index("expert")
    tok_rows, width = tokens.shape[1], tokens.shape[2]
    head_dim = width // HEADS
    heads = HEADS // seq_count
    cols = width // seq_count
    wrows = w_query.shape[0]
    length = tok_rows * seq_count
    experts_local = w_gate.shape[0]
    total_experts = experts_local * group_count
    slots = MOST
    score_scale = head_dim ** (-0.5)
    inputs = tokens[0].astype(F32)

    places = jnp.arange(length, dtype=jnp.int32)
    doc_ends = jnp.cumsum(lengths[0])
    passed = (places[:, None] >= doc_ends[None, :]).astype(jnp.int32)
    docs = jnp.sum(passed, axis=1)
    offsets = places - jnp.sum(passed * lengths[0][None, :], axis=1)
    allowed = (docs[:, None] == docs[None, :]) & (places[None, :] <= places[:, None])
    half = head_dim // 2
    inverse = 10000.0 ** (-jnp.arange(half, dtype=F32) / half)
    angles = offsets.astype(F32)[:, None] * inverse[None, :]
    cosine = jnp.cos(angles)[:, None, :]
    sine = jnp.sin(angles)[:, None, :]

    def turn(values, sine_table):
        first, second = values[..., :half], values[..., half:]
        return jnp.concatenate(
            [first * cosine - second * sine_table, second * cosine + first * sine_table], axis=-1
        )

    expert_ids = jnp.arange(128, dtype=jnp.int32)
    hits = jnp.any(routes[0][:, :, None] == expert_ids[None, None, :], axis=1).astype(BF)
    cot_all = lax.all_gather(cotangent[0], "expert", axis=0)
    w_rows = lax.all_gather(w_out, "expert", axis=0, tiled=True)
    normed, attn_norm_back = jax.vjp(rms_norm, inputs, gain_attn)
    wq_cols, wk_cols, wv_cols, normed_all, hits_all = gather_weights(
        w_query, w_key, w_value, normed.astype(BF), hits
    )
    normed_all = normed_all.reshape(length, width)
    w_cols = [w.reshape(width, cols) for w in (wq_cols, wk_cols, wv_cols)]
    query_raw = product(normed_all, w_cols[0])
    key_raw = product(normed_all, w_cols[1])
    value_low = product(normed_all, w_cols[2]).astype(BF).reshape(length, heads, head_dim)

    def row_sums(left, right):
        sums = jnp.stack([jnp.sum(left, axis=1), jnp.sum(right, axis=1)])
        return lax.psum(sums, "seq") / width

    inv_rms = lax.rsqrt(row_sums(query_raw**2, key_raw**2) + norm_eps)
    gain_q = lax.dynamic_slice_in_dim(gain_query, seq_me * cols, cols)
    gain_k = lax.dynamic_slice_in_dim(gain_key, seq_me * cols, cols)
    query_unit = query_raw * inv_rms[0][:, None]
    key_unit = key_raw * inv_rms[1][:, None]
    query_low = turn((query_unit * gain_q).reshape(length, heads, head_dim), sine).astype(BF)
    key_low = turn((key_unit * gain_k).reshape(length, heads, head_dim), sine).astype(BF)
    scores = jnp.einsum("qhd,khd->hqk", query_low, key_low, preferred_element_type=F32)
    scores = jnp.where(allowed[None], scores * score_scale, masked_score)
    top_score = jnp.max(scores, axis=-1, keepdims=True)
    weights = jnp.exp(scores - top_score)
    probs = weights / jnp.sum(weights, axis=-1, keepdims=True)
    probs_low = probs.astype(BF)
    attended = jnp.einsum("hqk,khd->qhd", probs_low, value_low, preferred_element_type=F32)
    attended_low = attended.reshape(length, cols).astype(BF)
    hidden_parts = product(attended_low, w_rows).astype(BF).reshape(seq_count, tok_rows, width)
    hidden, normed2_all = hidden_and_rows(hidden_parts, tokens[0], gain_mlp)
    normed2, mlp_norm_back = jax.vjp(rms_norm, hidden, gain_mlp)
    normed2_low = normed2.astype(BF)

    first_expert = group_me * experts_local
    hit = lax.dynamic_slice_in_dim(hits_all, first_expert, experts_local, axis=2)
    hit = hit.transpose(0, 2, 1)
    before = (jnp.arange(tok_rows)[:, None] < jnp.arange(tok_rows)[None, :]).astype(BF)
    rank = jnp.einsum("ejt,tu->eju", hit, before, preferred_element_type=F32)
    slot_ids = jnp.arange(slots, dtype=jnp.int32)
    chosen = (hit[:, :, None, :] > 0) & (rank.astype(jnp.int32)[:, :, None, :] == slot_ids[None, None, :, None])
    chosen_low = chosen.astype(BF)

    logits_all = jnp.einsum("etd,dn->etn", normed2_all, router, preferred_element_type=F32)
    probs_all = jax.nn.softmax(logits_all, axis=-1)
    mine = lax.dynamic_slice_in_dim(probs_all, first_expert, experts_local, axis=2)
    gate_rows = jnp.einsum(
        "ejmt,etj->jem", chosen.astype(F32), mine, precision=lax.Precision.HIGHEST
    )[..., None]

    roomy = group_count * slots <= 512
    if roomy:
        both = chosen_low.reshape(group_count, experts_local * slots, tok_rows)
        gate_wide = jnp.broadcast_to(
            gate_rows.reshape(experts_local, group_count * slots, 1),
            (experts_local, group_count * slots, 128),
        )
        rows_sum, out_parts, _, d_w_gate, up_parts, down_parts = run_experts(
            normed2_all, cot_all, both, both.transpose(0, 2, 1), gate_wide, w_gate, w_up, w_down
        )
        grad_normed2 = rows_sum[:, :width]
        grad_probs = (
            rows_sum[:, width : width + total_experts]
            + rows_sum[:, width + total_experts : width + 2 * total_experts]
        )
        expert_parts = (up_parts, down_parts)
    else:
        grad_normed2, grad_probs, out_parts, d_w_gate, d_w_up, d_w_down = plain_experts(
            normed2_all, cot_all, chosen, gate_rows, w_gate, w_up, w_down
        )
        expert_parts = ()
    out_sum = lax.psum_scatter(out_parts, "expert", scatter_dimension=0, tiled=False)

    router_probs, softmax_back = jax.vjp(
        partial(jax.nn.softmax, axis=-1), product(normed2_low, router)
    )
    (grad_logits,) = softmax_back(grad_probs)
    grad_logits_low = grad_logits.astype(BF)
    grad_router = jnp.einsum("td,te->ed", normed2_low, grad_logits_low, preferred_element_type=F32)
    grad_normed2 = grad_normed2 + jnp.einsum(
        "te,de->td", grad_logits_low, router, preferred_element_type=F32
    )
    grad_hidden_part, grad_gain_mlp = mlp_norm_back(grad_normed2)
    grad_hidden = cotangent[0].astype(F32) + grad_hidden_part

    grad_hidden_all = gather_pack(grad_hidden.astype(BF)).reshape(length, width)
    grad_attended = jnp.einsum(
        "te,de->td", grad_hidden_all, w_rows, preferred_element_type=F32
    ).astype(BF)
    grad_attended = grad_attended.reshape(length, heads, head_dim)
    grad_w_out = jnp.einsum(
        "td,te->de", attended_low, grad_hidden_all, preferred_element_type=F32
    ).astype(BF).reshape(group_count, wrows, width)
    grad_probs_attn = jnp.einsum(
        "qhd,khd->hqk", grad_attended, value_low, preferred_element_type=F32
    )
    row_dot = jnp.sum(probs * grad_probs_attn, axis=-1, keepdims=True)
    grad_scores = (probs * (grad_probs_attn - row_dot)).astype(BF)
    grad_query = jnp.einsum("hqk,khd->qhd", grad_scores, key_low, preferred_element_type=F32)
    grad_key = jnp.einsum("hqk,qhd->khd", grad_scores, query_low, preferred_element_type=F32)
    grad_value = jnp.einsum("hqk,qhd->khd", probs_low, grad_attended, preferred_element_type=F32)
    grad_query = turn(grad_query * score_scale, -sine).reshape(length, cols)
    grad_key = turn(grad_key * score_scale, -sine).reshape(length, cols)
    grad_gain_query = jnp.sum(grad_query * query_unit, axis=0)
    grad_gain_key = jnp.sum(grad_key * key_unit, axis=0)
    grad_query_g, grad_key_g = grad_query * gain_q, grad_key * gain_k
    means = row_sums(grad_query_g * query_unit, grad_key_g * key_unit)
    grad_query_low = (
        inv_rms[0][:, None] * (grad_query_g - query_unit * means[0][:, None])
    ).astype(BF)
    grad_key_low = (inv_rms[1][:, None] * (grad_key_g - key_unit * means[1][:, None])).astype(BF)
    grad_value_low = grad_value.reshape(length, cols).astype(BF)
    grad_three = jnp.concatenate([grad_query_low, grad_key_low, grad_value_low], axis=1)
    grad_normed_parts = each(grad_query_low, w_cols[0], "te,de->td")
    grad_normed_parts += each(grad_key_low, w_cols[1], "te,de->td")
    grad_normed_parts += each(grad_value_low, w_cols[2], "te,de->td")
    grad_normed_parts = grad_normed_parts.astype(BF).reshape(seq_count, tok_rows, width)
    grad_w_three = jnp.einsum(
        "td,te->de", normed_all, grad_three, preferred_element_type=F32
    ).astype(BF).reshape(seq_count, group_count, wrows, 3 * cols)
    grad_w_three = grad_w_three.transpose(1, 0, 2, 3).reshape(
        group_count, seq_count * wrows, 3 * cols
    )

    def full(value):
        return lax.dynamic_update_slice(jnp.zeros((width,), F32), value, (seq_me * cols,))

    rows = [grad_router, grad_gain_mlp[None], full(grad_gain_query)[None], full(grad_gain_key)[None]]
    small = jnp.concatenate(rows)
    spare = -(total_experts + 4) % 8 + 1
    small = jnp.concatenate([small, jnp.zeros((spare, width), F32)])
    d_tokens, d_three, d_w_out, small, *expert_sums = finish_all(
        grad_normed_parts, grad_w_three, grad_w_out, tokens[0], gain_attn, grad_hidden, small,
        *expert_parts,
    )
    mixed = hidden + after(out_sum, d_w_out).astype(F32)
    if roomy:
        d_w_gate = d_w_gate.reshape(experts_local, width // seq_count, -1)
        d_w_up = expert_sums[0].reshape(experts_local, width // seq_count, -1)
        d_w_down = expert_sums[1].reshape(experts_local, -1, width)
    d_three = d_three.reshape(seq_count, wrows, 3, cols).transpose(2, 1, 0, 3)
    d_three = d_three.reshape(3, wrows, width).astype(F32)
    return (
        mixed.astype(BF)[None],
        d_tokens[None],
        small[-1],
        d_three[0],
        d_three[1],
        d_three[2],
        small[total_experts + 1],
        small[total_experts + 2],
        d_w_out,
        small[total_experts],
        small[:total_experts].T,
        d_w_gate,
        d_w_up,
        d_w_down,
    )


def solution(mesh):
    return jax.shard_map(
        local,
        mesh=mesh,
        in_specs=(
            P("expert", "seq", None),
            P("expert", None),
            P("expert", "seq", None),
            P(),
            P(("seq", "expert"), None),
            P(("seq", "expert"), None),
            P(("seq", "expert"), None),
            P(),
            P(),
            P(("seq", "expert"), None),
            P(),
            P(),
            P("expert", None, None),
            P("expert", None, None),
            P("expert", None, None),
            P("expert", "seq", None),
        ),
        out_specs=(
            P("expert", "seq", None),
            P("expert", "seq", None),
            P(),
            P(("seq", "expert"), None),
            P(("seq", "expert"), None),
            P(("seq", "expert"), None),
            P(),
            P(),
            P(("seq", "expert"), None),
            P(),
            P(),
            P("expert", "seq", None),
            P("expert", "seq", None),
            P("expert", "seq", None),
        ),
        check_vma=False,
    )
```

```python
from functools import partial

import jax
import jax.numpy as jnp
from jax import lax
from jax.experimental import pallas as pl
from jax.experimental.pallas import tpu as pltpu
from jax.sharding import PartitionSpec as P

HEADS = 16
MOST = 64
BF = jnp.bfloat16
F32 = jnp.float32

norm_eps = 1e-05
masked_score = -1e30


MESH = pl.DeviceIdType.MESH
ANY = pl.BlockSpec(memory_space=pl.ANY)
IN_VMEM = pl.BlockSpec(memory_space=pltpu.VMEM)
VMEM_BYTES = 63 << 20


def product(left, right):
    return jnp.dot(left, right, preferred_element_type=F32)


def rms_norm(values, norm_gain):
    return (
        values * lax.rsqrt(jnp.mean(values * values, axis=-1, keepdims=True) + norm_eps) * norm_gain
    )


def swap(value, axis):
    n = lax.axis_size(axis)
    return lax.ppermute(value, axis, [(i, i ^ 1) for i in range(n)])


def shift(value, axis):
    n = lax.axis_size(axis)
    return lax.ppermute(value, axis, [(i, (i + 2) % n) for i in range(n)])


def flip(value, axis, delta):
    n = lax.axis_size(axis)
    return lax.ppermute(value, axis, [(i, i ^ delta) for i in range(n)])


def owners(axis):
    n = lax.axis_size(axis)
    me = lax.axis_index(axis)
    outer, inner = me // 2, me % 2
    return [((outer - i) % (n // 2)) * 2 + (inner ^ b) for i in range(n // 2) for b in range(2)]


def gather_blocks(value, axis):
    blocks = []
    current = value
    for i in range(lax.axis_size(axis) // 2):
        if i:
            current = shift(current, axis)
        blocks += [current, swap(current, axis)]
    return blocks


def add_low(left, right):
    return (left.astype(F32) + right.astype(F32)).astype(BF)


def scatter_sum(blocks, axis):
    outer_count = lax.axis_size(axis) // 2
    pairs = {}
    for t in list(range(1, outer_count)) + [0]:
        arrived = swap(blocks[2 * t + 1], axis)
        pairs[t] = blocks[2 * t].astype(F32) + arrived.astype(F32)
    total = pairs[1 % outer_count]
    for t in range(1, outer_count):
        arrived = shift(total.astype(BF), axis)
        total = arrived.astype(F32) + pairs[(t + 1) % outer_count]
    return total


def all_sum(value, axes):
    for axis in axes:
        delta = 1
        while delta < lax.axis_size(axis):
            value = value + flip(value, axis, delta)
            delta *= 2
    return value


def exchange(parts, axis):
    n = lax.axis_size(axis)
    me = lax.axis_index(axis)
    out = parts
    for delta in range(1, n):
        other = me ^ delta
        got = flip(lax.dynamic_index_in_dim(parts, other, 0, keepdims=False), axis, delta)
        out = lax.dynamic_update_index_in_dim(out, got, other, 0)
    return out


def after(value, *others):
    return lax.optimization_barrier((value,) + others)[0]


def remote(src, dst, send_sem, recv_sem, device):
    return pltpu.make_async_remote_copy(
        src_ref=src,
        dst_ref=dst,
        send_sem=send_sem,
        recv_sem=recv_sem,
        device_id=device,
        device_id_type=MESH,
    )


def greet(devices):
    barrier = pltpu.get_barrier_semaphore()
    for device in devices:
        pl.semaphore_signal(barrier, inc=1, device_id=device, device_id_type=MESH)
    pl.semaphore_wait(barrier, len(devices))


class Ring:
    def __init__(self, axis):
        self.axis = axis
        self.size = lax.axis_size(axis)
        self.outer_count = self.size // 2
        self.me = lax.axis_index(axis)
        self.outer, self.inner = self.me // 2, self.me % 2
        self.pair = {axis: self.outer * 2 + (1 - self.inner)}
        self.next = {axis: self.at(-1) * 2 + self.inner}
        self.last = {axis: self.at(1) * 2 + self.inner}

    def at(self, back):
        return lax.rem(self.outer - back + self.outer_count, self.outer_count)

    def partners(self):
        if self.outer_count == 1:
            return [self.pair]
        if self.outer_count == 2:
            return [self.pair, self.next]
        return [self.pair, self.next, self.last]


class Gather:
    def __init__(self, ring, place, send_sems, recv_sems):
        self.ring, self.place = ring, place
        self.send_sems, self.recv_sems = send_sems, recv_sems
        self.copies = []

    def block(self, back):
        return self.place(self.ring.at(back) * 2 + self.ring.inner)

    def _send(self, back, src):
        ring = self.ring
        if back < ring.outer_count - 1:
            copy = remote(src, self.block(back), self.send_sems.at[back, 0],
                          self.recv_sems.at[back + 1, 0], ring.next)
            copy.start()
            self.copies.append(copy)
        copy = remote(src, self.block(back), self.send_sems.at[back, 1],
                      self.recv_sems.at[back, 1], ring.pair)
        copy.start()
        self.copies.append(copy)

    def start(self, src):
        self._send(0, src)

    def relay(self, back):
        dst = self.block(back)
        remote(dst, dst, self.send_sems.at[back - 1, 0], self.recv_sems.at[back, 0],
               self.ring.next).wait_recv()
        self._send(back, dst)

    def finish(self):
        ring = self.ring
        for back in range(ring.outer_count):
            dst = self.place(ring.at(back) * 2 + 1 - ring.inner)
            remote(dst, dst, self.send_sems.at[back, 1], self.recv_sems.at[back, 1],
                   ring.pair).wait_recv()
        for copy in self.copies:
            copy.wait_send()


def gather_sems(ring, chunks):
    shape = (chunks, ring.outer_count, 2)
    return [pltpu.SemaphoreType.DMA(shape), pltpu.SemaphoreType.DMA(shape)]


class Scatter:
    def __init__(self, ring, x_ref, chunks, own, land, ringbuf, out, own_sems, sems):
        self.ring, self.x_ref, self.chunks = ring, x_ref, chunks
        self.own, self.land, self.ringbuf, self.out = own, land, ringbuf, out
        self.own_sems, self.sems = own_sems, sems
        self.order = list(range(1, ring.outer_count)) + [0]
        self.rows = x_ref.shape[1] // chunks

    def cut(self, c):
        return pl.ds(c * self.rows, self.rows)

    def pair_copy(self, t, c):
        ring = self.ring
        src = self.x_ref.at[ring.at(t) * 2 + 1 - ring.inner, self.cut(c)]
        return remote(src, self.land.at[t, self.cut(c)], self.sems.at[0, t, c],
                      self.sems.at[1, t, c], ring.pair)

    def slot(self, t):
        return (t - 2) % self.ring.outer_count

    def own_copy(self, t):
        src = self.x_ref.at[self.ring.at(t) * 2 + self.ring.inner]
        return pltpu.make_async_copy(src, self.own.at[t], self.own_sems.at[t])

    def ring_copy(self, t, c):
        to = (t + 1) % self.ring.outer_count
        return remote(self.out.at[t - 1, self.cut(c)], self.ringbuf.at[self.slot(to), self.cut(c)],
                      self.sems.at[2, t, c], self.sems.at[3, to, c], self.ring.next)

    def start_place(self, t):
        self.own_copy(t).start()
        for c in range(self.chunks):
            self.pair_copy(t, c).start()

    def start(self):
        for t in self.order:
            self.start_place(t)

    def mine(self, t, c):
        return self.own[t, self.cut(c)]

    def arrive(self, t, c):
        if c == 0:
            self.own_copy(t).wait()
        self.pair_copy(t, c).wait_recv()

    def step(self, t, c):
        self.arrive(t, c)
        cut = self.cut(c)
        total = self.mine(t, c).astype(F32) + self.land[t, cut].astype(F32)
        if t != self.order[0]:
            self.ring_copy((t - 1) % self.ring.outer_count, c).wait_recv()
            total = total + self.ringbuf[self.slot(t), cut].astype(F32)
        if t:
            self.out[t - 1, cut] = total.astype(BF)
            self.ring_copy(t, c).start()
        return total

    def finish(self):
        for t in self.order:
            for c in range(self.chunks):
                self.pair_copy(t, c).wait_send()
                if t:
                    self.ring_copy(t, c).wait_send()


class RingFirst:
    def __init__(self, ring, parts, land, ringbuf, sems):
        self.ring, self.parts, self.land, self.ringbuf, self.sems = ring, parts, land, ringbuf, sems
        self.order = list(range(1, ring.outer_count)) + [0]

    def two(self, t):
        return pl.ds(self.ring.at(t) * 2, 2)

    def ring_copy(self, t):
        to = (t + 1) % self.ring.outer_count
        slot = (to - 2) % self.ring.outer_count
        return remote(self.parts.at[self.two(t)], self.ringbuf.at[slot], self.sems.at[0, t],
                      self.sems.at[1, to], self.ring.next)

    def pair_copy(self):
        src = self.parts.at[self.ring.outer * 2 + 1 - self.ring.inner]
        return remote(src, self.land, self.sems.at[2, 0], self.sems.at[3, 0], self.ring.pair)

    def start(self):
        self.ring_copy(1).start()

    def step(self, t):
        self.ring_copy((t - 1) % self.ring.outer_count).wait_recv()
        slot = (t - 2) % self.ring.outer_count
        total = self.parts[self.two(t)].astype(F32) + self.ringbuf[slot].astype(F32)
        self.parts[self.two(t)] = total.astype(BF)
        if t:
            self.ring_copy(t).start()
        else:
            self.pair_copy().start()

    def last(self):
        self.pair_copy().wait_recv()
        mine = self.parts[self.ring.outer * 2 + self.ring.inner]
        return mine.astype(F32) + self.land[...].astype(F32)

    def finish(self):
        for t in self.order[:-1]:
            self.ring_copy(t).wait_send()
        self.pair_copy().wait_send()


def ring_first_scratch(axis, rows, columns):
    size = lax.axis_size(axis)
    low = lambda *shape: pltpu.VMEM(shape, BF)
    return [low(size, rows, columns), low(rows, columns), low(size // 2 - 1, 2, rows, columns),
            pltpu.SemaphoreType.DMA((4, size // 2))]


class KeptScatter(Scatter):
    def __init__(self, ring, x_ref, chunks, own, land, ringbuf, out, sems):
        super().__init__(ring, x_ref, chunks, own, land, ringbuf, out, None, sems)

    def start_place(self, t):
        for c in range(self.chunks):
            self.pair_copy(t, c).start()

    def mine(self, t, c):
        return self.own[pl.ds(t * self.x_ref.shape[1] + c * self.rows, self.rows)]

    def arrive(self, t, c):
        self.pair_copy(t, c).wait_recv()


class PlaceScatter(Scatter):
    def __init__(self, ring, parts, chunks, land, ringbuf, sems):
        super().__init__(ring, parts, chunks, None, land, ringbuf, None, None, sems)

    def block(self, t):
        return self.ring.at(t) * 2 + self.ring.inner

    def ring_copy(self, t, c):
        to = (t + 1) % self.ring.outer_count
        return remote(self.x_ref.at[self.block(t), self.cut(c)], self.ringbuf.at[self.slot(to), self.cut(c)],
                      self.sems.at[2, t, c], self.sems.at[3, to, c], self.ring.next)

    def start_place(self, t):
        for c in range(self.chunks):
            self.pair_copy(t, c).start()

    def step(self, t, c):
        self.pair_copy(t, c).wait_recv()
        cut, mine = self.cut(c), self.block(t)
        total = self.x_ref[mine, cut].astype(F32) + self.land[t, cut].astype(F32)
        if t != self.order[0]:
            self.ring_copy((t - 1) % self.ring.outer_count, c).wait_recv()
            total = total + self.ringbuf[self.slot(t), cut].astype(F32)
        if t:
            self.x_ref[mine, cut] = total.astype(BF)
            self.ring_copy(t, c).start()
        return total


def scatter_scratch(axis, rows, columns, chunks):
    outer_count = lax.axis_size(axis) // 2
    buf = pltpu.VMEM((outer_count, rows, columns), BF)
    less = pltpu.VMEM((max(outer_count - 1, 1), rows, columns), BF)
    return [buf, buf, less, less, pltpu.SemaphoreType.DMA((outer_count,)),
            pltpu.SemaphoreType.DMA((4, outer_count, chunks))]


def kept_scratch(axis, rows, columns, chunks):
    scratch = scatter_scratch(axis, rows, columns, chunks)
    return scratch[1:4] + scratch[5:]


SCATTER_REFS = 6


def kernel_params(number):
    return pltpu.CompilerParams(
        collective_id=number, has_side_effects=True, vmem_limit_bytes=VMEM_BYTES
    )


def call(kernel, number, micros, outs, scratch, *args, specs=None, out_specs=None):
    return pl.pallas_call(
        kernel,
        out_shape=outs,
        in_specs=specs or [ANY] * len(args),
        out_specs=out_specs or jax.tree.map(lambda _: ANY, outs),
        scratch_shapes=scratch,
        compiler_params=kernel_params(number),
        cost_estimate=pl.CostEstimate(
            flops=0, bytes_accessed=micros * 3_000_000, transcendentals=0
        ),
    )(*args)


def weights_kernel(
    wq, wk, wv, normed, hits, q_out, k_out, v_out, normed_out, hits_out,
    own_sems, swap_send, swap_recv, tok_send, tok_recv, g_send, g_recv,
):
    seq, group = Ring("seq"), Ring("expert")
    others = [{"seq": seq.me ^ d} for d in range(1, seq.size)]
    greet(others + group.partners())
    wrows = wq.shape[0]
    cols = wq.shape[1] // seq.size
    rows_mine = pl.ds(group.me * wrows, wrows)
    weights = [(wq, q_out), (wk, k_out), (wv, v_out)]

    def columns_of(ref, s):
        return ref.at[:, pl.ds(pl.multiple_of(s * cols, cols), cols)]

    def swap_copy(i, d):
        src, dst = weights[i]
        return remote(columns_of(src, seq.me ^ d), dst.at[seq.me, rows_mine],
                      swap_send.at[i, d], swap_recv.at[i, d], others[d - 1])

    def token_copy(d):
        return remote(normed, normed_out.at[seq.me], tok_send.at[d], tok_recv.at[d], others[d - 1])

    own = [
        pltpu.make_async_copy(columns_of(src, seq.me), dst.at[seq.me, rows_mine], own_sems.at[i])
        for i, (src, dst) in enumerate(weights)
    ]
    own.append(pltpu.make_async_copy(normed, normed_out.at[seq.me], own_sems.at[3]))
    own.append(pltpu.make_async_copy(hits, hits_out.at[group.me], own_sems.at[4]))
    for i in range(3):
        own[i].start()
        for d in range(1, seq.size):
            swap_copy(i, d).start()
    own[3].start()
    own[4].start()
    for d in range(1, seq.size):
        token_copy(d).start()

    def placed(ref):
        return lambda e: ref.at[:, pl.ds(e * wrows, wrows)]

    gathers = [
        Gather(group, placed(dst), g_send.at[i], g_recv.at[i])
        for i, (_, dst) in enumerate(weights)
    ]
    gathers.append(Gather(group, lambda e: hits_out.at[e], g_send.at[3], g_recv.at[3]))
    gathers[3].start(hits)
    for i in range(3):
        own[i].wait()
        for d in range(1, seq.size):
            remote(weights[i][1].at[seq.me ^ d, rows_mine], weights[i][1].at[seq.me ^ d, rows_mine],
                   swap_send.at[i, d], swap_recv.at[i, d], others[d - 1]).wait_recv()
        gathers[i].start(weights[i][1].at[:, rows_mine])
    for back in range(1, group.outer_count):
        for gather in gathers:
            gather.relay(back)
    for gather in gathers:
        gather.finish()
    for d in range(1, seq.size):
        there = normed_out.at[seq.me ^ d]
        remote(there, there, tok_send.at[d], tok_recv.at[d], others[d - 1]).wait_recv()
        token_copy(d).wait_send()
        for i in range(3):
            swap_copy(i, d).wait_send()
    own[3].wait()
    own[4].wait()


def gather_weights(wq, wk, wv, normed, hits):
    seq_count, group_count = lax.axis_size("seq"), lax.axis_size("expert")
    width = wq.shape[1]
    w_shape = jax.ShapeDtypeStruct((seq_count, width // seq_count, width // seq_count), BF)
    dma = pltpu.SemaphoreType.DMA
    return call(
        weights_kernel, 1, 90,
        (w_shape, w_shape, w_shape,
         jax.ShapeDtypeStruct((seq_count,) + normed.shape, BF),
         jax.ShapeDtypeStruct((group_count,) + hits.shape, BF)),
        [dma((5,)), dma((3, seq_count)), dma((3, seq_count)), dma((seq_count,)), dma((seq_count,)),
         dma((4, group_count // 2, 2)), dma((4, group_count // 2, 2))],
        wq, wk, wv, normed, hits,
    )


HIDDEN_CHUNKS = 2


def turn(values, cos_rows, sin_rows):
    return values * cos_rows + pltpu.roll(values, values.shape[1] // 2, 1) * sin_rows


def row_table(left, right):
    lanes = lax.broadcasted_iota(jnp.int32, (left.shape[0], 128), 1)
    return jnp.where(lanes == 0, left, jnp.where(lanes == 1, right, 0.0)).T[:8]


def from_row_table(table):
    return jnp.concatenate([table, jnp.zeros((120, table.shape[1]), F32)], axis=0).T


def attend_kernel(
    normed, wq, wk, wv, w_rows, bias, cosine, sine, gain_q, gain_k, tokens, gain,
    hidden_out, all_out, q_low, k_low, v_low, attended, probs_out, q_unit, k_unit, scales,
    parts, land, ringbuf, part_sems, low, normed_v, wq_v, wk_v, wv_v, rows_v, probs, row_send, row_land,
    load_sems, low_sems, g_send, g_recv, row_sems, probs_sems,
):
    seq, group = Ring("seq"), Ring("expert")
    others = [{"seq": seq.me ^ d} for d in range(1, seq.size)]
    loads = [
        pltpu.make_async_copy(src, dst, load_sems.at[i])
        for i, (src, dst) in enumerate(
            ((normed, normed_v), (wq, wq_v), (wk, wk_v), (wv, wv_v), (w_rows, rows_v))
        )
    ]
    for load in loads:
        load.start()
    greet(others + group.partners())
    length, cols = q_low.shape
    toks, width = tokens.shape
    head_dim = cosine.shape[1]
    heads = cols // head_dim
    scale = head_dim**-0.5

    def head(h):
        return slice(h * head_dim, (h + 1) * head_dim)

    def project(w, out):
        for c in range(0, cols, 256):
            out[:, c : c + 256] = dot(normed_v[...], w[:, c : c + 256]).astype(out.dtype)

    loads[0].wait()
    loads[1].wait()
    project(wq_v, q_unit)
    loads[2].wait()
    project(wk_v, k_unit)
    squares = [jnp.sum(u[...] * u[...], axis=1, keepdims=True) for u in (q_unit, k_unit)]
    row_send[...] = row_table(*squares)

    def row_copy(d):
        return remote(row_send, row_land.at[d], row_sems.at[0, d], row_sems.at[1, d], others[d - 1])

    for d in range(1, seq.size):
        row_copy(d).start()
    loads[3].wait()
    project(wv_v, v_low)
    total = row_send[...]
    for d in range(1, seq.size):
        row_copy(d).wait_recv()
        total = total + row_land[d]
    for d in range(1, seq.size):
        row_copy(d).wait_send()
    inv = from_row_table(lax.rsqrt(total / width + norm_eps))
    scales[...] = inv
    cos_rows, sin_rows = cosine[...], -sine[...]
    for i, (unit, gains, out) in enumerate(((q_unit, gain_q, q_low), (k_unit, gain_k, k_low))):
        for h in range(heads):
            value = unit[:, head(h)] * inv[:, i : i + 1]
            unit[:, head(h)] = value
            out[:, head(h)] = turn(value * gains[:, head(h)], cos_rows, sin_rows).astype(BF)

    def probs_copy(h):
        return pltpu.make_async_copy(probs.at[h], probs_out.at[h], probs_sems.at[h])

    for h in range(heads):
        for b in range(0, length, Q_BLOCK):
            rows = slice(b, b + Q_BLOCK)
            scores = dot(q_low[rows, head(h)], k_low[:, head(h)], 1, 1) * scale + bias[rows]
            weights = jnp.exp(scores - jnp.max(scores, axis=-1, keepdims=True))
            prob = weights / jnp.sum(weights, axis=-1, keepdims=True)
            probs[h, rows] = prob
            attended[rows, head(h)] = dot(prob.astype(BF), v_low[:, head(h)]).astype(BF)
        probs_copy(h).start()

    scatter = PlaceScatter(seq, parts, HIDDEN_CHUNKS, land, ringbuf, part_sems)
    loads[4].wait()

    def out_rows(s):
        at = pl.ds(pl.multiple_of(s * toks, toks), toks)
        parts[s] = dot(attended[at], rows_v[...]).astype(BF)

    for t in scatter.order:
        out_rows(seq.at(t) * 2 + 1 - seq.inner)
        scatter.start_place(t)
        out_rows(seq.at(t) * 2 + seq.inner)
    for t in scatter.order[:-1]:
        for c in range(HIDDEN_CHUNKS):
            scatter.step(t, c)
    gathers, own = [], []
    for c in range(HIDDEN_CHUNKS):
        cut = scatter.cut(c)
        hidden = tokens[cut].astype(F32) + scatter.step(0, c)
        hidden_out[cut] = hidden
        inv = lax.rsqrt(jnp.mean(hidden * hidden, axis=-1, keepdims=True) + norm_eps)
        low[cut] = (hidden * inv * gain[...]).astype(BF)
        own.append(pltpu.make_async_copy(low.at[cut], all_out.at[group.me, cut], low_sems.at[c]))
        own[c].start()
        gathers.append(
            Gather(group, lambda e, cut=cut: all_out.at[e, cut], g_send.at[c], g_recv.at[c])
        )
        gathers[c].start(low.at[cut])
    for back in range(1, group.outer_count):
        for gather in gathers:
            gather.relay(back)
    for c in range(HIDDEN_CHUNKS):
        gathers[c].finish()
        own[c].wait()
    scatter.finish()
    for h in range(heads):
        probs_copy(h).wait()


def attend(normed, wq, wk, wv, w_rows, bias, cosine, sine, gain_q, gain_k, tokens, gain):
    seq_count, group_count = lax.axis_size("seq"), lax.axis_size("expert")
    toks, width = tokens.shape
    length, cols = normed.shape[0], wq.shape[1]
    heads = cols // cosine.shape[1]
    dma = pltpu.SemaphoreType.DMA
    low = lambda *shape: pltpu.VMEM(shape, BF)
    full = lambda *shape: pltpu.VMEM(shape, F32)
    out = jax.ShapeDtypeStruct
    flat = [out((length, cols), BF)] * 4
    return call(
        attend_kernel, 2, 80,
        (out((toks, width), F32), out((group_count, toks, width), BF), *flat,
         out((heads, length, length), F32), out((length, cols), F32), out((length, cols), F32),
         out((length, 128), F32)),
        place_scratch("seq", seq_count, toks, width, HIDDEN_CHUNKS)
        + [low(toks, width), low(length, width), low(width, cols), low(width, cols), low(width, cols),
           low(cols, width), full(heads, length, length), full(8, length), full(seq_count, 8, length),
           dma((5,)), dma((HIDDEN_CHUNKS,)), dma((HIDDEN_CHUNKS, group_count // 2, 2)),
           dma((HIDDEN_CHUNKS, group_count // 2, 2)), dma((2, seq_count)), dma((heads,))],
        normed, wq, wk, wv, w_rows, bias, cosine, sine, gain_q, gain_k, tokens, gain,
        specs=[ANY] * 5 + [IN_VMEM] * 7,
        out_specs=(IN_VMEM, ANY) + (IN_VMEM,) * 4 + (ANY,) + (IN_VMEM,) * 3,
    )


ROW_CHUNKS = 2


def rows_kernel(parts, out, *scratch):
    group = Ring("expert")
    greet(group.partners())
    scatter = Scatter(group, parts, ROW_CHUNKS, *scratch)
    scatter.start()
    for t in scatter.order:
        for c in range(ROW_CHUNKS):
            total = scatter.step(t, c)
            if not t:
                out[scatter.cut(c)] = total
    scatter.finish()


def sum_rows(parts):
    rows, width = parts.shape[1:]
    return call(
        rows_kernel, 3, 50, jax.ShapeDtypeStruct((rows, width), F32),
        scatter_scratch("expert", rows, width, ROW_CHUNKS), parts, out_specs=IN_VMEM,
    )


def dot(left, right, left_dim=1, right_dim=0):
    return lax.dot_general(
        left, right, (((left_dim,), (right_dim,)), ((), ())), preferred_element_type=F32
    )


GRAD_CHUNKS = 2
TILE = 256


def expert_kernel(
    n2, cot, sel, sel_t, gates, wg, wu, wd,
    rows_out, out_parts, d_gate, d_up, d_down,
    stage, parts, routed, cot_rows, wg_v, wu_v, wd_v, scaled, ggate, gup, gate_sums,
    land, ringbuf, in_sems, w_sems, part_sems, wide_sems, out_sems, *dw_scratch,
):
    seq, group = Ring("seq"), Ring("expert")
    greet(seq.partners() + group.partners())
    groups, toks, width = n2.shape
    experts, rows, _ = routed.shape
    slots = rows // groups
    ff = wg_v.shape[1]
    n_total = experts * groups

    def stage_copy(e):
        return pltpu.make_async_copy(n2.at[e], stage.at[e], in_sems.at[0, e])

    def cot_copy(e):
        return pltpu.make_async_copy(cot.at[e], parts.at[e, :, pl.ds(0, width)], in_sems.at[1, e])

    def weight_copy(i, j):
        src, dst = ((wg, wg_v), (wu, wu_v), (wd, wd_v))[i]
        return pltpu.make_async_copy(src.at[j], dst, w_sems.at[i])

    def each(count, body):
        lax.fori_loop(0, count, lambda i, _: (body(i), 0)[1], 0)

    each(groups, lambda e: stage_copy(e).start())
    for i in range(3):
        weight_copy(i, 0).start()
    each(groups, lambda e: cot_copy(e).start())

    def pick(copy, src, dst):
        def body(e):
            copy(e).wait()
            got = dot(sel[e], src[e, :, pl.ds(0, width)]).astype(BF)
            at = pl.ds(pl.multiple_of(e * slots, slots), slots)
            for j in range(experts):
                dst[j, at] = got[j * slots : (j + 1) * slots]
        return body

    each(groups, pick(stage_copy, stage, routed))
    each(groups, pick(cot_copy, parts, cot_rows))

    for j in range(experts):
        for i in range(3):
            weight_copy(i, j).wait()
        gate_sums[j] = jnp.zeros_like(gate_sums[j])

        def hidden_tile(f, j=j):
            at = pl.ds(pl.multiple_of(f * TILE, TILE), TILE)
            gate_pre = dot(routed[j], wg_v[:, at])
            up_pre = dot(routed[j], wu_v[:, at])
            unit = dot(cot_rows[j], wd_v[at, :], 1, 1)
            gate = gates[j][:, :1]
            sig = 1.0 / (1.0 + jnp.exp(-gate_pre))
            silu = gate_pre * sig
            active = silu * up_pre
            low = active.astype(BF).astype(F32)
            gate_sums[j] += jnp.sum(unit * low, axis=-1, keepdims=True)
            scaled[j, :, at] = (low * gate).astype(BF)
            grad_active = unit * gate
            ggate[j, :, at] = (grad_active * up_pre * sig * (1.0 + gate_pre * (1.0 - sig))).astype(BF)
            gup[j, :, at] = (grad_active * silu).astype(BF)

        each(ff // TILE, hidden_tile)
        if j + 1 < experts:
            weight_copy(2, j + 1).start()

        def row_tile(d, j=j):
            at = pl.ds(pl.multiple_of(d * TILE, TILE), TILE)
            grad = dot(ggate[j], wg_v[at, :], 1, 1) + dot(gup[j], wu_v[at, :], 1, 1)
            stage[:, j * slots : (j + 1) * slots, at] = grad.astype(BF).reshape(groups, slots, TILE)

        each(width // TILE, row_tile)
        if j + 1 < experts:
            weight_copy(0, j + 1).start()
            weight_copy(1, j + 1).start()
    weight_copy(2, 0).start()

    scatter = PlaceScatter(group, parts, GRAD_CHUNKS, land, ringbuf, part_sems)
    lanes = lax.broadcasted_iota(jnp.int32, (slots, 128), 1)

    def place(e):
        parts[e, :, pl.ds(0, width)] = dot(sel_t[e], stage[e]).astype(BF)
        at = pl.ds(pl.multiple_of(e * slots, slots), slots)
        high, low = [], []
        for j in range(experts):
            value = gate_sums[j, at]
            first = value.astype(BF)
            rest = (value - first.astype(F32)).astype(BF)
            mine = group.me * experts + j
            high.append(jnp.where(lanes == mine, first.astype(F32),
                                  jnp.where(lanes == mine + n_total, rest.astype(F32), 0.0)))
        parts[e, :, pl.ds(width, 128)] = dot(
            sel_t[e], jnp.concatenate(high, axis=0).astype(BF)
        ).astype(BF)

    for t in scatter.order:
        place(group.at(t) * 2 + 1 - group.inner)
        scatter.start_place(t)
        place(group.at(t) * 2 + group.inner)

    def grad_step(t):
        for c in range(GRAD_CHUNKS):
            total = scatter.step(t, c)
            if not t:
                rows_out[scatter.cut(c)] = total

    side, short = width // seq.size, ff // seq.size

    def wide_grad(right, s, j):
        at = pl.ds(pl.multiple_of(s * side, side), side)
        return dot(routed[j, :, at], right[j], 0, 0).astype(BF)

    def send_wide(right, out, s):
        copies = [
            pltpu.make_async_copy(
                wg_v.at[pl.ds(j * side, side)], out.at[s, pl.ds(j * side, side)], wide_sems.at[j]
            )
            for j in range(experts)
        ]
        for j in range(experts):
            wg_v[pl.ds(j * side, side)] = wide_grad(right, s, j)
            copies[j].start()
        for copy in copies:
            copy.wait()

    def send_tall(s):
        at = pl.ds(pl.multiple_of(s * short, short), short)
        per = short // toks
        copies = []
        for j in range(experts):
            value = dot(scaled[j, :, at], cot_rows[j], 0, 0).astype(BF)
            for i in range(per):
                place_at = j * per + i
                stage[place_at] = value[i * toks : (i + 1) * toks]
                copies.append(pltpu.make_async_copy(
                    stage.at[place_at], d_down.at[s, pl.ds(place_at * toks, toks)],
                    out_sems.at[place_at]))
                copies[-1].start()
        for copy in copies:
            copy.wait()

    dw = KeptScatter(seq, d_gate[0], 1, wu_v, *dw_scratch)
    for t in dw.order:
        send_wide(ggate, d_gate[0], seq.at(t) * 2 + 1 - seq.inner)
        dw.start_place(t)
    grad_step(scatter.order[0])
    for t in dw.order:
        for j in range(experts):
            wu_v[pl.ds((t * experts + j) * side, side)] = wide_grad(
                ggate, seq.at(t) * 2 + seq.inner, j
            )
        if t:
            dw.step(t, 0)
    if len(scatter.order) > 2:
        grad_step(scatter.order[1])
    each(seq.size, lambda s: send_wide(gup, d_up, s))
    for t in scatter.order[2:-1]:
        grad_step(t)
    each(seq.size, send_tall)

    for j in range(experts):
        weight_copy(2, j).wait()

        def out_tile(d, j=j):
            at = pl.ds(pl.multiple_of(d * TILE, TILE), TILE)
            value = dot(scaled[j], wd_v[:, at])
            stage[:, j * slots : (j + 1) * slots, at] = value.astype(BF).reshape(groups, slots, TILE)

        each(width // TILE, out_tile)
        if j + 1 < experts:
            weight_copy(2, j + 1).start()

    def out_copy(e):
        return pltpu.make_async_copy(stage.at[e], out_parts.at[e], out_sems.at[e])

    def out_place(e):
        stage[e] = dot(sel_t[e], stage[e]).astype(BF)
        out_copy(e).start()

    each(groups, out_place)
    grad_step(0)
    d_gate[1][...] = dw.step(0, 0)
    each(groups, lambda e: out_copy(e).wait())
    scatter.finish()
    dw.finish()


def run_experts(n2, cot, sel, sel_t, gates, wg, wu, wd):
    seq_count, group_count = lax.axis_size("seq"), lax.axis_size("expert")
    experts, width, ff = wg.shape
    toks = n2.shape[1]
    rows = gates.shape[1]
    outer_count = group_count // 2
    columns = width + 128
    dma = pltpu.SemaphoreType.DMA
    side, short = width // seq_count, ff // seq_count

    def kernel(*refs):
        ins, outs, scratch = refs[:8], refs[8:14], refs[14:]
        expert_kernel(*ins, outs[0], outs[1], (outs[2], outs[3]), outs[4], outs[5], *scratch)

    low = lambda *shape: pltpu.VMEM(shape, BF)
    return call(
        kernel, 6, 120,
        (jax.ShapeDtypeStruct((toks, columns), F32),
         jax.ShapeDtypeStruct((group_count, toks, width), BF),
         jax.ShapeDtypeStruct((seq_count, experts * side, ff), BF),
         jax.ShapeDtypeStruct((experts * side, ff), F32),
         jax.ShapeDtypeStruct((seq_count, experts * side, ff), BF),
         jax.ShapeDtypeStruct((seq_count, experts * short, width), BF)),
        [low(group_count, toks, width), low(group_count, toks, columns),
         low(experts, rows, width), low(experts, rows, width),
         low(width, ff), low(width, ff), low(ff, width),
         low(experts, rows, ff), low(experts, rows, ff), low(experts, rows, ff),
         pltpu.VMEM((experts, rows, 128), F32),
         low(outer_count, toks, columns), low(outer_count - 1, toks, columns),
         dma((2, group_count)), dma((3,)), dma((4, outer_count, GRAD_CHUNKS)), dma((experts,)),
         dma((group_count,))]
        + kept_scratch("seq", experts * side, ff, 1),
        n2, cot, sel, sel_t, gates, wg, wu, wd,
        specs=[ANY, ANY, IN_VMEM, IN_VMEM, IN_VMEM, ANY, ANY, ANY],
        out_specs=(IN_VMEM, ANY, ANY, IN_VMEM, ANY, ANY),
    )


NORMED_CHUNKS = 2
CROSS_CHUNKS = 8


class Cross:
    def __init__(self, seq, parts, land, mine, crossed, bufs, stage, sems):
        self.seq, self.parts, self.land, self.mine, self.crossed = seq, parts, land, mine, crossed
        self.bufs, self.stage, self.sems = bufs, stage, sems
        self.rows = parts.shape[1] // CROSS_CHUNKS

    def swap(self, t):
        src = self.parts.at[self.seq.at(t) * 2 + 1 - self.seq.inner]
        return remote(src, self.land.at[t], self.sems.at[0, t], self.sems.at[1, t], self.seq.pair)

    def start(self):
        self.swap(1).start()
        self.swap(0).start()

    def loads(self, i):
        t, c = 1 - i // CROSS_CHUNKS, i % CROSS_CHUNKS
        cut = pl.ds(c * self.rows, self.rows)
        own = self.parts.at[self.seq.at(t) * 2 + self.seq.inner, cut]
        return [
            pltpu.make_async_copy(own, self.bufs.at[i % 2, 0], self.sems.at[2, i % 2]),
            pltpu.make_async_copy(self.land.at[t, cut], self.bufs.at[i % 2, 1], self.sems.at[3, i % 2]),
        ]

    def load(self, i):
        if i >= 2 * CROSS_CHUNKS:
            return
        if i % CROSS_CHUNKS == 0:
            self.swap(1 - i // CROSS_CHUNKS).wait_recv()
        for copy in self.loads(i):
            copy.start()

    def send(self, i):
        cut = pl.ds((i % CROSS_CHUNKS) * self.rows, self.rows)
        if i < CROSS_CHUNKS:
            return remote(self.stage.at[i % 2], self.crossed.at[cut], self.sems.at[4, i % 2],
                          self.sems.at[5, i % CROSS_CHUNKS], self.seq.next)
        return pltpu.make_async_copy(self.stage.at[i % 2], self.mine.at[cut], self.sems.at[4, i % 2])

    def wait_sent(self, i):
        if i < CROSS_CHUNKS:
            self.send(i).wait_send()
        else:
            self.send(i).wait()

    def tick(self, i):
        if i == 0:
            self.load(0)
        for copy in self.loads(i):
            copy.wait()
        self.load(i + 1)
        if i >= 2:
            self.wait_sent(i - 2)
        total = self.bufs[i % 2, 0].astype(F32) + self.bufs[i % 2, 1].astype(F32)
        self.stage[i % 2] = total.astype(BF)
        self.send(i).start()

    def finish(self):
        last = 2 * CROSS_CHUNKS
        self.wait_sent(last - 2)
        self.wait_sent(last - 1)
        for c in range(CROSS_CHUNKS):
            self.send(c).wait_recv()
        self.swap(0).wait_send()
        self.swap(1).wait_send()


def cross_scratch(parts):
    rows, columns = parts.shape[1] // CROSS_CHUNKS, parts.shape[2]
    return [pltpu.VMEM((2, 2, rows, columns), BF), pltpu.VMEM((2, rows, columns), BF),
            pltpu.SemaphoreType.DMA((6, CROSS_CHUNKS))]


def place_scratch(axis, size, rows, columns, chunks):
    outer_count = lax.axis_size(axis) // 2
    return [pltpu.VMEM((size, rows, columns), BF), pltpu.VMEM((outer_count, rows, columns), BF),
            pltpu.VMEM((max(outer_count - 1, 1), rows, columns), BF),
            pltpu.SemaphoreType.DMA((4, outer_count, chunks))]


Q_BLOCK = 256
LATE = ("w_rows", "normed", "probs", "q_unit", "k_unit", "wq", "wk", "wv")
LATE_AT = (4, 17, 9, 10, 11, 18, 19, 20)


def last_kernel(
    grad_low, grad_hidden, tokens, gain, w_rows, q_low, k_low, v_low, attended, probs,
    q_unit, k_unit, scales, gain_q, gain_k, cosine, sine, normed, wq, wk, wv, small, *refs,
    crossings,
):
    expert_parts, refs = refs[:crossings], refs[crossings:]
    late = {}
    refs, copies, load_sems = refs[: -len(LATE) - 1], refs[-len(LATE) - 1 : -1], refs[-1]
    arrays = dict(w_rows=w_rows, probs=probs, q_unit=q_unit, k_unit=k_unit, normed=normed,
                  wq=wq, wk=wk, wv=wv)
    for i, name in enumerate(LATE):
        late[name] = pltpu.make_async_copy(arrays[name], copies[i], load_sems.at[i])
    w_rows, normed, probs, q_unit, k_unit, wq, wk, wv = copies
    d_tokens, d_q, d_k, d_v, d_out, small_out = refs[:6]
    refs = refs[6:]
    cross_out, refs = refs[: 3 * crossings], refs[3 * crossings :]
    cross_bufs, refs = refs[: 3 * crossings], refs[3 * crossings :]
    place = [refs[4 * i : 4 * i + 4] for i in range(5)]
    (grad_all, normed_t, grad_att, grad_g, grad_three, dk_sum, row_send, row_land,
     low_send, low_land, sum_buf, sum_land,
     own_sem, pack_send, pack_recv, row_sems, swap_sems, sum_sems) = refs[20:]
    seq, group = Ring("seq"), Ring("expert")
    others = [{"seq": seq.me ^ d} for d in range(1, seq.size)]
    known = [{"expert": group.me ^ (1 << i)} for i in range((group.size - 1).bit_length())]
    steps = known + [{"seq": seq.me ^ (1 << i)} for i in range((seq.size - 1).bit_length())]
    for name in LATE:
        late[name].start()
    greet(others + known + [group.next, group.last])
    length, cols = q_low.shape
    width = tokens.shape[1]
    toks = tokens.shape[0]
    head_dim = cosine.shape[1]
    heads = cols // head_dim
    wrows = d_out.shape[0]
    scale = head_dim**-0.5

    crosses = [
        Cross(seq, expert_parts[i], *cross_out[3 * i : 3 * i + 3], *cross_bufs[3 * i : 3 * i + 3])
        for i in range(crossings)
    ]
    ticks = [(cross, i) for i in range(2 * CROSS_CHUNKS) for cross in crosses]
    ticks = [t for t in ticks if t[1] < CROSS_CHUNKS] + [t for t in ticks if t[1] >= CROSS_CHUNKS]

    def tick(count=1):
        for _ in range(count):
            if ticks:
                cross, i = ticks.pop(0)
                cross.tick(i)

    own = pltpu.make_async_copy(grad_low, grad_all.at[seq.me], own_sem.at[0])
    own.start()
    pack = Gather(seq, lambda s: grad_all.at[s], pack_send, pack_recv)
    pack.start(grad_low)
    for cross in crosses:
        cross.start()
    size = width // seq.size
    late["normed"].wait()
    for s in range(seq.size):
        normed_t[pl.ds(s * size, size)] = normed[:, s * size : (s + 1) * size].T
    for back in range(1, seq.outer_count):
        pack.relay(back)
    tick()
    own.wait()
    pack.finish()

    late["w_rows"].wait()
    for c in range(0, cols, Q_BLOCK):
        at = slice(c, c + Q_BLOCK)
        grad_att[:, at] = dot(
            grad_all[...].reshape(length, width), w_rows[at, :], 1, 1
        ).astype(BF)

    query_sums, key_sums, value_sums = [
        PlaceScatter(group, p[0], 1, p[1], p[2], p[3]) for p in place[:3]
    ]
    out_sums = RingFirst(group, *place[3])
    normed_sums = PlaceScatter(seq, place[4][0], NORMED_CHUNKS, *place[4][1:])

    def head(h):
        return slice(h * head_dim, (h + 1) * head_dim)

    late["probs"].wait()
    for h in range(heads):
        grad_three[2, :, head(h)] = dot(
            probs[h].astype(BF), grad_att[:, head(h)], 0, 0
        ).astype(BF)

    def weight_grad(i, sums):
        for s in range(seq.size):
            value = dot(normed_t[pl.ds(s * size, size)], grad_three[i])
            sums.x_ref[:, pl.ds(s * wrows, wrows)] = value.astype(BF).reshape(
                group.size, wrows, cols
            )
        sums.start()

    weight_grad(2, value_sums)
    tick()
    for c in range(0, width, 512):
        at = slice(c, c + 512)
        value = dot(attended[...], grad_all[:, :, at].reshape(length, 512), 0, 0)
        out_sums.parts[:, :, at] = value.astype(BF).reshape(group.size, wrows, 512)
    out_sums.start()
    tick()
    out_order, value_order = list(out_sums.order[1:]), list(value_sums.order)

    def out_step():
        if len(out_order) > 1:
            out_sums.step(out_order.pop(0))

    def value_step():
        if len(value_order) > 1:
            value_sums.step(value_order.pop(0), 0)

    row_sums = [jnp.zeros((length, 1), F32), jnp.zeros((length, 1), F32)]
    gain_row = 0
    cos_rows, sin_rows = cosine[...], sine[...]

    def through_rope(i, h, grad, unit, gains):
        turned = turn(grad, cos_rows, sin_rows)
        sum_buf[0, pl.ds(gain_rows[i], 1), pl.ds(pl.multiple_of(seq.me * cols, 128) + h * head_dim, head_dim)] = (
            jnp.sum(turned * unit, axis=0, keepdims=True)
        )
        gained = turned * gains
        grad_g[i, :, head(h)] = gained
        row_sums[i] = row_sums[i] + jnp.sum(gained * unit, axis=1, keepdims=True)

    late["q_unit"].wait()
    late["k_unit"].wait()
    sum_buf[0] = small[...]
    gain_rows = (small.shape[0] - 3, small.shape[0] - 2)
    for h in range(heads):
        queries = []
        for b in range(0, length, Q_BLOCK):
            rows = slice(b, b + Q_BLOCK)
            prob = probs[h, rows]
            grad = dot(grad_att[rows, head(h)], v_low[:, head(h)], 1, 1)
            row_dot = jnp.sum(prob * grad, axis=-1, keepdims=True)
            grad_scores = (prob * (grad - row_dot)).astype(BF)
            queries.append(dot(grad_scores, k_low[:, head(h)]) * scale)
            keys = dot(grad_scores, q_low[rows, head(h)], 0, 0)
            dk_sum[...] = keys if b == 0 else dk_sum[...] + keys
        through_rope(0, h, jnp.concatenate(queries, axis=0), q_unit[:, head(h)], gain_q[:, head(h)])
        through_rope(1, h, dk_sum[...] * scale, k_unit[:, head(h)], gain_k[:, head(h)])
        if h == 1:
            value_step()

    lanes = lax.broadcasted_iota(jnp.int32, (length, 128), 1)
    table = jnp.where(lanes == 0, row_sums[0], jnp.where(lanes == 1, row_sums[1], 0.0))
    row_send[...] = table.T[:8]

    def row_copy(d):
        return remote(row_send, row_land.at[d], row_sems.at[0, d], row_sems.at[1, d], others[d - 1])

    for d in range(1, seq.size):
        row_copy(d).start()
    out_step()
    total = row_send[...]
    for d in range(1, seq.size):
        row_copy(d).wait_recv()
        total = total + row_land[d]
    for d in range(1, seq.size):
        row_copy(d).wait_send()
    tick(2)
    means = jnp.concatenate([total / width, jnp.zeros((120, length), F32)], axis=0).T
    for i, (unit, sums) in enumerate(((q_unit, query_sums), (k_unit, key_sums))):
        for h in range(heads):
            value = grad_g[i, :, head(h)] - unit[:, head(h)] * means[:, i : i + 1]
            grad_three[i, :, head(h)] = (value * scales[:, i : i + 1]).astype(BF)
        weight_grad(i, sums)
        value_step()
    for name in ("wq", "wk", "wv"):
        late[name].wait()
    for c in range(0, width, 512):
        at = slice(c, c + 512)
        value = dot(grad_three[0], wq[at, :], 1, 1) + dot(grad_three[1], wk[at, :], 1, 1)
        value = value + dot(grad_three[2], wv[at, :], 1, 1)
        normed_sums.x_ref[:, :, at] = value.astype(BF).reshape(seq.size, toks, 512)
    normed_sums.start()
    out_step()
    tick()

    swaps = {}

    def swap_copy(i, d):
        src = low_send.at[i, pl.ds((seq.me ^ d) * wrows, wrows)]
        return remote(src, low_land.at[i, seq.me], swap_sems.at[0, i, d], swap_sems.at[1, i, d], others[d - 1])

    def send_columns(i, sums):
        low_send[i] = sums.step(0, 0).astype(BF)
        for d in range(1, seq.size):
            swap_copy(i, d).start()

    while len(value_order) > 1:
        value_step()
    for t in normed_sums.order[:-1]:
        for c in range(NORMED_CHUNKS):
            normed_sums.step(t, c)
    first, *middle = group_order(group)[:-1]
    query_sums.step(first, 0)
    tick()
    key_sums.step(first, 0)
    tick()
    while len(out_order) > 1:
        out_step()
    gain_sum = jnp.zeros((1, width), F32)
    for c in range(NORMED_CHUNKS):
        cut = normed_sums.cut(c)
        grad = normed_sums.step(0, c)
        value = tokens[cut].astype(F32)
        inv = lax.rsqrt(jnp.mean(value * value, axis=-1, keepdims=True) + norm_eps)
        unit = value * inv
        gained = grad * gain[...]
        mean = jnp.mean(gained * unit, axis=-1, keepdims=True)
        d_tokens[cut] = grad_hidden[cut] + inv * (gained - unit * mean)
        gain_sum = gain_sum + jnp.sum(grad * unit, axis=0, keepdims=True)
    sum_buf[0, pl.ds(small.shape[0] - 1, 1)] = gain_sum
    tick()
    send_columns(2, value_sums)
    out_sums.step(0)
    for t in middle:
        query_sums.step(t, 0)
        tick(2)
        key_sums.step(t, 0)
        tick(2)
    d_out[...] = out_sums.last()
    tick()
    send_columns(0, query_sums)
    send_columns(1, key_sums)

    def sum_copy(i):
        return remote(sum_buf.at[i], sum_land.at[i], sum_sems.at[0, i], sum_sems.at[1, i], steps[i])

    sum_copy(0).start()
    for i in range(len(steps)):
        sum_copy(i).wait_recv()
        total = sum_buf[i] + sum_land[i]
        if i + 1 < len(steps):
            sum_buf[i + 1] = total
            sum_copy(i + 1).start()
        else:
            small_out[...] = total
        tick()
    tick(len(ticks))
    for i, out in ((2, d_v), (0, d_q), (1, d_k)):
        for d in range(1, seq.size):
            there = low_land.at[i, seq.me ^ d]
            remote(there, there, swap_sems.at[0, i, d], swap_sems.at[1, i, d], others[d - 1]).wait_recv()
            swap_copy(i, d).wait_send()
        low_land[i, seq.me] = low_send[i, pl.ds(pl.multiple_of(seq.me * wrows, wrows), wrows)]
        for s in range(seq.size):
            out[:, s * cols : (s + 1) * cols] = low_land[i, s].astype(F32)
    for i in range(len(steps)):
        sum_copy(i).wait_send()
    for cross in crosses:
        cross.finish()
    for sums in (query_sums, key_sums, value_sums, out_sums, normed_sums):
        sums.finish()


def group_order(ring):
    return list(range(1, ring.outer_count)) + [0]


def finish_all(ins, expert_parts):
    seq_count, group_count = lax.axis_size("seq"), lax.axis_size("expert")
    (grad_low, grad_hidden, tokens, gain, w_rows, q_low, *_) = ins
    small = ins[-1]
    rows, width = tokens.shape
    length, cols = q_low.shape
    head_dim = width // HEADS
    wrows = cols // group_count
    side = seq_count * wrows
    count = (seq_count - 1).bit_length() + (group_count - 1).bit_length()
    dma = pltpu.SemaphoreType.DMA
    low = lambda *shape: pltpu.VMEM(shape, BF)
    full = lambda *shape: pltpu.VMEM(shape, F32)
    shape = lambda *dims: jax.ShapeDtypeStruct(dims, F32)
    outs = [shape(rows, width)] + [shape(wrows, width)] * 4 + [shape(*small.shape)]
    cross_outs, scratch = [], []
    for parts in expert_parts:
        size = parts.shape[1:]
        cross_outs += [jax.ShapeDtypeStruct((2,) + size, BF), jax.ShapeDtypeStruct(size, BF),
                       jax.ShapeDtypeStruct(size, BF)]
        scratch += cross_scratch(parts)
    for _ in range(3):
        scratch += place_scratch("expert", group_count, side, cols, 1)
    scratch += ring_first_scratch("expert", wrows, width)
    scratch += place_scratch("seq", seq_count, rows, width, NORMED_CHUNKS)
    scratch += [
        low(seq_count, rows, width), low(width, length), low(length, cols),
        full(2, length, cols), low(3, length, cols), full(length, head_dim),
        full(8, length), full(seq_count, 8, length),
        low(3, side, cols), low(3, seq_count, wrows, cols),
        full(count, *small.shape), full(count, *small.shape),
        dma((1,)), dma((seq_count // 2, 2)), dma((seq_count // 2, 2)), dma((2, seq_count)),
        dma((2, 3, seq_count)), dma((2, count)),
    ]
    scratch += [pltpu.VMEM(ins[i].shape, ins[i].dtype) for i in LATE_AT] + [dma((len(LATE),))]
    return call(
        partial(last_kernel, crossings=len(expert_parts)), 5, 150,
        tuple(outs + cross_outs), scratch, *ins, *expert_parts,
        specs=[ANY if i in (0, *LATE_AT) else IN_VMEM for i in range(len(ins))]
        + [ANY] * len(expert_parts),
        out_specs=tuple([IN_VMEM] * len(outs) + [ANY] * len(cross_outs)),
    )


def each(left, right, how):
    return jnp.einsum(how, left, right, preferred_element_type=F32)


def plain_experts(normed2_all, cot_all, chosen, gate_rows, w_gate, w_up, w_down):
    seq_count, group_count = lax.axis_size("seq"), lax.axis_size("expert")
    experts_local, tok_rows = w_gate.shape[0], chosen.shape[-1]
    total_experts = experts_local * group_count
    chosen_low = chosen.astype(BF)

    def pick_rows(values):
        return jnp.einsum("ejmt,etd->jemd", chosen_low, values, preferred_element_type=F32).astype(BF)

    def place_rows(values):
        return jnp.einsum("ejmt,jemd->etd", chosen_low, values, preferred_element_type=F32).astype(BF)

    routed = pick_rows(normed2_all)
    cot_rows = pick_rows(cot_all)

    gate_pre = each(routed, w_gate, "jemd,jdf->jemf")
    up_pre = each(routed, w_up, "jemd,jdf->jemf")
    sigmoid_gate = jax.nn.sigmoid(gate_pre)
    silu_gate = gate_pre * sigmoid_gate
    active = silu_gate * up_pre
    active_low = active.astype(BF)
    grad_unit = each(cot_rows, w_down, "jemd,jfd->jemf")
    grad_gate_rows = jnp.sum(grad_unit * active_low.astype(F32), axis=-1)
    grad_active = grad_unit * gate_rows
    grad_gate_low = (
        grad_active * up_pre * sigmoid_gate * (1.0 + gate_pre * (1.0 - sigmoid_gate))
    ).astype(BF)
    grad_up_low = (grad_active * silu_gate).astype(BF)
    grad_routed = each(grad_gate_low, w_gate, "jemf,jdf->jemd")
    grad_routed = (grad_routed + each(grad_up_low, w_up, "jemf,jdf->jemd")).astype(BF)
    grad_parts = place_rows(grad_routed)
    grad_normed2 = sum_rows(grad_parts)
    grad_probs_parts = jnp.einsum(
        "ejmt,jem->etj", chosen.astype(F32), grad_gate_rows, precision=lax.Precision.HIGHEST
    )
    grad_probs = lax.all_to_all(grad_probs_parts, "expert", split_axis=0, concat_axis=0, tiled=True)
    grad_probs = grad_probs.transpose(1, 0, 2).reshape(tok_rows, total_experts)

    expert_out = each(active_low, w_down, "jemf,jfd->jemd") * gate_rows
    out_parts = place_rows(expert_out.astype(BF))

    active_scaled = (active_low.astype(F32) * gate_rows).astype(BF)

    def expert_grad(left, right):
        grad = jnp.einsum("jemd,jemf->jdf", left, right, preferred_element_type=F32).astype(BF)
        rows = grad.shape[1] // seq_count
        grad = grad.reshape(experts_local, seq_count, rows, grad.shape[2])
        return scatter_sum(
            [lax.dynamic_index_in_dim(grad, o, 1, keepdims=False) for o in owners("seq")], "seq"
        )

    d_w_gate = expert_grad(routed, grad_gate_low)
    d_w_up = expert_grad(routed, grad_up_low)
    d_w_down = expert_grad(active_scaled, cot_rows)
    return grad_normed2, grad_probs, out_parts, d_w_gate, d_w_up, d_w_down


def local(
    tokens,
    lengths,
    routes,
    gain_attn,
    w_query,
    w_key,
    w_value,
    gain_query,
    gain_key,
    w_out,
    gain_mlp,
    router,
    w_gate,
    w_up,
    w_down,
    cotangent,
):
    seq_count = lax.axis_size("seq")
    group_count = lax.axis_size("expert")
    seq_me = lax.axis_index("seq")
    group_me = lax.axis_index("expert")
    tok_rows, width = tokens.shape[1], tokens.shape[2]
    head_dim = width // HEADS
    heads = HEADS // seq_count
    cols = width // seq_count
    wrows = w_query.shape[0]
    length = tok_rows * seq_count
    experts_local = w_gate.shape[0]
    total_experts = experts_local * group_count
    slots = MOST
    score_scale = head_dim ** (-0.5)
    inputs = tokens[0].astype(F32)

    places = jnp.arange(length, dtype=jnp.int32)
    doc_ends = jnp.cumsum(lengths[0])
    passed = (places[:, None] >= doc_ends[None, :]).astype(jnp.int32)
    docs = jnp.sum(passed, axis=1)
    offsets = places - jnp.sum(passed * lengths[0][None, :], axis=1)
    allowed = (docs[:, None] == docs[None, :]) & (places[None, :] <= places[:, None])
    half = head_dim // 2
    inverse = 10000.0 ** (-jnp.arange(half, dtype=F32) / half)
    angles = offsets.astype(F32)[:, None] * inverse[None, :]
    cosine, sine = jnp.cos(angles), jnp.sin(angles)
    cosine = jnp.concatenate([cosine, cosine], axis=1)
    sine = jnp.concatenate([sine, -sine], axis=1)
    bias = jnp.where(allowed, 0.0, masked_score).astype(F32)

    expert_ids = jnp.arange(128, dtype=jnp.int32)
    hits = jnp.any(routes[0][:, :, None] == expert_ids[None, None, :], axis=1).astype(BF)
    cot_all = lax.all_gather(cotangent[0], "expert", axis=0)
    w_rows = lax.all_gather(w_out, "expert", axis=0, tiled=True)
    normed, attn_norm_back = jax.vjp(rms_norm, inputs, gain_attn)
    wq_cols, wk_cols, wv_cols, normed_all, hits_all = gather_weights(
        w_query, w_key, w_value, normed.astype(BF), hits
    )
    normed_all = normed_all.reshape(length, width)
    w_cols = [w.reshape(width, cols) for w in (wq_cols, wk_cols, wv_cols)]
    gain_q = lax.dynamic_slice_in_dim(gain_query, seq_me * cols, cols)
    gain_k = lax.dynamic_slice_in_dim(gain_key, seq_me * cols, cols)
    (hidden, normed2_all, query_low, key_low, value_low, attended_low, probs, query_unit, key_unit,
     scales) = attend(normed_all, *w_cols, w_rows, bias, cosine, sine, gain_q[None], gain_k[None],
                      tokens[0], gain_mlp[None])
    normed2, mlp_norm_back = jax.vjp(rms_norm, hidden, gain_mlp)
    normed2_low = normed2.astype(BF)

    first_expert = group_me * experts_local
    hit = lax.dynamic_slice_in_dim(hits_all, first_expert, experts_local, axis=2)
    hit = hit.transpose(0, 2, 1)
    before = (jnp.arange(tok_rows)[:, None] < jnp.arange(tok_rows)[None, :]).astype(BF)
    rank = jnp.einsum("ejt,tu->eju", hit, before, preferred_element_type=F32)
    slot_ids = jnp.arange(slots, dtype=jnp.int32)
    chosen = (hit[:, :, None, :] > 0) & (rank.astype(jnp.int32)[:, :, None, :] == slot_ids[None, None, :, None])
    chosen_low = chosen.astype(BF)

    logits_all = jnp.einsum("etd,dn->etn", normed2_all, router, preferred_element_type=F32)
    probs_all = jax.nn.softmax(logits_all, axis=-1)
    mine = lax.dynamic_slice_in_dim(probs_all, first_expert, experts_local, axis=2)
    gate_rows = jnp.einsum(
        "ejmt,etj->jem", chosen.astype(F32), mine, precision=lax.Precision.HIGHEST
    )[..., None]

    roomy = group_count * slots <= 512
    if roomy:
        both = chosen_low.reshape(group_count, experts_local * slots, tok_rows)
        gate_wide = jnp.broadcast_to(
            gate_rows.reshape(experts_local, group_count * slots, 1),
            (experts_local, group_count * slots, 128),
        )
        rows_sum, out_parts, _, d_w_gate, up_parts, down_parts = run_experts(
            normed2_all, cot_all, both, both.transpose(0, 2, 1), gate_wide, w_gate, w_up, w_down
        )
        grad_normed2 = rows_sum[:, :width]
        grad_probs = (
            rows_sum[:, width : width + total_experts]
            + rows_sum[:, width + total_experts : width + 2 * total_experts]
        )
        expert_parts = (up_parts, down_parts)
    else:
        grad_normed2, grad_probs, out_parts, d_w_gate, d_w_up, d_w_down = plain_experts(
            normed2_all, cot_all, chosen, gate_rows, w_gate, w_up, w_down
        )
        expert_parts = ()
    out_sum = lax.psum_scatter(out_parts, "expert", scatter_dimension=0, tiled=False)

    router_probs, softmax_back = jax.vjp(
        partial(jax.nn.softmax, axis=-1), product(normed2_low, router)
    )
    (grad_logits,) = softmax_back(grad_probs)
    grad_logits_low = grad_logits.astype(BF)
    grad_router = jnp.einsum("td,te->ed", normed2_low, grad_logits_low, preferred_element_type=F32)
    grad_normed2 = grad_normed2 + jnp.einsum(
        "te,de->td", grad_logits_low, router, preferred_element_type=F32
    )
    grad_hidden_part, grad_gain_mlp = mlp_norm_back(grad_normed2)
    grad_hidden = cotangent[0].astype(F32) + grad_hidden_part

    spare = -(total_experts + 4) % 8 + 3
    small = jnp.concatenate([grad_router, grad_gain_mlp[None], jnp.zeros((spare, width), F32)])
    d_tokens, d_w_query, d_w_key, d_w_value, d_w_out, small, *crossed = finish_all(
        (grad_hidden.astype(BF), grad_hidden, tokens[0], gain_attn[None], w_rows, query_low,
         key_low, value_low, attended_low, probs, query_unit, key_unit, scales,
         gain_q[None], gain_k[None], cosine, sine, normed_all, *w_cols, small),
        expert_parts,
    )
    mixed = hidden + after(out_sum, d_w_out).astype(F32)
    if roomy:
        d_w_gate = d_w_gate.reshape(experts_local, width // seq_count, -1)
        d_w_up = (crossed[1].astype(F32) + crossed[2].astype(F32)).reshape(d_w_gate.shape)
        d_w_down = (crossed[4].astype(F32) + crossed[5].astype(F32)).reshape(
            experts_local, -1, width
        )
    return (
        mixed.astype(BF)[None],
        d_tokens[None],
        small[-1],
        d_w_query,
        d_w_key,
        d_w_value,
        small[-3],
        small[-2],
        d_w_out,
        small[total_experts],
        small[:total_experts].T,
        d_w_gate,
        d_w_up,
        d_w_down,
    )


def solution(mesh):
    return jax.shard_map(
        local,
        mesh=mesh,
        in_specs=(
            P("expert", "seq", None),
            P("expert", None),
            P("expert", "seq", None),
            P(),
            P(("seq", "expert"), None),
            P(("seq", "expert"), None),
            P(("seq", "expert"), None),
            P(),
            P(),
            P(("seq", "expert"), None),
            P(),
            P(),
            P("expert", None, None),
            P("expert", None, None),
            P("expert", None, None),
            P("expert", "seq", None),
        ),
        out_specs=(
            P("expert", "seq", None),
            P("expert", "seq", None),
            P(),
            P(("seq", "expert"), None),
            P(("seq", "expert"), None),
            P(("seq", "expert"), None),
            P(),
            P(),
            P(("seq", "expert"), None),
            P(),
            P(),
            P("expert", "seq", None),
            P("expert", "seq", None),
            P("expert", "seq", None),
        ),
        check_vma=False,
    )
```

```python
from functools import partial

import jax
import jax.numpy as jnp
from jax import lax
from jax.experimental import pallas as pl
from jax.experimental.pallas import tpu as pltpu
from jax.sharding import PartitionSpec as P

HEADS = 16
MOST = 64
BF = jnp.bfloat16
F32 = jnp.float32

norm_eps = 1e-05
masked_score = -1e30


MESH = pl.DeviceIdType.MESH
ANY = pl.BlockSpec(memory_space=pl.ANY)
IN_VMEM = pl.BlockSpec(memory_space=pltpu.VMEM)
VMEM_BYTES = 63 << 20


def product(left, right):
    return jnp.dot(left, right, preferred_element_type=F32)


def rms_norm(values, norm_gain):
    return (
        values * lax.rsqrt(jnp.mean(values * values, axis=-1, keepdims=True) + norm_eps) * norm_gain
    )


def swap(value, axis):
    n = lax.axis_size(axis)
    return lax.ppermute(value, axis, [(i, i ^ 1) for i in range(n)])


def shift(value, axis):
    n = lax.axis_size(axis)
    return lax.ppermute(value, axis, [(i, (i + 2) % n) for i in range(n)])


def flip(value, axis, delta):
    n = lax.axis_size(axis)
    return lax.ppermute(value, axis, [(i, i ^ delta) for i in range(n)])


def owners(axis):
    n = lax.axis_size(axis)
    me = lax.axis_index(axis)
    outer, inner = me // 2, me % 2
    return [((outer - i) % (n // 2)) * 2 + (inner ^ b) for i in range(n // 2) for b in range(2)]


def gather_blocks(value, axis):
    blocks = []
    current = value
    for i in range(lax.axis_size(axis) // 2):
        if i:
            current = shift(current, axis)
        blocks += [current, swap(current, axis)]
    return blocks


def add_low(left, right):
    return (left.astype(F32) + right.astype(F32)).astype(BF)


def scatter_sum(blocks, axis):
    outer_count = lax.axis_size(axis) // 2
    pairs = {}
    for t in list(range(1, outer_count)) + [0]:
        arrived = swap(blocks[2 * t + 1], axis)
        pairs[t] = blocks[2 * t].astype(F32) + arrived.astype(F32)
    total = pairs[1 % outer_count]
    for t in range(1, outer_count):
        arrived = shift(total.astype(BF), axis)
        total = arrived.astype(F32) + pairs[(t + 1) % outer_count]
    return total


def all_sum(value, axes):
    for axis in axes:
        delta = 1
        while delta < lax.axis_size(axis):
            value = value + flip(value, axis, delta)
            delta *= 2
    return value


def exchange(parts, axis):
    n = lax.axis_size(axis)
    me = lax.axis_index(axis)
    out = parts
    for delta in range(1, n):
        other = me ^ delta
        got = flip(lax.dynamic_index_in_dim(parts, other, 0, keepdims=False), axis, delta)
        out = lax.dynamic_update_index_in_dim(out, got, other, 0)
    return out


def after(value, *others):
    return lax.optimization_barrier((value,) + others)[0]


def remote(src, dst, send_sem, recv_sem, device):
    return pltpu.make_async_remote_copy(
        src_ref=src,
        dst_ref=dst,
        send_sem=send_sem,
        recv_sem=recv_sem,
        device_id=device,
        device_id_type=MESH,
    )


def greet(devices):
    barrier = pltpu.get_barrier_semaphore()
    for device in devices:
        pl.semaphore_signal(barrier, inc=1, device_id=device, device_id_type=MESH)
    pl.semaphore_wait(barrier, len(devices))


class Ring:
    def __init__(self, axis):
        self.axis = axis
        self.size = lax.axis_size(axis)
        self.outer_count = self.size // 2
        self.me = lax.axis_index(axis)
        self.outer, self.inner = self.me // 2, self.me % 2
        self.pair = {axis: self.outer * 2 + (1 - self.inner)}
        self.next = {axis: self.at(-1) * 2 + self.inner}
        self.last = {axis: self.at(1) * 2 + self.inner}

    def at(self, back):
        return lax.rem(self.outer - back + self.outer_count, self.outer_count)

    def partners(self):
        if self.outer_count == 1:
            return [self.pair]
        if self.outer_count == 2:
            return [self.pair, self.next]
        return [self.pair, self.next, self.last]


class Gather:
    def __init__(self, ring, place, send_sems, recv_sems):
        self.ring, self.place = ring, place
        self.send_sems, self.recv_sems = send_sems, recv_sems
        self.copies = []

    def block(self, back):
        return self.place(self.ring.at(back) * 2 + self.ring.inner)

    def _send(self, back, src):
        ring = self.ring
        if back < ring.outer_count - 1:
            copy = remote(src, self.block(back), self.send_sems.at[back, 0],
                          self.recv_sems.at[back + 1, 0], ring.next)
            copy.start()
            self.copies.append(copy)
        copy = remote(src, self.block(back), self.send_sems.at[back, 1],
                      self.recv_sems.at[back, 1], ring.pair)
        copy.start()
        self.copies.append(copy)

    def start(self, src):
        self._send(0, src)

    def relay(self, back):
        dst = self.block(back)
        remote(dst, dst, self.send_sems.at[back - 1, 0], self.recv_sems.at[back, 0],
               self.ring.next).wait_recv()
        self._send(back, dst)

    def finish(self):
        ring = self.ring
        for back in range(ring.outer_count):
            dst = self.place(ring.at(back) * 2 + 1 - ring.inner)
            remote(dst, dst, self.send_sems.at[back, 1], self.recv_sems.at[back, 1],
                   ring.pair).wait_recv()
        for copy in self.copies:
            copy.wait_send()


def gather_sems(ring, chunks):
    shape = (chunks, ring.outer_count, 2)
    return [pltpu.SemaphoreType.DMA(shape), pltpu.SemaphoreType.DMA(shape)]


class Scatter:
    def __init__(self, ring, x_ref, chunks, own, land, ringbuf, out, own_sems, sems):
        self.ring, self.x_ref, self.chunks = ring, x_ref, chunks
        self.own, self.land, self.ringbuf, self.out = own, land, ringbuf, out
        self.own_sems, self.sems = own_sems, sems
        self.order = list(range(1, ring.outer_count)) + [0]
        self.rows = x_ref.shape[1] // chunks

    def cut(self, c):
        return pl.ds(c * self.rows, self.rows)

    def pair_copy(self, t, c):
        ring = self.ring
        src = self.x_ref.at[ring.at(t) * 2 + 1 - ring.inner, self.cut(c)]
        return remote(src, self.land.at[t, self.cut(c)], self.sems.at[0, t, c],
                      self.sems.at[1, t, c], ring.pair)

    def slot(self, t):
        return (t - 2) % self.ring.outer_count

    def own_copy(self, t):
        src = self.x_ref.at[self.ring.at(t) * 2 + self.ring.inner]
        return pltpu.make_async_copy(src, self.own.at[t], self.own_sems.at[t])

    def ring_copy(self, t, c):
        to = (t + 1) % self.ring.outer_count
        return remote(self.out.at[t - 1, self.cut(c)], self.ringbuf.at[self.slot(to), self.cut(c)],
                      self.sems.at[2, t, c], self.sems.at[3, to, c], self.ring.next)

    def start_place(self, t):
        self.own_copy(t).start()
        for c in range(self.chunks):
            self.pair_copy(t, c).start()

    def start(self):
        for t in self.order:
            self.start_place(t)

    def mine(self, t, c):
        return self.own[t, self.cut(c)]

    def arrive(self, t, c):
        if c == 0:
            self.own_copy(t).wait()
        self.pair_copy(t, c).wait_recv()

    def step(self, t, c):
        self.arrive(t, c)
        cut = self.cut(c)
        total = self.mine(t, c).astype(F32) + self.land[t, cut].astype(F32)
        if t != self.order[0]:
            self.ring_copy((t - 1) % self.ring.outer_count, c).wait_recv()
            total = total + self.ringbuf[self.slot(t), cut].astype(F32)
        if t:
            self.out[t - 1, cut] = total.astype(BF)
            self.ring_copy(t, c).start()
        return total

    def finish(self):
        for t in self.order:
            for c in range(self.chunks):
                self.pair_copy(t, c).wait_send()
                if t:
                    self.ring_copy(t, c).wait_send()


class RingFirst:
    def __init__(self, ring, parts, land, ringbuf, sems):
        self.ring, self.parts, self.land, self.ringbuf, self.sems = ring, parts, land, ringbuf, sems
        self.order = list(range(1, ring.outer_count)) + [0]

    def two(self, t):
        return pl.ds(self.ring.at(t) * 2, 2)

    def ring_copy(self, t):
        to = (t + 1) % self.ring.outer_count
        slot = (to - 2) % self.ring.outer_count
        return remote(self.parts.at[self.two(t)], self.ringbuf.at[slot], self.sems.at[0, t],
                      self.sems.at[1, to], self.ring.next)

    def pair_copy(self):
        src = self.parts.at[self.ring.outer * 2 + 1 - self.ring.inner]
        return remote(src, self.land, self.sems.at[2, 0], self.sems.at[3, 0], self.ring.pair)

    def start(self):
        self.ring_copy(1).start()

    def step(self, t):
        self.ring_copy((t - 1) % self.ring.outer_count).wait_recv()
        slot = (t - 2) % self.ring.outer_count
        total = self.parts[self.two(t)].astype(F32) + self.ringbuf[slot].astype(F32)
        self.parts[self.two(t)] = total.astype(BF)
        if t:
            self.ring_copy(t).start()
        else:
            self.pair_copy().start()

    def last(self):
        self.pair_copy().wait_recv()
        mine = self.parts[self.ring.outer * 2 + self.ring.inner]
        return mine.astype(F32) + self.land[...].astype(F32)

    def finish(self):
        for t in self.order[:-1]:
            self.ring_copy(t).wait_send()
        self.pair_copy().wait_send()


def ring_first_scratch(axis, rows, columns):
    size = lax.axis_size(axis)
    low = lambda *shape: pltpu.VMEM(shape, BF)
    return [low(size, rows, columns), low(rows, columns), low(size // 2 - 1, 2, rows, columns),
            pltpu.SemaphoreType.DMA((4, size // 2))]


class PlaceScatter(Scatter):
    def __init__(self, ring, parts, chunks, land, ringbuf, sems):
        super().__init__(ring, parts, chunks, None, land, ringbuf, None, None, sems)

    def block(self, t):
        return self.ring.at(t) * 2 + self.ring.inner

    def ring_copy(self, t, c):
        to = (t + 1) % self.ring.outer_count
        return remote(self.x_ref.at[self.block(t), self.cut(c)], self.ringbuf.at[self.slot(to), self.cut(c)],
                      self.sems.at[2, t, c], self.sems.at[3, to, c], self.ring.next)

    def start_place(self, t):
        for c in range(self.chunks):
            self.pair_copy(t, c).start()

    def step(self, t, c):
        self.pair_copy(t, c).wait_recv()
        cut, mine = self.cut(c), self.block(t)
        total = self.x_ref[mine, cut].astype(F32) + self.land[t, cut].astype(F32)
        if t != self.order[0]:
            self.ring_copy((t - 1) % self.ring.outer_count, c).wait_recv()
            total = total + self.ringbuf[self.slot(t), cut].astype(F32)
        if t:
            self.x_ref[mine, cut] = total.astype(BF)
            self.ring_copy(t, c).start()
        return total


def scatter_scratch(axis, rows, columns, chunks):
    outer_count = lax.axis_size(axis) // 2
    buf = pltpu.VMEM((outer_count, rows, columns), BF)
    less = pltpu.VMEM((max(outer_count - 1, 1), rows, columns), BF)
    return [buf, buf, less, less, pltpu.SemaphoreType.DMA((outer_count,)),
            pltpu.SemaphoreType.DMA((4, outer_count, chunks))]


SCATTER_REFS = 6


def kernel_params(number):
    return pltpu.CompilerParams(
        collective_id=number, has_side_effects=True, vmem_limit_bytes=VMEM_BYTES
    )


def call(kernel, number, micros, outs, scratch, *args, specs=None, out_specs=None):
    return pl.pallas_call(
        kernel,
        out_shape=outs,
        in_specs=specs or [ANY] * len(args),
        out_specs=out_specs or jax.tree.map(lambda _: ANY, outs),
        scratch_shapes=scratch,
        compiler_params=kernel_params(number),
        cost_estimate=pl.CostEstimate(
            flops=0, bytes_accessed=micros * 3_000_000, transcendentals=0
        ),
    )(*args)


def weights_kernel(
    wq, wk, wv, tokens, gain, routes, lengths, frequency,
    q_out, k_out, v_out, normed_out, hits_out, cos_out, sin_out, bias_out,
    normed, hits, own_sems, swap_send, swap_recv, tok_send, tok_recv, g_send, g_recv,
):
    seq, group = Ring("seq"), Ring("expert")
    others = [{"seq": seq.me ^ d} for d in range(1, seq.size)]
    value = tokens[...].astype(F32)
    inv = lax.rsqrt(jnp.mean(value * value, axis=-1, keepdims=True) + norm_eps)
    normed[...] = (value * inv * gain[...]).astype(BF)
    names = lax.broadcasted_iota(jnp.int32, hits.shape, 1)
    hit = jnp.zeros(hits.shape, F32)
    for k in range(routes.shape[1]):
        hit = jnp.where(routes[:, k : k + 1] == names, 1.0, hit)
    hits[...] = hit.astype(BF)
    greet(others + group.partners())
    wrows = wq.shape[0]
    cols = wq.shape[1] // seq.size
    rows_mine = pl.ds(group.me * wrows, wrows)
    weights = [(wq, q_out), (wk, k_out), (wv, v_out)]

    def columns_of(ref, s):
        return ref.at[:, pl.ds(pl.multiple_of(s * cols, cols), cols)]

    def swap_copy(i, d):
        src, dst = weights[i]
        return remote(columns_of(src, seq.me ^ d), dst.at[seq.me, rows_mine],
                      swap_send.at[i, d], swap_recv.at[i, d], others[d - 1])

    def token_copy(d):
        return remote(normed, normed_out.at[seq.me], tok_send.at[d], tok_recv.at[d], others[d - 1])

    own = [
        pltpu.make_async_copy(columns_of(src, seq.me), dst.at[seq.me, rows_mine], own_sems.at[i])
        for i, (src, dst) in enumerate(weights)
    ]
    own.append(pltpu.make_async_copy(normed, normed_out.at[seq.me], own_sems.at[3]))
    own.append(pltpu.make_async_copy(hits, hits_out.at[group.me], own_sems.at[4]))
    for i in range(3):
        own[i].start()
        for d in range(1, seq.size):
            swap_copy(i, d).start()
    own[3].start()
    own[4].start()
    for d in range(1, seq.size):
        token_copy(d).start()

    length = bias_out.shape[0]

    def starts_of(places):
        first, doc = jnp.zeros_like(places), jnp.zeros_like(places)
        end = jnp.zeros((1, 1), jnp.int32)
        for d in range(lengths.shape[1]):
            end = end + lengths[:, d : d + 1]
            passed = places >= end
            first = jnp.where(passed, end, first)
            doc = doc + jnp.where(passed, 1, 0)
        return first, doc

    column = lax.broadcasted_iota(jnp.int32, (length, 128), 0)
    first, doc = starts_of(column)
    angles = (column - first).astype(F32) * frequency[...]
    left = lax.broadcasted_iota(jnp.int32, (length, 128), 1) < 64
    cos_out[...] = jnp.cos(angles)
    sine = jnp.sin(angles)
    sin_out[...] = jnp.where(left, sine, -sine)
    row = lax.broadcasted_iota(jnp.int32, (1, length), 1)
    row_doc = starts_of(row)[1]
    bias_out[...] = jnp.where(
        (doc[:, :1] == row_doc) & (row <= column[:, :1]), 0.0, masked_score
    )

    def placed(ref):
        return lambda e: ref.at[:, pl.ds(e * wrows, wrows)]

    gathers = [
        Gather(group, placed(dst), g_send.at[i], g_recv.at[i])
        for i, (_, dst) in enumerate(weights)
    ]
    gathers.append(Gather(group, lambda e: hits_out.at[e], g_send.at[3], g_recv.at[3]))
    gathers[3].start(hits)
    for i in range(3):
        own[i].wait()
        for d in range(1, seq.size):
            remote(weights[i][1].at[seq.me ^ d, rows_mine], weights[i][1].at[seq.me ^ d, rows_mine],
                   swap_send.at[i, d], swap_recv.at[i, d], others[d - 1]).wait_recv()
        gathers[i].start(weights[i][1].at[:, rows_mine])
    for back in range(1, group.outer_count):
        for gather in gathers:
            gather.relay(back)
    for gather in gathers:
        gather.finish()
    for d in range(1, seq.size):
        there = normed_out.at[seq.me ^ d]
        remote(there, there, tok_send.at[d], tok_recv.at[d], others[d - 1]).wait_recv()
        token_copy(d).wait_send()
        for i in range(3):
            swap_copy(i, d).wait_send()
    own[3].wait()
    own[4].wait()


def gather_weights(wq, wk, wv, tokens, gain, routes, lengths, frequency):
    seq_count, group_count = lax.axis_size("seq"), lax.axis_size("expert")
    width = wq.shape[1]
    w_shape = jax.ShapeDtypeStruct((seq_count, width // seq_count, width // seq_count), BF)
    rows = tokens.shape[0]
    length = rows * seq_count
    dma = pltpu.SemaphoreType.DMA
    return call(
        weights_kernel, 1, 90,
        (w_shape, w_shape, w_shape,
         jax.ShapeDtypeStruct((seq_count,) + tokens.shape, BF),
         jax.ShapeDtypeStruct((group_count, rows, 128), BF),
         jax.ShapeDtypeStruct((length, 128), F32), jax.ShapeDtypeStruct((length, 128), F32),
         jax.ShapeDtypeStruct((length, length), F32)),
        [pltpu.VMEM(tokens.shape, BF), pltpu.VMEM((rows, 128), BF), dma((5,)), dma((3, seq_count)), dma((3, seq_count)), dma((seq_count,)), dma((seq_count,)),
         dma((4, group_count // 2, 2)), dma((4, group_count // 2, 2))],
        wq, wk, wv, tokens, gain, routes, lengths, frequency,
        specs=[ANY] * 3 + [IN_VMEM] * 5, out_specs=(ANY,) * 5 + (IN_VMEM,) * 3,
    )


HIDDEN_CHUNKS = 2


def turn(values, cos_rows, sin_rows):
    return values * cos_rows + pltpu.roll(values, values.shape[1] // 2, 1) * sin_rows


def row_table(left, right):
    lanes = lax.broadcasted_iota(jnp.int32, (left.shape[0], 128), 1)
    return jnp.where(lanes == 0, left, jnp.where(lanes == 1, right, 0.0)).T[:8]


def from_row_table(table):
    return jnp.concatenate([table, jnp.zeros((120, table.shape[1]), F32)], axis=0).T


def attend_kernel(
    normed, wq, wk, wv, w_rows, bias, cosine, sine, gain_q, gain_k, tokens, gain,
    hidden_out, all_out, q_low, k_low, v_low, attended, probs_out, q_unit, k_unit, scales,
    parts, land, ringbuf, part_sems, low, normed_v, wq_v, wk_v, wv_v, rows_v, probs, row_send, row_land,
    load_sems, low_sems, g_send, g_recv, row_sems, probs_sems,
):
    seq, group = Ring("seq"), Ring("expert")
    others = [{"seq": seq.me ^ d} for d in range(1, seq.size)]
    loads = [
        pltpu.make_async_copy(src, dst, load_sems.at[i])
        for i, (src, dst) in enumerate(
            ((normed, normed_v), (wq, wq_v), (wk, wk_v), (wv, wv_v), (w_rows, rows_v))
        )
    ]
    for load in loads:
        load.start()
    greet(others + group.partners())
    length, cols = q_low.shape
    toks, width = tokens.shape
    head_dim = cosine.shape[1]
    heads = cols // head_dim
    scale = head_dim**-0.5

    def head(h):
        return slice(h * head_dim, (h + 1) * head_dim)

    def project(w, out):
        for c in range(0, cols, 256):
            out[:, c : c + 256] = dot(normed_v[...], w[:, c : c + 256]).astype(out.dtype)

    loads[0].wait()
    loads[1].wait()
    project(wq_v, q_unit)
    loads[2].wait()
    project(wk_v, k_unit)
    squares = [jnp.sum(u[...] * u[...], axis=1, keepdims=True) for u in (q_unit, k_unit)]
    row_send[...] = row_table(*squares)

    def row_copy(d):
        return remote(row_send, row_land.at[d], row_sems.at[0, d], row_sems.at[1, d], others[d - 1])

    for d in range(1, seq.size):
        row_copy(d).start()
    loads[3].wait()
    project(wv_v, v_low)
    total = row_send[...]
    for d in range(1, seq.size):
        row_copy(d).wait_recv()
        total = total + row_land[d]
    for d in range(1, seq.size):
        row_copy(d).wait_send()
    inv = from_row_table(lax.rsqrt(total / width + norm_eps))
    scales[...] = inv
    cos_rows, sin_rows = cosine[...], -sine[...]
    for i, (unit, gains, out) in enumerate(((q_unit, gain_q, q_low), (k_unit, gain_k, k_low))):
        for h in range(heads):
            value = unit[:, head(h)] * inv[:, i : i + 1]
            unit[:, head(h)] = value
            at = pl.ds(pl.multiple_of(seq.me * cols + h * head_dim, head_dim), head_dim)
            out[:, head(h)] = turn(value * gains[:, at], cos_rows, sin_rows).astype(BF)

    def probs_copy(h):
        return pltpu.make_async_copy(probs.at[h], probs_out.at[h], probs_sems.at[h])

    for h in range(heads):
        for b in range(0, length, Q_BLOCK):
            rows = slice(b, b + Q_BLOCK)
            scores = dot(q_low[rows, head(h)], k_low[:, head(h)], 1, 1) * scale + bias[rows]
            weights = jnp.exp(scores - jnp.max(scores, axis=-1, keepdims=True))
            prob = weights / jnp.sum(weights, axis=-1, keepdims=True)
            probs[h, rows] = prob
            attended[rows, head(h)] = dot(prob.astype(BF), v_low[:, head(h)]).astype(BF)
        probs_copy(h).start()

    scatter = PlaceScatter(seq, parts, HIDDEN_CHUNKS, land, ringbuf, part_sems)
    loads[4].wait()

    def out_rows(s):
        at = pl.ds(pl.multiple_of(s * toks, toks), toks)
        parts[s] = dot(attended[at], rows_v[...]).astype(BF)

    for t in scatter.order:
        out_rows(seq.at(t) * 2 + 1 - seq.inner)
        scatter.start_place(t)
        out_rows(seq.at(t) * 2 + seq.inner)
    for t in scatter.order[:-1]:
        for c in range(HIDDEN_CHUNKS):
            scatter.step(t, c)
    gathers, own = [], []
    for c in range(HIDDEN_CHUNKS):
        cut = scatter.cut(c)
        hidden = tokens[cut].astype(F32) + scatter.step(0, c)
        hidden_out[cut] = hidden
        inv = lax.rsqrt(jnp.mean(hidden * hidden, axis=-1, keepdims=True) + norm_eps)
        low[cut] = (hidden * inv * gain[...]).astype(BF)
        own.append(pltpu.make_async_copy(low.at[cut], all_out.at[group.me, cut], low_sems.at[c]))
        own[c].start()
        gathers.append(
            Gather(group, lambda e, cut=cut: all_out.at[e, cut], g_send.at[c], g_recv.at[c])
        )
        gathers[c].start(low.at[cut])
    for back in range(1, group.outer_count):
        for gather in gathers:
            gather.relay(back)
    for c in range(HIDDEN_CHUNKS):
        gathers[c].finish()
        own[c].wait()
    scatter.finish()
    for h in range(heads):
        probs_copy(h).wait()


def attend(normed, wq, wk, wv, w_rows, bias, cosine, sine, gain_q, gain_k, tokens, gain):
    seq_count, group_count = lax.axis_size("seq"), lax.axis_size("expert")
    toks, width = tokens.shape
    length, cols = normed.shape[0], wq.shape[1]
    heads = cols // cosine.shape[1]
    dma = pltpu.SemaphoreType.DMA
    low = lambda *shape: pltpu.VMEM(shape, BF)
    full = lambda *shape: pltpu.VMEM(shape, F32)
    out = jax.ShapeDtypeStruct
    flat = [out((length, cols), BF)] * 4
    return call(
        attend_kernel, 2, 80,
        (out((toks, width), F32), out((group_count, toks, width), BF), *flat,
         out((heads, length, length), F32), out((length, cols), F32), out((length, cols), F32),
         out((length, 128), F32)),
        place_scratch("seq", seq_count, toks, width, HIDDEN_CHUNKS)
        + [low(toks, width), low(length, width), low(width, cols), low(width, cols), low(width, cols),
           low(cols, width), full(heads, length, length), full(8, length), full(seq_count, 8, length),
           dma((5,)), dma((HIDDEN_CHUNKS,)), dma((HIDDEN_CHUNKS, group_count // 2, 2)),
           dma((HIDDEN_CHUNKS, group_count // 2, 2)), dma((2, seq_count)), dma((heads,))],
        normed, wq, wk, wv, w_rows, bias, cosine, sine, gain_q, gain_k, tokens, gain,
        specs=[ANY] * 5 + [IN_VMEM] * 7,
        out_specs=(IN_VMEM, ANY) + (IN_VMEM,) * 4 + (ANY,) + (IN_VMEM,) * 3,
    )


ROW_CHUNKS = 2


def rows_kernel(parts, out, *scratch):
    group = Ring("expert")
    greet(group.partners())
    scatter = Scatter(group, parts, ROW_CHUNKS, *scratch)
    scatter.start()
    for t in scatter.order:
        for c in range(ROW_CHUNKS):
            total = scatter.step(t, c)
            if not t:
                out[scatter.cut(c)] = total
    scatter.finish()


def sum_rows(parts):
    rows, width = parts.shape[1:]
    return call(
        rows_kernel, 3, 50, jax.ShapeDtypeStruct((rows, width), F32),
        scatter_scratch("expert", rows, width, ROW_CHUNKS), parts, out_specs=IN_VMEM,
    )


def dot(left, right, left_dim=1, right_dim=0):
    return lax.dot_general(
        left, right, (((left_dim,), (right_dim,)), ((), ())), preferred_element_type=F32
    )


GRAD_CHUNKS = 2
TILE = 256


def expert_kernel(
    n2, cot, hits, router, wg, wu, wd, hidden, cot_mine, gain,
    grad_out, low_out, small_out, out_parts, d_gate, d_up, d_down,
    stage, parts, routed, cot_rows, wg_v, wu_v, wd_v, scaled, ggate, gup, gate_sums, gates, one_hots,
    land, ringbuf, in_sems, w_sems, part_sems, wide_sems, out_sems, last_sem,
    gate_send, gate_keep, gate_land, gate_out, gate_in, gate_sems,
):
    seq, group = Ring("seq"), Ring("expert")
    groups, toks, width = n2.shape
    experts, rows, _ = routed.shape
    slots = rows // groups
    ff = wg_v.shape[1]
    n_total = experts * groups
    order = group_order(group)
    pairs = len(order)
    wide_at = pl.ds(0, width)

    def two(k):
        return pl.ds(group.at(order[k]) * 2, 2)

    def stage_copy(k):
        return pltpu.make_async_copy(n2.at[two(k)], stage.at[pl.ds(2 * k, 2)], in_sems.at[0, k])

    def cot_copy(k):
        return pltpu.make_async_copy(cot.at[two(k)], parts.at[two(k), :, wide_at], in_sems.at[1, k])

    def weight_copy(i, j):
        src, dst = ((wg, wg_v), (wu, wu_v), (wd, wd_v))[i]
        return pltpu.make_async_copy(src.at[j], dst, w_sems.at[i])

    def each(count, body):
        lax.fori_loop(0, count, lambda i, _: (body(i), 0)[1], 0)

    for k in range(pairs):
        stage_copy(k).start()
    for i in range(3):
        weight_copy(i, 0).start()
    for k in range(pairs):
        cot_copy(k).start()
    greet(seq.partners() + group.partners())

    lanes = lax.broadcasted_iota(jnp.int32, (toks, 128), 1)
    first_half = lanes < slots
    slot_of = jnp.where(first_half, lanes, lanes - slots).astype(F32)
    earlier = jnp.where(
        lax.broadcasted_iota(jnp.int32, (toks, toks), 0)
        > lax.broadcasted_iota(jnp.int32, (toks, toks), 1), 1.0, 0.0
    ).astype(BF)

    def softmax(logits):
        known = lax.broadcasted_iota(jnp.int32, logits.shape, 1) < n_total
        logits = jnp.where(known, logits, masked_score)
        weights = jnp.exp(logits - jnp.max(logits, axis=-1, keepdims=True))
        return weights / jnp.sum(weights, axis=-1, keepdims=True)

    def of_mine(values):
        first, second = [
            jnp.sum(jnp.where(lanes == group.me * experts + j, values, 0.0), axis=1, keepdims=True)
            for j in range(experts)
        ]
        return jnp.where(first_half, first, second)

    one_hots[...] = jnp.zeros_like(one_hots)
    for k in range(pairs):
        stage_copy(k).wait()
        for b in range(2):
            p = 2 * k + b
            hit = hits[group.at(order[k]) * 2 + b]
            rank = of_mine(dot(earlier, hit))
            chosen = (of_mine(hit.astype(F32)) > 0.0) & (rank == slot_of)
            one_hot = jnp.where(chosen, 1.0, 0.0)
            gate = of_mine(softmax(dot(stage[p], router[...])))
            row = jnp.sum(one_hot * gate, axis=0, keepdims=True)
            column = jnp.broadcast_to(row, (128, 128)).T
            for j in range(experts):
                gates[j, p * slots : (p + 1) * slots] = column[j * slots : (j + 1) * slots]
            one_hots[k, b * toks : (b + 1) * toks, b * 128 : (b + 1) * 128] = one_hot.astype(BF)

    def pick(k, values, dst):
        got = dot(one_hots[k], values.reshape(2 * toks, width), 0, 0).astype(BF)
        for b in range(2):
            at = slice((2 * k + b) * slots, (2 * k + b + 1) * slots)
            for j in range(experts):
                start = b * 128 + j * slots
                dst[j, at] = got[start : start + slots]

    for k in range(pairs):
        pick(k, stage[2 * k : 2 * k + 2], routed)
    for k in range(pairs):
        cot_copy(k).wait()
        pick(k, parts[two(k), :, wide_at], cot_rows)

    def hidden_tiles(j, start, count):
        span = slice(start, start + count)

        def tile(f):
            at = pl.ds(pl.multiple_of(f * TILE, TILE), TILE)
            gate_pre = dot(routed[j, span], wg_v[:, at])
            up_pre = dot(routed[j, span], wu_v[:, at])
            unit = dot(cot_rows[j, span], wd_v[at, :], 1, 1)
            gate = gates[j, span][:, :1]
            sig = 1.0 / (1.0 + jnp.exp(-gate_pre))
            silu = gate_pre * sig
            active = silu * up_pre
            low = active.astype(BF).astype(F32)
            gate_sums[j, span] += jnp.sum(unit * low, axis=-1, keepdims=True)
            scaled[j, span, at] = (low * gate).astype(BF)
            grad_active = unit * gate
            ggate[j, span, at] = (
                grad_active * up_pre * sig * (1.0 + gate_pre * (1.0 - sig))
            ).astype(BF)
            gup[j, span, at] = (grad_active * silu).astype(BF)

        each(ff // TILE, tile)

    def row_tiles(j, start, count):
        span = slice(start, start + count)
        blocks = slice(start // slots, (start + count) // slots)

        def tile(d):
            at = pl.ds(pl.multiple_of(d * TILE, TILE), TILE)
            grad = dot(ggate[j, span], wg_v[at, :], 1, 1) + dot(gup[j, span], wu_v[at, :], 1, 1)
            stage[blocks, j * slots : (j + 1) * slots, at] = grad.astype(BF).reshape(
                count // slots, slots, TILE
            )

        each(width // TILE, tile)

    scatter = PlaceScatter(group, parts, GRAD_CHUNKS, land, ringbuf, part_sems)
    row_lanes = lanes[:slots]

    def place(k):
        value = dot(one_hots[k], stage[2 * k : 2 * k + 2].reshape(2 * toks, width))
        parts[two(k), :, wide_at] = value.astype(BF).reshape(2, toks, width)
        sums = []
        for p in (2 * k, 2 * k + 1):
            for j in range(experts):
                value = gate_sums[j, p * slots : (p + 1) * slots]
                first = value.astype(BF).astype(F32)
                mine = group.me * experts + j
                sums.append(jnp.where(row_lanes == mine, first,
                                      jnp.where(row_lanes == mine + n_total, value - first, 0.0)))
        value = dot(one_hots[k], jnp.concatenate(sums, axis=0).astype(BF))
        parts[two(k), :, pl.ds(width, 128)] = value.astype(BF).reshape(2, toks, 128)
        scatter.start_place(order[k])

    side, short = width // seq.size, ff // seq.size

    def wide_grad(right, s, j):
        at = pl.ds(pl.multiple_of(s * side, side), side)
        return dot(routed[j, :, at], right[j], 0, 0).astype(BF)

    def rows_of(j):
        return pl.ds(j * side, side)

    def gate_pair(t, j):
        return remote(gate_send, gate_land.at[t, rows_of(j)], gate_sems.at[0, t, j],
                      gate_sems.at[1, t, j], seq.pair)

    def gate_cross(j):
        return remote(gate_out.at[rows_of(j)], gate_in.at[rows_of(j)], gate_sems.at[2, 0, j],
                      gate_sems.at[3, 0, j], seq.next)

    def gate_part(j):
        for t in (1, 0):
            if t == 0:
                gate_pair(1, j).wait_send()
            elif j:
                gate_pair(0, j - 1).wait_send()
            gate_send[...] = wide_grad(ggate, seq.at(t) * 2 + 1 - seq.inner, j)
            gate_pair(t, j).start()
            mine = wide_grad(ggate, seq.at(t) * 2 + seq.inner, j)
            if t:
                gate_pair(t, j).wait_recv()
                total = mine.astype(F32) + gate_land[t, rows_of(j)].astype(F32)
                gate_out[rows_of(j)] = total.astype(BF)
                gate_cross(j).start()
            else:
                gate_keep[rows_of(j)] = mine

    gate_sums[...] = jnp.zeros_like(gate_sums)
    half = rows // 2
    for j in range(experts):
        for i in range(3):
            weight_copy(i, j).wait()
        if j + 1 < experts:
            hidden_tiles(j, 0, rows)
            weight_copy(2, j + 1).start()
            row_tiles(j, 0, rows)
            weight_copy(0, j + 1).start()
            weight_copy(1, j + 1).start()
            gate_part(j)
        else:
            hidden_tiles(j, 0, half)
            row_tiles(j, 0, half)
            for k in range(pairs // 2):
                place(k)
            hidden_tiles(j, half, half)
            weight_copy(2, 0).start()
            row_tiles(j, half, half)
            for k in range(pairs // 2, pairs):
                place(k)

    def grad_step(t):
        for c in range(GRAD_CHUNKS):
            total = scatter.step(t, c)
            if not t:
                finish_rows(c, total)

    def finish_rows(c, total):
        cut = scatter.cut(c)
        value = hidden[cut]
        inv = lax.rsqrt(jnp.mean(value * value, axis=-1, keepdims=True) + norm_eps)
        unit = value * inv
        normed2 = (unit * gain[...]).astype(BF)
        probs = softmax(dot(normed2, router[...]))
        both = total[:, width:]
        grad_probs = jnp.where(
            lax.broadcasted_iota(jnp.int32, both.shape, 1) < n_total,
            both + pltpu.roll(both, 128 - n_total, 1), 0.0,
        )
        grad_logits = probs * (grad_probs - jnp.sum(probs * grad_probs, axis=-1, keepdims=True))
        grad_logits = grad_logits.astype(BF)
        grad = total[:, :width] + dot(grad_logits, router[...], 1, 1)
        gained = grad * gain[...]
        mean = jnp.mean(gained * unit, axis=-1, keepdims=True)
        result = cot_mine[cut].astype(F32) + inv * (gained - unit * mean)
        grad_out[cut] = result
        low_out[cut] = result.astype(BF)
        count = small_out.shape[0]
        sums = dot(grad_logits, normed2, 0, 0)[:count]
        line = lax.broadcasted_iota(jnp.int32, sums.shape, 0)
        sums = jnp.where(line == n_total, jnp.sum(grad * unit, axis=0, keepdims=True), sums)
        small_out[...] = sums if c == 0 else small_out[...] + sums

    def send_wide(right, out, s):
        copies = [
            pltpu.make_async_copy(
                wg_v.at[pl.ds(j * side, side)], out.at[s, pl.ds(j * side, side)], wide_sems.at[j]
            )
            for j in range(experts)
        ]
        for j in range(experts):
            wg_v[pl.ds(j * side, side)] = wide_grad(right, s, j)
            copies[j].start()
        for copy in copies:
            copy.wait()

    def send_tall(s):
        at = pl.ds(pl.multiple_of(s * short, short), short)
        per = short // toks
        copies = []
        for j in range(experts):
            value = dot(scaled[j, :, at], cot_rows[j], 0, 0).astype(BF)
            for i in range(per):
                place_at = j * per + i
                stage[place_at] = value[i * toks : (i + 1) * toks]
                copies.append(pltpu.make_async_copy(
                    stage.at[place_at], d_down.at[s, pl.ds(place_at * toks, toks)],
                    out_sems.at[place_at]))
                copies[-1].start()
        for copy in copies:
            copy.wait()

    for j in range(1, experts):
        gate_part(j)
    grad_step(scatter.order[0])
    if len(scatter.order) > 2:
        grad_step(scatter.order[1])
    each(seq.size, lambda s: send_wide(gup, d_up, s))
    for t in scatter.order[2:-1]:
        grad_step(t)
    each(seq.size, send_tall)

    for j in range(experts):
        weight_copy(2, j).wait()

        def out_tile(d, j=j):
            at = pl.ds(pl.multiple_of(d * TILE, TILE), TILE)
            value = dot(scaled[j], wd_v[:, at])
            stage[:, j * slots : (j + 1) * slots, at] = value.astype(BF).reshape(groups, slots, TILE)

        each(width // TILE, out_tile)
        if j + 1 < experts:
            weight_copy(2, j + 1).start()

    def out_copy(k):
        return pltpu.make_async_copy(stage.at[pl.ds(2 * k, 2)], out_parts.at[two(k)], out_sems.at[k])

    for k in range(pairs):
        value = dot(one_hots[k], stage[2 * k : 2 * k + 2].reshape(2 * toks, width))
        stage[2 * k : 2 * k + 2] = value.astype(BF).reshape(2, toks, width)
        out_copy(k).start()
    grad_step(0)
    for j in range(experts):
        gate_pair(0, j).wait_recv()
        gate_cross(j).wait_recv()
        at = rows_of(j)
        total = gate_keep[at].astype(F32) + gate_land[0, at].astype(F32) + gate_in[at].astype(F32)
        gate_keep[at] = total.astype(BF)
    gate_copy = pltpu.make_async_copy(gate_keep, d_gate, last_sem.at[0])
    gate_copy.start()
    for k in range(pairs):
        out_copy(k).wait()
    gate_copy.wait()
    scatter.finish()
    gate_pair(0, experts - 1).wait_send()
    for j in range(experts):
        gate_cross(j).wait_send()


def run_experts(n2, cot, hits, router, wg, wu, wd, hidden, cot_mine, gain):
    seq_count, group_count = lax.axis_size("seq"), lax.axis_size("expert")
    experts, width, ff = wg.shape
    toks = n2.shape[1]
    rows = group_count * MOST
    outer_count = group_count // 2
    columns = width + 128
    small_rows = -(-(experts * group_count + 1) // 8) * 8
    dma = pltpu.SemaphoreType.DMA
    side, short = width // seq_count, ff // seq_count

    low = lambda *shape: pltpu.VMEM(shape, BF)
    out = jax.ShapeDtypeStruct
    return call(
        expert_kernel, 6, 100,
        (out((toks, width), F32), out((toks, width), BF), out((small_rows, width), F32),
         out((group_count, toks, width), BF),
         out((experts * side, ff), BF),
         out((seq_count, experts * side, ff), BF), out((seq_count, experts * short, width), BF)),
        [low(group_count, toks, width), low(group_count, toks, columns),
         low(experts, rows, width), low(experts, rows, width),
         low(width, ff), low(width, ff), low(ff, width),
         low(experts, rows, ff), low(experts, rows, ff), low(experts, rows, ff),
         pltpu.VMEM((experts, rows, 128), F32), pltpu.VMEM((experts, rows, 128), F32),
         low(outer_count, 2 * toks, 256),
         low(outer_count, toks, columns), low(outer_count - 1, toks, columns),
         dma((2, outer_count)), dma((3,)), dma((4, outer_count, GRAD_CHUNKS)), dma((experts,)),
         dma((group_count,)), dma((1,)),
         low(side, ff), low(experts * side, ff), low(2, experts * side, ff),
         low(experts * side, ff), low(experts * side, ff), dma((4, 2, experts))],
        n2, cot, hits, router, wg, wu, wd, hidden, cot_mine, gain,
        specs=[ANY, ANY, IN_VMEM, IN_VMEM, ANY, ANY, ANY, IN_VMEM, IN_VMEM, IN_VMEM],
        out_specs=(IN_VMEM, IN_VMEM, IN_VMEM, ANY, ANY, ANY, ANY),
    )


NORMED_CHUNKS = 2
CROSS_CHUNKS = 8


class AllSum:
    def __init__(self, steps, sums, land, sems):
        self.steps, self.sums, self.land, self.sems = steps, sums, land, sems
        self.at = 0

    def copy(self, i):
        return remote(self.sums.at[i], self.land.at[i], self.sems.at[0, i], self.sems.at[1, i], self.steps[i])

    def start(self):
        self.copy(0).start()

    def hop(self):
        i = self.at
        if i == len(self.steps):
            return
        self.at += 1
        self.copy(i).wait_recv()
        self.sums[i + 1] = self.sums[i] + self.land[i]
        if self.at < len(self.steps):
            self.copy(self.at).start()

    def result(self):
        while self.at < len(self.steps):
            self.hop()
        for i in range(len(self.steps)):
            self.copy(i).wait_send()
        return self.sums[len(self.steps)]


class Cross:
    def __init__(self, seq, parts, land, crossed, bufs, stage, sems):
        self.seq, self.parts, self.land, self.crossed = seq, parts, land, crossed
        self.bufs, self.stage, self.sems = bufs, stage, sems
        self.rows = parts.shape[1] // CROSS_CHUNKS

    def swap(self, t):
        src = self.parts.at[self.seq.at(t) * 2 + 1 - self.seq.inner]
        return remote(src, self.land.at[t], self.sems.at[0, t], self.sems.at[1, t], self.seq.pair)

    def loads(self, i):
        cut = pl.ds(i * self.rows, self.rows)
        own = self.parts.at[self.seq.at(1) * 2 + self.seq.inner, cut]
        return [
            pltpu.make_async_copy(own, self.bufs.at[i % 2, 0], self.sems.at[2, i % 2]),
            pltpu.make_async_copy(self.land.at[1, cut], self.bufs.at[i % 2, 1], self.sems.at[3, i % 2]),
        ]

    def load(self, i):
        if i == 0:
            self.swap(1).wait_recv()
        if i < CROSS_CHUNKS:
            for copy in self.loads(i):
                copy.start()

    def send(self, i):
        cut = pl.ds(i * self.rows, self.rows)
        return remote(self.stage.at[i % 2], self.crossed.at[cut], self.sems.at[4, i % 2],
                      self.sems.at[5, i], self.seq.next)

    def tick(self, i):
        if i == 0:
            self.load(0)
        for copy in self.loads(i):
            copy.wait()
        self.load(i + 1)
        if i >= 2:
            self.send(i - 2).wait_send()
        total = self.bufs[i % 2, 0].astype(F32) + self.bufs[i % 2, 1].astype(F32)
        self.stage[i % 2] = total.astype(BF)
        self.send(i).start()

    def finish(self):
        self.send(CROSS_CHUNKS - 2).wait_send()
        self.send(CROSS_CHUNKS - 1).wait_send()
        for c in range(CROSS_CHUNKS):
            self.send(c).wait_recv()
        self.swap(0).wait_recv()
        self.swap(0).wait_send()
        self.swap(1).wait_send()


def cross_scratch(parts):
    rows, columns = parts.shape[1] // CROSS_CHUNKS, parts.shape[2]
    return [pltpu.VMEM((2, 2, rows, columns), BF), pltpu.VMEM((2, rows, columns), BF),
            pltpu.SemaphoreType.DMA((6, CROSS_CHUNKS))]


def place_scratch(axis, size, rows, columns, chunks):
    outer_count = lax.axis_size(axis) // 2
    return [pltpu.VMEM((size, rows, columns), BF), pltpu.VMEM((outer_count, rows, columns), BF),
            pltpu.VMEM((max(outer_count - 1, 1), rows, columns), BF),
            pltpu.SemaphoreType.DMA((4, outer_count, chunks))]


Q_BLOCK = 256
LATE = ("w_rows", "normed", "probs", "q_unit", "k_unit", "wq", "wk", "wv")
LATE_AT = (4, 17, 9, 10, 11, 18, 19, 20)


def last_kernel(
    grad_low, grad_hidden, tokens, gain, w_rows, q_low, k_low, v_low, attended, probs,
    q_unit, k_unit, scales, gain_q, gain_k, cosine, sine, normed, wq, wk, wv, small, *refs,
    crossings,
):
    expert_parts, refs = refs[:crossings], refs[crossings:]
    late = {}
    refs, copies, load_sems = refs[: -len(LATE) - 1], refs[-len(LATE) - 1 : -1], refs[-1]
    arrays = dict(w_rows=w_rows, probs=probs, q_unit=q_unit, k_unit=k_unit, normed=normed,
                  wq=wq, wk=wk, wv=wv)
    for i, name in enumerate(LATE):
        late[name] = pltpu.make_async_copy(arrays[name], copies[i], load_sems.at[i])
    w_rows, normed, probs, q_unit, k_unit, wq, wk, wv = copies
    d_tokens, d_q, d_k, d_v, d_out, small_out = refs[:6]
    refs = refs[6:]
    cross_out, refs = refs[: 2 * crossings], refs[2 * crossings :]
    cross_bufs, refs = refs[: 3 * crossings], refs[3 * crossings :]
    place = [refs[4 * i : 4 * i + 4] for i in range(5)]
    (grad_all, normed_t, grad_att, grad_g, grad_three, dk_sum, row_send, row_land,
     low_send, low_land, early_buf, early_land, late_buf, late_land,
     own_sem, pack_send, pack_recv, row_sems, swap_sems, early_sems, late_sems) = refs[20:]
    seq, group = Ring("seq"), Ring("expert")
    others = [{"seq": seq.me ^ d} for d in range(1, seq.size)]
    known = [{"expert": group.me ^ (1 << i)} for i in range((group.size - 1).bit_length())]
    across = [{"seq": seq.me ^ (1 << i)} for i in range((seq.size - 1).bit_length())]
    early_sums = AllSum(known[::-1] + across, early_buf, early_land, early_sems)
    late_sums = AllSum(across[:1] + known[::-1] + across[1:], late_buf, late_land, late_sems)
    early_rows = small.shape[0]
    for name in LATE:
        late[name].start()
    greet(others + known + [group.next, group.last])
    length, cols = q_low.shape
    width = tokens.shape[1]
    toks = tokens.shape[0]
    head_dim = cosine.shape[1]
    heads = cols // head_dim
    wrows = d_out.shape[0]
    scale = head_dim**-0.5

    crosses = [
        Cross(seq, expert_parts[i], *cross_out[2 * i : 2 * i + 2], *cross_bufs[3 * i : 3 * i + 3])
        for i in range(crossings)
    ]
    ticks = [(cross, i) for i in range(CROSS_CHUNKS) for cross in crosses]

    def tick(count=1):
        for _ in range(count):
            if ticks:
                cross, i = ticks.pop(0)
                cross.tick(i)

    own = pltpu.make_async_copy(grad_low, grad_all.at[seq.me], own_sem.at[0])
    own.start()
    pack = Gather(seq, lambda s: grad_all.at[s], pack_send, pack_recv)
    pack.start(grad_low)
    early_buf[0] = small[...]
    early_sums.start()
    late_buf[0] = jnp.zeros_like(late_buf[0])
    for t in (1, 0):
        for cross in crosses:
            cross.swap(t).start()
    size = width // seq.size
    late["normed"].wait()
    for s in range(seq.size):
        normed_t[pl.ds(s * size, size)] = normed[:, s * size : (s + 1) * size].T
        if s % 2:
            early_sums.hop()
    for back in range(1, seq.outer_count):
        pack.relay(back)
    tick(2)
    own.wait()
    pack.finish()

    late["w_rows"].wait()
    for c in range(0, cols, Q_BLOCK):
        at = slice(c, c + Q_BLOCK)
        grad_att[:, at] = dot(
            grad_all[...].reshape(length, width), w_rows[at, :], 1, 1
        ).astype(BF)

    query_sums, key_sums, value_sums = [
        PlaceScatter(group, p[0], 1, p[1], p[2], p[3]) for p in place[:3]
    ]
    out_sums = RingFirst(group, *place[3])
    normed_sums = PlaceScatter(seq, place[4][0], NORMED_CHUNKS, *place[4][1:])

    def head(h):
        return slice(h * head_dim, (h + 1) * head_dim)

    early_sums.hop()
    late["probs"].wait()
    for h in range(heads):
        grad_three[2, :, head(h)] = dot(
            probs[h].astype(BF), grad_att[:, head(h)], 0, 0
        ).astype(BF)

    def weight_grad(i, sums):
        for s in range(seq.size):
            value = dot(normed_t[pl.ds(s * size, size)], grad_three[i])
            sums.x_ref[:, pl.ds(s * wrows, wrows)] = value.astype(BF).reshape(
                group.size, wrows, cols
            )
        sums.start()

    tick()
    weight_grad(2, value_sums)
    early_sums.hop()
    for c in range(0, width, 512):
        at = slice(c, c + 512)
        value = dot(attended[...], grad_all[:, :, at].reshape(length, 512), 0, 0)
        out_sums.parts[:, :, at] = value.astype(BF).reshape(group.size, wrows, 512)
    out_sums.start()
    tick()
    out_order, value_order = list(out_sums.order[1:]), list(value_sums.order)

    def out_step():
        if len(out_order) > 1:
            out_sums.step(out_order.pop(0))

    def value_step():
        if len(value_order) > 1:
            value_sums.step(value_order.pop(0), 0)

    row_sums = [jnp.zeros((length, 1), F32), jnp.zeros((length, 1), F32)]
    gain_row = 0
    cos_rows, sin_rows = cosine[...], sine[...]

    def through_rope(i, h, grad, unit, gains):
        turned = turn(grad, cos_rows, sin_rows)
        late_buf[0, pl.ds(i, 1), pl.ds(pl.multiple_of(seq.me * cols, 128) + h * head_dim, head_dim)] = (
            jnp.sum(turned * unit, axis=0, keepdims=True)
        )
        gained = turned * gains
        grad_g[i, :, head(h)] = gained
        row_sums[i] = row_sums[i] + jnp.sum(gained * unit, axis=1, keepdims=True)

    late["q_unit"].wait()
    late["k_unit"].wait()
    early_sums.hop()
    for h in range(heads):
        queries = []
        for b in range(0, length, Q_BLOCK):
            rows = slice(b, b + Q_BLOCK)
            prob = probs[h, rows]
            grad = dot(grad_att[rows, head(h)], v_low[:, head(h)], 1, 1)
            row_dot = jnp.sum(prob * grad, axis=-1, keepdims=True)
            grad_scores = (prob * (grad - row_dot)).astype(BF)
            queries.append(dot(grad_scores, k_low[:, head(h)]) * scale)
            keys = dot(grad_scores, q_low[rows, head(h)], 0, 0)
            dk_sum[...] = keys if b == 0 else dk_sum[...] + keys
        at = pl.ds(pl.multiple_of(seq.me * cols + h * head_dim, head_dim), head_dim)
        through_rope(0, h, jnp.concatenate(queries, axis=0), q_unit[:, head(h)], gain_q[:, at])
        through_rope(1, h, dk_sum[...] * scale, k_unit[:, head(h)], gain_k[:, at])
        if h == 1:
            value_step()

    lanes = lax.broadcasted_iota(jnp.int32, (length, 128), 1)
    table = jnp.where(lanes == 0, row_sums[0], jnp.where(lanes == 1, row_sums[1], 0.0))
    row_send[...] = table.T[:8]

    def row_copy(d):
        return remote(row_send, row_land.at[d], row_sems.at[0, d], row_sems.at[1, d], others[d - 1])

    for d in range(1, seq.size):
        row_copy(d).start()
    out_step()
    total = row_send[...]
    for d in range(1, seq.size):
        row_copy(d).wait_recv()
        total = total + row_land[d]
    for d in range(1, seq.size):
        row_copy(d).wait_send()
    tick(3)
    means = jnp.concatenate([total / width, jnp.zeros((120, length), F32)], axis=0).T
    for i, (unit, sums) in enumerate(((q_unit, query_sums), (k_unit, key_sums))):
        for h in range(heads):
            value = grad_g[i, :, head(h)] - unit[:, head(h)] * means[:, i : i + 1]
            grad_three[i, :, head(h)] = (value * scales[:, i : i + 1]).astype(BF)
        weight_grad(i, sums)
        value_step()
    for name in ("wq", "wk", "wv"):
        late[name].wait()
    for c in range(0, width, 512):
        at = slice(c, c + 512)
        value = dot(grad_three[0], wq[at, :], 1, 1) + dot(grad_three[1], wk[at, :], 1, 1)
        value = value + dot(grad_three[2], wv[at, :], 1, 1)
        normed_sums.x_ref[:, :, at] = value.astype(BF).reshape(seq.size, toks, 512)
    normed_sums.start()
    out_step()
    tick(2)

    swaps = {}

    def swap_copy(i, d):
        src = low_send.at[i, pl.ds((seq.me ^ d) * wrows, wrows)]
        return remote(src, low_land.at[i, seq.me], swap_sems.at[0, i, d], swap_sems.at[1, i, d], others[d - 1])

    def send_columns(i, sums):
        low_send[i] = sums.step(0, 0).astype(BF)
        for d in range(1, seq.size):
            swap_copy(i, d).start()

    while len(value_order) > 1:
        value_step()
    for t in normed_sums.order[:-1]:
        for c in range(NORMED_CHUNKS):
            normed_sums.step(t, c)
    first, *middle = group_order(group)[:-1]
    query_sums.step(first, 0)
    tick()
    key_sums.step(first, 0)
    tick()
    while len(out_order) > 1:
        out_step()
    gain_sum = jnp.zeros((1, width), F32)
    for c in range(NORMED_CHUNKS):
        cut = normed_sums.cut(c)
        grad = normed_sums.step(0, c)
        value = tokens[cut].astype(F32)
        inv = lax.rsqrt(jnp.mean(value * value, axis=-1, keepdims=True) + norm_eps)
        unit = value * inv
        gained = grad * gain[...]
        mean = jnp.mean(gained * unit, axis=-1, keepdims=True)
        d_tokens[cut] = grad_hidden[cut] + inv * (gained - unit * mean)
        gain_sum = gain_sum + jnp.sum(grad * unit, axis=0, keepdims=True)
    late_buf[0, pl.ds(2, 1)] = gain_sum

    late_sums.start()
    tick()
    send_columns(2, value_sums)
    out_sums.step(0)
    for t in middle:
        query_sums.step(t, 0)
        tick(2)
        key_sums.step(t, 0)
        tick(2)
        late_sums.hop()
    d_out[...] = out_sums.last()
    tick()
    send_columns(0, query_sums)
    late_sums.hop()
    send_columns(1, key_sums)
    late_sums.hop()

    tick(len(ticks))
    for i, out in ((2, d_v), (0, d_q), (1, d_k)):
        for d in range(1, seq.size):
            there = low_land.at[i, seq.me ^ d]
            remote(there, there, swap_sems.at[0, i, d], swap_sems.at[1, i, d], others[d - 1]).wait_recv()
            swap_copy(i, d).wait_send()
        low_land[i, seq.me] = low_send[i, pl.ds(pl.multiple_of(seq.me * wrows, wrows), wrows)]
        for s in range(seq.size):
            out[:, s * cols : (s + 1) * cols] = low_land[i, s].astype(F32)
    small_out[pl.ds(0, early_rows)] = early_sums.result()
    small_out[pl.ds(early_rows, 8)] = late_sums.result()
    for cross in crosses:
        cross.finish()
    for sums in (query_sums, key_sums, value_sums, out_sums, normed_sums):
        sums.finish()


def group_order(ring):
    return list(range(1, ring.outer_count)) + [0]


def finish_all(ins, expert_parts):
    seq_count, group_count = lax.axis_size("seq"), lax.axis_size("expert")
    (grad_low, grad_hidden, tokens, gain, w_rows, q_low, *_) = ins
    small = ins[-1]
    rows, width = tokens.shape
    length, cols = q_low.shape
    head_dim = width // HEADS
    wrows = cols // group_count
    side = seq_count * wrows
    count = (seq_count - 1).bit_length() + (group_count - 1).bit_length()
    dma = pltpu.SemaphoreType.DMA
    low = lambda *shape: pltpu.VMEM(shape, BF)
    full = lambda *shape: pltpu.VMEM(shape, F32)
    shape = lambda *dims: jax.ShapeDtypeStruct(dims, F32)
    outs = [shape(rows, width)] + [shape(wrows, width)] * 4 + [shape(small.shape[0] + 8, width)]
    cross_outs, scratch = [], []
    for parts in expert_parts:
        size = parts.shape[1:]
        cross_outs += [jax.ShapeDtypeStruct((2,) + size, BF), jax.ShapeDtypeStruct(size, BF)]
        scratch += cross_scratch(parts)
    for _ in range(3):
        scratch += place_scratch("expert", group_count, side, cols, 1)
    scratch += ring_first_scratch("expert", wrows, width)
    scratch += place_scratch("seq", seq_count, rows, width, NORMED_CHUNKS)
    scratch += [
        low(seq_count, rows, width), low(width, length), low(length, cols),
        full(2, length, cols), low(3, length, cols), full(length, head_dim),
        full(8, length), full(seq_count, 8, length),
        low(3, side, cols), low(3, seq_count, wrows, cols),
        full(count + 1, *small.shape), full(count, *small.shape),
        full(count + 1, 8, width), full(count, 8, width),
        dma((1,)), dma((seq_count // 2, 2)), dma((seq_count // 2, 2)), dma((2, seq_count)),
        dma((2, 3, seq_count)), dma((2, count)), dma((2, count)),
    ]
    scratch += [pltpu.VMEM(ins[i].shape, ins[i].dtype) for i in LATE_AT] + [dma((len(LATE),))]
    return call(
        partial(last_kernel, crossings=len(expert_parts)), 5, 150,
        tuple(outs + cross_outs), scratch, *ins, *expert_parts,
        specs=[ANY if i in (0, *LATE_AT) else IN_VMEM for i in range(len(ins))]
        + [ANY] * len(expert_parts),
        out_specs=tuple([IN_VMEM] * len(outs) + [ANY] * len(cross_outs)),
    )


ADD_STEPS = 8


def add_kernel(
    place, gate, up, up_land, up_in, down, down_land, down_in, hidden, out_sum, *refs
):
    copies, refs = refs[:5], refs[5:]
    d_gate, d_up, d_down, mixed = refs[:4]
    d_gate[...] = gate[...].astype(F32)
    d_up[...] = up[0].astype(F32) + up_land[0].astype(F32) + up_in[...].astype(F32)
    d_down[...] = down[0].astype(F32) + down_land[0].astype(F32) + down_in[...].astype(F32)
    mixed[...] = (hidden[...] + out_sum[...].astype(F32)).astype(BF)
    for src, dst in zip(copies, refs[4:]):
        dst[...] = src[...]


def add_up(place, gate, up, up_land, up_in, down, down_land, down_in, hidden, out_sum, *copies):
    def flat(array):
        rows, columns = array.shape
        return pl.BlockSpec((rows // ADD_STEPS, columns), lambda i, s: (i, 0))

    def first(array):
        _, rows, columns = array.shape
        return pl.BlockSpec((1, rows // ADD_STEPS, columns), lambda i, s: (0, i, 0))

    def own(array):
        _, rows, columns = array.shape
        return pl.BlockSpec((1, rows // ADD_STEPS, columns), lambda i, s: (s[0], i, 0))

    outs = [jax.ShapeDtypeStruct(a.shape, F32) for a in (gate, up_in, down_in)]
    outs += [jax.ShapeDtypeStruct(hidden.shape, BF)]
    outs += [jax.ShapeDtypeStruct(c.shape, c.dtype) for c in copies]
    return pl.pallas_call(
        add_kernel,
        out_shape=outs,
        grid_spec=pltpu.PrefetchScalarGridSpec(
            num_scalar_prefetch=1,
            grid=(ADD_STEPS,),
            in_specs=[flat(gate), own(up), first(up_land), flat(up_in),
                      own(down), first(down_land), flat(down_in), flat(hidden), flat(out_sum)]
            + [flat(c) for c in copies],
            out_specs=[flat(o) for o in outs],
        ),
    )(place, gate, up, up_land, up_in, down, down_land, down_in, hidden, out_sum, *copies)


def each(left, right, how):
    return jnp.einsum(how, left, right, preferred_element_type=F32)


def plain_experts(normed2_all, cot_all, chosen, gate_rows, w_gate, w_up, w_down):
    seq_count, group_count = lax.axis_size("seq"), lax.axis_size("expert")
    experts_local, tok_rows = w_gate.shape[0], chosen.shape[-1]
    total_experts = experts_local * group_count
    chosen_low = chosen.astype(BF)

    def pick_rows(values):
        return jnp.einsum("ejmt,etd->jemd", chosen_low, values, preferred_element_type=F32).astype(BF)

    def place_rows(values):
        return jnp.einsum("ejmt,jemd->etd", chosen_low, values, preferred_element_type=F32).astype(BF)

    routed = pick_rows(normed2_all)
    cot_rows = pick_rows(cot_all)

    gate_pre = each(routed, w_gate, "jemd,jdf->jemf")
    up_pre = each(routed, w_up, "jemd,jdf->jemf")
    sigmoid_gate = jax.nn.sigmoid(gate_pre)
    silu_gate = gate_pre * sigmoid_gate
    active = silu_gate * up_pre
    active_low = active.astype(BF)
    grad_unit = each(cot_rows, w_down, "jemd,jfd->jemf")
    grad_gate_rows = jnp.sum(grad_unit * active_low.astype(F32), axis=-1)
    grad_active = grad_unit * gate_rows
    grad_gate_low = (
        grad_active * up_pre * sigmoid_gate * (1.0 + gate_pre * (1.0 - sigmoid_gate))
    ).astype(BF)
    grad_up_low = (grad_active * silu_gate).astype(BF)
    grad_routed = each(grad_gate_low, w_gate, "jemf,jdf->jemd")
    grad_routed = (grad_routed + each(grad_up_low, w_up, "jemf,jdf->jemd")).astype(BF)
    grad_parts = place_rows(grad_routed)
    grad_normed2 = sum_rows(grad_parts)
    grad_probs_parts = jnp.einsum(
        "ejmt,jem->etj", chosen.astype(F32), grad_gate_rows, precision=lax.Precision.HIGHEST
    )
    grad_probs = lax.all_to_all(grad_probs_parts, "expert", split_axis=0, concat_axis=0, tiled=True)
    grad_probs = grad_probs.transpose(1, 0, 2).reshape(tok_rows, total_experts)

    expert_out = each(active_low, w_down, "jemf,jfd->jemd") * gate_rows
    out_parts = place_rows(expert_out.astype(BF))

    active_scaled = (active_low.astype(F32) * gate_rows).astype(BF)

    def expert_grad(left, right):
        grad = jnp.einsum("jemd,jemf->jdf", left, right, preferred_element_type=F32).astype(BF)
        rows = grad.shape[1] // seq_count
        grad = grad.reshape(experts_local, seq_count, rows, grad.shape[2])
        return scatter_sum(
            [lax.dynamic_index_in_dim(grad, o, 1, keepdims=False) for o in owners("seq")], "seq"
        )

    d_w_gate = expert_grad(routed, grad_gate_low)
    d_w_up = expert_grad(routed, grad_up_low)
    d_w_down = expert_grad(active_scaled, cot_rows)
    return grad_normed2, grad_probs, out_parts, d_w_gate, d_w_up, d_w_down


def local(
    tokens,
    lengths,
    routes,
    gain_attn,
    w_query,
    w_key,
    w_value,
    gain_query,
    gain_key,
    w_out,
    gain_mlp,
    router,
    w_gate,
    w_up,
    w_down,
    cotangent,
):
    seq_count = lax.axis_size("seq")
    group_count = lax.axis_size("expert")
    seq_me = lax.axis_index("seq")
    group_me = lax.axis_index("expert")
    tok_rows, width = tokens.shape[1], tokens.shape[2]
    head_dim = width // HEADS
    heads = HEADS // seq_count
    cols = width // seq_count
    wrows = w_query.shape[0]
    length = tok_rows * seq_count
    experts_local = w_gate.shape[0]
    total_experts = experts_local * group_count
    slots = MOST
    score_scale = head_dim ** (-0.5)
    half = head_dim // 2
    inverse = 10000.0 ** (-jnp.arange(half, dtype=F32) / half)
    frequency = jnp.concatenate([inverse, inverse])[None]

    cot_all = lax.all_gather(cotangent[0], "expert", axis=0)
    w_rows = lax.all_gather(w_out, "expert", axis=0, tiled=True)
    wq_cols, wk_cols, wv_cols, normed_all, hits_all, cosine, sine, bias = gather_weights(
        w_query, w_key, w_value, tokens[0], gain_attn[None], routes[0], lengths, frequency
    )
    normed_all = normed_all.reshape(length, width)
    w_cols = [w.reshape(width, cols) for w in (wq_cols, wk_cols, wv_cols)]
    (hidden, normed2_all, query_low, key_low, value_low, attended_low, probs, query_unit, key_unit,
     scales) = attend(normed_all, *w_cols, w_rows, bias, cosine, sine, gain_query[None], gain_key[None],
                      tokens[0], gain_mlp[None])
    roomy = group_count * slots <= 512 and seq_count == 4
    if roomy:
        router_wide = jnp.concatenate(
            [router, jnp.zeros((width, 128 - total_experts), BF)], axis=1
        )
        grad_hidden, grad_low, small, out_parts, gate_sum, up_parts, down_parts = run_experts(
            normed2_all, cot_all, hits_all, router_wide, w_gate, w_up, w_down, hidden,
            cotangent[0], gain_mlp[None]
        )
        expert_parts = (up_parts, down_parts)
    else:
        normed2, mlp_norm_back = jax.vjp(rms_norm, hidden, gain_mlp)
        normed2_low = normed2.astype(BF)

        first_expert = group_me * experts_local
        hit = lax.dynamic_slice_in_dim(hits_all, first_expert, experts_local, axis=2)
        hit = hit.transpose(0, 2, 1)
        before = (jnp.arange(tok_rows)[:, None] < jnp.arange(tok_rows)[None, :]).astype(BF)
        rank = jnp.einsum("ejt,tu->eju", hit, before, preferred_element_type=F32)
        slot_ids = jnp.arange(slots, dtype=jnp.int32)
        chosen = (hit[:, :, None, :] > 0) & (rank.astype(jnp.int32)[:, :, None, :] == slot_ids[None, None, :, None])
        chosen_low = chosen.astype(BF)

        logits_all = jnp.einsum("etd,dn->etn", normed2_all, router, preferred_element_type=F32)
        probs_all = jax.nn.softmax(logits_all, axis=-1)
        mine = lax.dynamic_slice_in_dim(probs_all, first_expert, experts_local, axis=2)
        gate_rows = jnp.einsum(
            "ejmt,etj->jem", chosen.astype(F32), mine, precision=lax.Precision.HIGHEST
        )[..., None]

        grad_normed2, grad_probs, out_parts, d_w_gate, d_w_up, d_w_down = plain_experts(
            normed2_all, cot_all, chosen, gate_rows, w_gate, w_up, w_down
        )
        expert_parts = ()
        router_probs, softmax_back = jax.vjp(
            partial(jax.nn.softmax, axis=-1), product(normed2_low, router)
        )
        (grad_logits,) = softmax_back(grad_probs)
        grad_logits_low = grad_logits.astype(BF)
        grad_router = jnp.einsum("td,te->ed", normed2_low, grad_logits_low, preferred_element_type=F32)
        grad_normed2 = grad_normed2 + jnp.einsum(
            "te,de->td", grad_logits_low, router, preferred_element_type=F32
        )
        grad_hidden_part, grad_gain_mlp = mlp_norm_back(grad_normed2)
        grad_hidden = cotangent[0].astype(F32) + grad_hidden_part
        grad_low = grad_hidden.astype(BF)
        spare = -(total_experts + 1) % 8
        small = jnp.concatenate([grad_router, grad_gain_mlp[None], jnp.zeros((spare, width), F32)])

    out_sum = lax.psum_scatter(out_parts, "expert", scatter_dimension=0, tiled=False)

    d_tokens, d_w_query, d_w_key, d_w_value, d_w_out, small, *crossed = finish_all(
        (grad_low, grad_hidden, tokens[0], gain_attn[None], w_rows, query_low,
         key_low, value_low, attended_low, probs, query_unit, key_unit, scales,
         gain_query[None], gain_key[None], cosine, sine, normed_all, *w_cols, small),
        expert_parts,
    )
    out_sum = after(out_sum, d_w_out)
    if roomy:
        (d_w_gate, d_w_up, d_w_down, mixed, d_tokens, d_w_query, d_w_key, d_w_value,
         d_w_out) = add_up(
            seq_me.astype(jnp.int32)[None], gate_sum,
            up_parts, crossed[0], crossed[1], down_parts, crossed[2], crossed[3],
            hidden, out_sum, d_tokens, d_w_query, d_w_key, d_w_value, d_w_out,
        )
        d_w_gate = d_w_gate.reshape(experts_local, width // seq_count, -1)
        d_w_up = d_w_up.reshape(d_w_gate.shape)
        d_w_down = d_w_down.reshape(experts_local, -1, width)
    else:
        mixed = (hidden + out_sum.astype(F32)).astype(BF)
    return (
        mixed[None],
        d_tokens[None],
        small[-6],
        d_w_query,
        d_w_key,
        d_w_value,
        small[-8],
        small[-7],
        d_w_out,
        small[total_experts],
        small[:total_experts].T,
        d_w_gate,
        d_w_up,
        d_w_down,
    )


def solution(mesh):
    return jax.shard_map(
        local,
        mesh=mesh,
        in_specs=(
            P("expert", "seq", None),
            P("expert", None),
            P("expert", "seq", None),
            P(),
            P(("seq", "expert"), None),
            P(("seq", "expert"), None),
            P(("seq", "expert"), None),
            P(),
            P(),
            P(("seq", "expert"), None),
            P(),
            P(),
            P("expert", None, None),
            P("expert", None, None),
            P("expert", None, None),
            P("expert", "seq", None),
        ),
        out_specs=(
            P("expert", "seq", None),
            P("expert", "seq", None),
            P(),
            P(("seq", "expert"), None),
            P(("seq", "expert"), None),
            P(("seq", "expert"), None),
            P(),
            P(),
            P(("seq", "expert"), None),
            P(),
            P(),
            P("expert", "seq", None),
            P("expert", "seq", None),
            P("expert", "seq", None),
        ),
        check_vma=False,
    )
```

```python
from functools import partial

import jax
import jax.numpy as jnp
from jax import lax
from jax.experimental import pallas as pl
from jax.experimental.pallas import tpu as pltpu
from jax.sharding import PartitionSpec as P

HEADS = 16
MOST = 64
BF = jnp.bfloat16
F32 = jnp.float32

norm_eps = 1e-05
masked_score = -1e30


MESH = pl.DeviceIdType.MESH
ANY = pl.BlockSpec(memory_space=pl.ANY)
IN_VMEM = pl.BlockSpec(memory_space=pltpu.VMEM)
VMEM_BYTES = 63 << 20


def product(left, right):
    return jnp.dot(left, right, preferred_element_type=F32)


def rms_norm(values, norm_gain):
    return (
        values * lax.rsqrt(jnp.mean(values * values, axis=-1, keepdims=True) + norm_eps) * norm_gain
    )


def swap(value, axis):
    n = lax.axis_size(axis)
    return lax.ppermute(value, axis, [(i, i ^ 1) for i in range(n)])


def shift(value, axis):
    n = lax.axis_size(axis)
    return lax.ppermute(value, axis, [(i, (i + 2) % n) for i in range(n)])


def flip(value, axis, delta):
    n = lax.axis_size(axis)
    return lax.ppermute(value, axis, [(i, i ^ delta) for i in range(n)])


def owners(axis):
    n = lax.axis_size(axis)
    me = lax.axis_index(axis)
    outer, inner = me // 2, me % 2
    return [((outer - i) % (n // 2)) * 2 + (inner ^ b) for i in range(n // 2) for b in range(2)]


def gather_blocks(value, axis):
    blocks = []
    current = value
    for i in range(lax.axis_size(axis) // 2):
        if i:
            current = shift(current, axis)
        blocks += [current, swap(current, axis)]
    return blocks


def add_low(left, right):
    return (left.astype(F32) + right.astype(F32)).astype(BF)


def scatter_sum(blocks, axis):
    outer_count = lax.axis_size(axis) // 2
    pairs = {}
    for t in list(range(1, outer_count)) + [0]:
        arrived = swap(blocks[2 * t + 1], axis)
        pairs[t] = blocks[2 * t].astype(F32) + arrived.astype(F32)
    total = pairs[1 % outer_count]
    for t in range(1, outer_count):
        arrived = shift(total.astype(BF), axis)
        total = arrived.astype(F32) + pairs[(t + 1) % outer_count]
    return total


def all_sum(value, axes):
    for axis in axes:
        delta = 1
        while delta < lax.axis_size(axis):
            value = value + flip(value, axis, delta)
            delta *= 2
    return value


def exchange(parts, axis):
    n = lax.axis_size(axis)
    me = lax.axis_index(axis)
    out = parts
    for delta in range(1, n):
        other = me ^ delta
        got = flip(lax.dynamic_index_in_dim(parts, other, 0, keepdims=False), axis, delta)
        out = lax.dynamic_update_index_in_dim(out, got, other, 0)
    return out


def after(value, *others):
    return lax.optimization_barrier((value,) + others)[0]


def remote(src, dst, send_sem, recv_sem, device):
    return pltpu.make_async_remote_copy(
        src_ref=src,
        dst_ref=dst,
        send_sem=send_sem,
        recv_sem=recv_sem,
        device_id=device,
        device_id_type=MESH,
    )


def greet(devices):
    barrier = pltpu.get_barrier_semaphore()
    for device in devices:
        pl.semaphore_signal(barrier, inc=1, device_id=device, device_id_type=MESH)
    pl.semaphore_wait(barrier, len(devices))


class Ring:
    def __init__(self, axis):
        self.axis = axis
        self.size = lax.axis_size(axis)
        self.outer_count = self.size // 2
        self.me = lax.axis_index(axis)
        self.outer, self.inner = self.me // 2, self.me % 2
        self.pair = {axis: self.outer * 2 + (1 - self.inner)}
        self.next = {axis: self.at(-1) * 2 + self.inner}
        self.last = {axis: self.at(1) * 2 + self.inner}

    def at(self, back):
        return lax.rem(self.outer - back + self.outer_count, self.outer_count)

    def partners(self):
        if self.outer_count == 1:
            return [self.pair]
        if self.outer_count == 2:
            return [self.pair, self.next]
        return [self.pair, self.next, self.last]


class Gather:
    def __init__(self, ring, place, send_sems, recv_sems):
        self.ring, self.place = ring, place
        self.send_sems, self.recv_sems = send_sems, recv_sems
        self.copies = []

    def block(self, back):
        return self.place(self.ring.at(back) * 2 + self.ring.inner)

    def _send(self, back, src):
        ring = self.ring
        if back < ring.outer_count - 1:
            copy = remote(src, self.block(back), self.send_sems.at[back, 0],
                          self.recv_sems.at[back + 1, 0], ring.next)
            copy.start()
            self.copies.append(copy)
        copy = remote(src, self.block(back), self.send_sems.at[back, 1],
                      self.recv_sems.at[back, 1], ring.pair)
        copy.start()
        self.copies.append(copy)

    def start(self, src):
        self._send(0, src)

    def relay(self, back):
        dst = self.block(back)
        remote(dst, dst, self.send_sems.at[back - 1, 0], self.recv_sems.at[back, 0],
               self.ring.next).wait_recv()
        self._send(back, dst)

    def finish(self):
        ring = self.ring
        for back in range(ring.outer_count):
            dst = self.place(ring.at(back) * 2 + 1 - ring.inner)
            remote(dst, dst, self.send_sems.at[back, 1], self.recv_sems.at[back, 1],
                   ring.pair).wait_recv()
        for copy in self.copies:
            copy.wait_send()


def gather_sems(ring, chunks):
    shape = (chunks, ring.outer_count, 2)
    return [pltpu.SemaphoreType.DMA(shape), pltpu.SemaphoreType.DMA(shape)]


class Scatter:
    def __init__(self, ring, x_ref, chunks, own, land, ringbuf, out, own_sems, sems):
        self.ring, self.x_ref, self.chunks = ring, x_ref, chunks
        self.own, self.land, self.ringbuf, self.out = own, land, ringbuf, out
        self.own_sems, self.sems = own_sems, sems
        self.order = list(range(1, ring.outer_count)) + [0]
        self.rows = x_ref.shape[1] // chunks

    def cut(self, c):
        return pl.ds(c * self.rows, self.rows)

    def pair_copy(self, t, c):
        ring = self.ring
        src = self.x_ref.at[ring.at(t) * 2 + 1 - ring.inner, self.cut(c)]
        return remote(src, self.land.at[t, self.cut(c)], self.sems.at[0, t, c],
                      self.sems.at[1, t, c], ring.pair)

    def slot(self, t):
        return (t - 2) % self.ring.outer_count

    def own_copy(self, t):
        src = self.x_ref.at[self.ring.at(t) * 2 + self.ring.inner]
        return pltpu.make_async_copy(src, self.own.at[t], self.own_sems.at[t])

    def ring_copy(self, t, c):
        to = (t + 1) % self.ring.outer_count
        return remote(self.out.at[t - 1, self.cut(c)], self.ringbuf.at[self.slot(to), self.cut(c)],
                      self.sems.at[2, t, c], self.sems.at[3, to, c], self.ring.next)

    def start_place(self, t):
        self.own_copy(t).start()
        for c in range(self.chunks):
            self.pair_copy(t, c).start()

    def start(self):
        for t in self.order:
            self.start_place(t)

    def mine(self, t, c):
        return self.own[t, self.cut(c)]

    def arrive(self, t, c):
        if c == 0:
            self.own_copy(t).wait()
        self.pair_copy(t, c).wait_recv()

    def step(self, t, c):
        self.arrive(t, c)
        cut = self.cut(c)
        total = self.mine(t, c).astype(F32) + self.land[t, cut].astype(F32)
        if t != self.order[0]:
            self.ring_copy((t - 1) % self.ring.outer_count, c).wait_recv()
            total = total + self.ringbuf[self.slot(t), cut].astype(F32)
        if t:
            self.out[t - 1, cut] = total.astype(BF)
            self.ring_copy(t, c).start()
        return total

    def finish(self):
        for t in self.order:
            for c in range(self.chunks):
                self.pair_copy(t, c).wait_send()
                if t:
                    self.ring_copy(t, c).wait_send()


class RingFirst:
    def __init__(self, ring, parts, land, ringbuf, sems):
        self.ring, self.parts, self.land, self.ringbuf, self.sems = ring, parts, land, ringbuf, sems
        self.order = list(range(1, ring.outer_count)) + [0]

    def two(self, t):
        return pl.ds(self.ring.at(t) * 2, 2)

    def ring_copy(self, t):
        to = (t + 1) % self.ring.outer_count
        slot = (to - 2) % self.ring.outer_count
        return remote(self.parts.at[self.two(t)], self.ringbuf.at[slot], self.sems.at[0, t],
                      self.sems.at[1, to], self.ring.next)

    def pair_copy(self):
        src = self.parts.at[self.ring.outer * 2 + 1 - self.ring.inner]
        return remote(src, self.land, self.sems.at[2, 0], self.sems.at[3, 0], self.ring.pair)

    def start(self):
        self.ring_copy(1).start()

    def step(self, t):
        self.ring_copy((t - 1) % self.ring.outer_count).wait_recv()
        slot = (t - 2) % self.ring.outer_count
        total = self.parts[self.two(t)].astype(F32) + self.ringbuf[slot].astype(F32)
        self.parts[self.two(t)] = total.astype(BF)
        if t:
            self.ring_copy(t).start()
        else:
            self.pair_copy().start()

    def last(self):
        self.pair_copy().wait_recv()
        mine = self.parts[self.ring.outer * 2 + self.ring.inner]
        return mine.astype(F32) + self.land[...].astype(F32)

    def finish(self):
        for t in self.order[:-1]:
            self.ring_copy(t).wait_send()
        self.pair_copy().wait_send()


def ring_first_scratch(axis, rows, columns):
    size = lax.axis_size(axis)
    low = lambda *shape: pltpu.VMEM(shape, BF)
    return [low(size, rows, columns), low(rows, columns), low(size // 2 - 1, 2, rows, columns),
            pltpu.SemaphoreType.DMA((4, size // 2))]


class PlaceScatter(Scatter):
    def __init__(self, ring, parts, chunks, land, ringbuf, sems):
        super().__init__(ring, parts, chunks, None, land, ringbuf, None, None, sems)

    def block(self, t):
        return self.ring.at(t) * 2 + self.ring.inner

    def ring_copy(self, t, c):
        to = (t + 1) % self.ring.outer_count
        return remote(self.x_ref.at[self.block(t), self.cut(c)], self.ringbuf.at[self.slot(to), self.cut(c)],
                      self.sems.at[2, t, c], self.sems.at[3, to, c], self.ring.next)

    def start_place(self, t):
        for c in range(self.chunks):
            self.pair_copy(t, c).start()

    def step(self, t, c):
        self.pair_copy(t, c).wait_recv()
        cut, mine = self.cut(c), self.block(t)
        total = self.x_ref[mine, cut].astype(F32) + self.land[t, cut].astype(F32)
        if t != self.order[0]:
            self.ring_copy((t - 1) % self.ring.outer_count, c).wait_recv()
            total = total + self.ringbuf[self.slot(t), cut].astype(F32)
        if t:
            self.x_ref[mine, cut] = total.astype(BF)
            self.ring_copy(t, c).start()
        return total


def scatter_scratch(axis, rows, columns, chunks):
    outer_count = lax.axis_size(axis) // 2
    buf = pltpu.VMEM((outer_count, rows, columns), BF)
    less = pltpu.VMEM((max(outer_count - 1, 1), rows, columns), BF)
    return [buf, buf, less, less, pltpu.SemaphoreType.DMA((outer_count,)),
            pltpu.SemaphoreType.DMA((4, outer_count, chunks))]


SCATTER_REFS = 6


def kernel_params(number):
    return pltpu.CompilerParams(
        collective_id=number, has_side_effects=True, vmem_limit_bytes=VMEM_BYTES
    )


def call(kernel, number, micros, outs, scratch, *args, specs=None, out_specs=None):
    return pl.pallas_call(
        kernel,
        out_shape=outs,
        in_specs=specs or [ANY] * len(args),
        out_specs=out_specs or jax.tree.map(lambda _: ANY, outs),
        scratch_shapes=scratch,
        compiler_params=kernel_params(number),
        cost_estimate=pl.CostEstimate(
            flops=0, bytes_accessed=micros * 3_000_000, transcendentals=0
        ),
    )(*args)


def weights_kernel(
    wq, wk, wv, tokens, gain, routes, lengths, frequency,
    q_out, k_out, v_out, normed_out, hits_out, cos_out, sin_out, bias_out,
    normed, hits, own_sems, swap_send, swap_recv, tok_send, tok_recv, g_send, g_recv,
):
    seq, group = Ring("seq"), Ring("expert")
    others = [{"seq": seq.me ^ d} for d in range(1, seq.size)]
    greet(others + group.partners())
    wrows = wq.shape[0]
    cols = wq.shape[1] // seq.size
    rows_mine = pl.ds(group.me * wrows, wrows)
    weights = [(wq, q_out), (wk, k_out), (wv, v_out)]

    def columns_of(ref, s):
        return ref.at[:, pl.ds(pl.multiple_of(s * cols, cols), cols)]

    def swap_copy(i, d):
        src, dst = weights[i]
        return remote(columns_of(src, seq.me ^ d), dst.at[seq.me, rows_mine],
                      swap_send.at[i, d], swap_recv.at[i, d], others[d - 1])

    def token_copy(d):
        return remote(normed, normed_out.at[seq.me], tok_send.at[d], tok_recv.at[d], others[d - 1])

    own = [
        pltpu.make_async_copy(columns_of(src, seq.me), dst.at[seq.me, rows_mine], own_sems.at[i])
        for i, (src, dst) in enumerate(weights)
    ]
    own.append(pltpu.make_async_copy(normed, normed_out.at[seq.me], own_sems.at[3]))
    own.append(pltpu.make_async_copy(hits, hits_out.at[group.me], own_sems.at[4]))
    for i in range(3):
        own[i].start()
        for d in range(1, seq.size):
            swap_copy(i, d).start()
    value = tokens[...].astype(F32)
    inv = lax.rsqrt(jnp.mean(value * value, axis=-1, keepdims=True) + norm_eps)
    normed[...] = (value * inv * gain[...]).astype(BF)
    names = lax.broadcasted_iota(jnp.int32, hits.shape, 1)
    hit = jnp.zeros(hits.shape, F32)
    for k in range(routes.shape[1]):
        hit = jnp.where(routes[:, k : k + 1] == names, 1.0, hit)
    hits[...] = hit.astype(BF)
    own[3].start()
    own[4].start()
    for d in range(1, seq.size):
        token_copy(d).start()

    length = bias_out.shape[0]

    def starts_of(places):
        first, doc = jnp.zeros_like(places), jnp.zeros_like(places)
        end = jnp.zeros((1, 1), jnp.int32)
        for d in range(lengths.shape[1]):
            end = end + lengths[:, d : d + 1]
            passed = places >= end
            first = jnp.where(passed, end, first)
            doc = doc + jnp.where(passed, 1, 0)
        return first, doc

    column = lax.broadcasted_iota(jnp.int32, (length, 128), 0)
    first, doc = starts_of(column)
    angles = (column - first).astype(F32) * frequency[...]
    left = lax.broadcasted_iota(jnp.int32, (length, 128), 1) < 64
    cos_out[...] = jnp.cos(angles)
    sine = jnp.sin(angles)
    sin_out[...] = jnp.where(left, sine, -sine)
    row = lax.broadcasted_iota(jnp.int32, (1, length), 1)
    row_doc = starts_of(row)[1]
    bias_out[...] = jnp.where(
        (doc[:, :1] == row_doc) & (row <= column[:, :1]), 0.0, masked_score
    )

    def placed(ref):
        return lambda e: ref.at[:, pl.ds(e * wrows, wrows)]

    gathers = [
        Gather(group, placed(dst), g_send.at[i], g_recv.at[i])
        for i, (_, dst) in enumerate(weights)
    ]
    gathers.append(Gather(group, lambda e: hits_out.at[e], g_send.at[3], g_recv.at[3]))
    gathers[3].start(hits)
    for i in range(3):
        own[i].wait()
        for d in range(1, seq.size):
            remote(weights[i][1].at[seq.me ^ d, rows_mine], weights[i][1].at[seq.me ^ d, rows_mine],
                   swap_send.at[i, d], swap_recv.at[i, d], others[d - 1]).wait_recv()
        gathers[i].start(weights[i][1].at[:, rows_mine])
    for back in range(1, group.outer_count):
        for gather in gathers:
            gather.relay(back)
    for gather in gathers:
        gather.finish()
    for d in range(1, seq.size):
        there = normed_out.at[seq.me ^ d]
        remote(there, there, tok_send.at[d], tok_recv.at[d], others[d - 1]).wait_recv()
        token_copy(d).wait_send()
        for i in range(3):
            swap_copy(i, d).wait_send()
    own[3].wait()
    own[4].wait()


def gather_weights(wq, wk, wv, tokens, gain, routes, lengths, frequency):
    seq_count, group_count = lax.axis_size("seq"), lax.axis_size("expert")
    width = wq.shape[1]
    w_shape = jax.ShapeDtypeStruct((seq_count, width // seq_count, width // seq_count), BF)
    rows = tokens.shape[0]
    length = rows * seq_count
    dma = pltpu.SemaphoreType.DMA
    return call(
        weights_kernel, 1, 90,
        (w_shape, w_shape, w_shape,
         jax.ShapeDtypeStruct((seq_count,) + tokens.shape, BF),
         jax.ShapeDtypeStruct((group_count, rows, 128), BF),
         jax.ShapeDtypeStruct((length, 128), F32), jax.ShapeDtypeStruct((length, 128), F32),
         jax.ShapeDtypeStruct((length, length), F32)),
        [pltpu.VMEM(tokens.shape, BF), pltpu.VMEM((rows, 128), BF), dma((5,)), dma((3, seq_count)), dma((3, seq_count)), dma((seq_count,)), dma((seq_count,)),
         dma((4, group_count // 2, 2)), dma((4, group_count // 2, 2))],
        wq, wk, wv, tokens, gain, routes, lengths, frequency,
        specs=[ANY] * 3 + [IN_VMEM] * 5, out_specs=(ANY,) * 5 + (IN_VMEM,) * 3,
    )


HIDDEN_CHUNKS = 4


def turn(values, cos_rows, sin_rows):
    return values * cos_rows + pltpu.roll(values, values.shape[1] // 2, 1) * sin_rows


def row_table(left, right):
    lanes = lax.broadcasted_iota(jnp.int32, (left.shape[0], 128), 1)
    return jnp.where(lanes == 0, left, jnp.where(lanes == 1, right, 0.0)).T[:8]


def from_row_table(table):
    return jnp.concatenate([table, jnp.zeros((120, table.shape[1]), F32)], axis=0).T


def attend_kernel(
    normed, wq, wk, wv, w_rows, bias, cosine, sine, gain_q, gain_k, tokens, gain,
    hidden_out, all_out, q_low, k_low, v_low, attended, probs_out, q_unit, k_unit, scales,
    parts, land, ringbuf, part_sems, low, normed_v, wq_v, wk_v, wv_v, rows_v, probs, row_send, row_land,
    load_sems, low_sems, g_send, g_recv, row_sems, probs_sems,
):
    seq, group = Ring("seq"), Ring("expert")
    others = [{"seq": seq.me ^ d} for d in range(1, seq.size)]
    loads = [
        pltpu.make_async_copy(src, dst, load_sems.at[i])
        for i, (src, dst) in enumerate(
            ((normed, normed_v), (wq, wq_v), (wk, wk_v), (wv, wv_v), (w_rows, rows_v))
        )
    ]
    for load in loads:
        load.start()
    greet(others + group.partners())
    length, cols = q_low.shape
    toks, width = tokens.shape
    head_dim = cosine.shape[1]
    heads = cols // head_dim
    scale = head_dim**-0.5

    def head(h):
        return slice(h * head_dim, (h + 1) * head_dim)

    def project(w, out):
        for c in range(0, cols, 256):
            out[:, c : c + 256] = dot(normed_v[...], w[:, c : c + 256]).astype(out.dtype)

    loads[0].wait()
    loads[1].wait()
    project(wq_v, q_unit)
    loads[2].wait()
    project(wk_v, k_unit)
    squares = [jnp.sum(u[...] * u[...], axis=1, keepdims=True) for u in (q_unit, k_unit)]
    row_send[...] = row_table(*squares)

    def row_copy(d):
        return remote(row_send, row_land.at[d], row_sems.at[0, d], row_sems.at[1, d], others[d - 1])

    for d in range(1, seq.size):
        row_copy(d).start()
    loads[3].wait()
    project(wv_v, v_low)
    total = row_send[...]
    for d in range(1, seq.size):
        row_copy(d).wait_recv()
        total = total + row_land[d]
    for d in range(1, seq.size):
        row_copy(d).wait_send()
    inv = from_row_table(lax.rsqrt(total / width + norm_eps))
    scales[...] = inv
    cos_rows, sin_rows = cosine[...], -sine[...]
    for i, (unit, gains, out) in enumerate(((q_unit, gain_q, q_low), (k_unit, gain_k, k_low))):
        for h in range(heads):
            value = unit[:, head(h)] * inv[:, i : i + 1]
            unit[:, head(h)] = value
            at = pl.ds(pl.multiple_of(seq.me * cols + h * head_dim, head_dim), head_dim)
            out[:, head(h)] = turn(value * gains[:, at], cos_rows, sin_rows).astype(BF)

    def probs_copy(h):
        return pltpu.make_async_copy(probs.at[h], probs_out.at[h], probs_sems.at[h])

    for h in range(heads):
        for b in range(0, length, Q_BLOCK):
            rows = slice(b, b + Q_BLOCK)
            scores = dot(q_low[rows, head(h)], k_low[:, head(h)], 1, 1) * scale + bias[rows]
            weights = jnp.exp(scores - jnp.max(scores, axis=-1, keepdims=True))
            prob = weights / jnp.sum(weights, axis=-1, keepdims=True)
            probs[h, rows] = prob
            attended[rows, head(h)] = dot(prob.astype(BF), v_low[:, head(h)]).astype(BF)
        probs_copy(h).start()

    scatter = PlaceScatter(seq, parts, HIDDEN_CHUNKS, land, ringbuf, part_sems)
    loads[4].wait()

    def out_rows(s):
        at = pl.ds(pl.multiple_of(s * toks, toks), toks)
        parts[s] = dot(attended[at], rows_v[...]).astype(BF)

    for t in scatter.order:
        out_rows(seq.at(t) * 2 + 1 - seq.inner)
        scatter.start_place(t)
        out_rows(seq.at(t) * 2 + seq.inner)
    for t in scatter.order[:-1]:
        for c in range(HIDDEN_CHUNKS):
            scatter.step(t, c)
    gathers, own = [], []
    for c in range(HIDDEN_CHUNKS):
        cut = scatter.cut(c)
        hidden = tokens[cut].astype(F32) + scatter.step(0, c)
        hidden_out[cut] = hidden
        inv = lax.rsqrt(jnp.mean(hidden * hidden, axis=-1, keepdims=True) + norm_eps)
        low[cut] = (hidden * inv * gain[...]).astype(BF)
        own.append(pltpu.make_async_copy(low.at[cut], all_out.at[group.me, cut], low_sems.at[c]))
        own[c].start()
        gathers.append(
            Gather(group, lambda e, cut=cut: all_out.at[e, cut], g_send.at[c], g_recv.at[c])
        )
        gathers[c].start(low.at[cut])
    for back in range(1, group.outer_count):
        for gather in gathers:
            gather.relay(back)
    for c in range(HIDDEN_CHUNKS):
        gathers[c].finish()
        own[c].wait()
    scatter.finish()
    for h in range(heads):
        probs_copy(h).wait()


def attend(normed, wq, wk, wv, w_rows, bias, cosine, sine, gain_q, gain_k, tokens, gain):
    seq_count, group_count = lax.axis_size("seq"), lax.axis_size("expert")
    toks, width = tokens.shape
    length, cols = normed.shape[0], wq.shape[1]
    heads = cols // cosine.shape[1]
    dma = pltpu.SemaphoreType.DMA
    low = lambda *shape: pltpu.VMEM(shape, BF)
    full = lambda *shape: pltpu.VMEM(shape, F32)
    out = jax.ShapeDtypeStruct
    flat = [out((length, cols), BF)] * 4
    return call(
        attend_kernel, 2, 80,
        (out((toks, width), F32), out((group_count, toks, width), BF), *flat,
         out((heads, length, length), F32), out((length, cols), F32), out((length, cols), F32),
         out((length, 128), F32)),
        place_scratch("seq", seq_count, toks, width, HIDDEN_CHUNKS)
        + [low(toks, width), low(length, width), low(width, cols), low(width, cols), low(width, cols),
           low(cols, width), full(heads, length, length), full(8, length), full(seq_count, 8, length),
           dma((5,)), dma((HIDDEN_CHUNKS,)), dma((HIDDEN_CHUNKS, group_count // 2, 2)),
           dma((HIDDEN_CHUNKS, group_count // 2, 2)), dma((2, seq_count)), dma((heads,))],
        normed, wq, wk, wv, w_rows, bias, cosine, sine, gain_q, gain_k, tokens, gain,
        specs=[ANY] * 5 + [IN_VMEM] * 7,
        out_specs=(IN_VMEM, ANY) + (IN_VMEM,) * 4 + (ANY,) + (IN_VMEM,) * 3,
    )


ROW_CHUNKS = 2


def rows_kernel(parts, out, *scratch):
    group = Ring("expert")
    greet(group.partners())
    scatter = Scatter(group, parts, ROW_CHUNKS, *scratch)
    scatter.start()
    for t in scatter.order:
        for c in range(ROW_CHUNKS):
            total = scatter.step(t, c)
            if not t:
                out[scatter.cut(c)] = total
    scatter.finish()


def sum_rows(parts):
    rows, width = parts.shape[1:]
    return call(
        rows_kernel, 3, 50, jax.ShapeDtypeStruct((rows, width), F32),
        scatter_scratch("expert", rows, width, ROW_CHUNKS), parts, out_specs=IN_VMEM,
    )


def dot(left, right, left_dim=1, right_dim=0):
    return lax.dot_general(
        left, right, (((left_dim,), (right_dim,)), ((), ())), preferred_element_type=F32
    )


GRAD_CHUNKS = 2
TILE = 256


def expert_kernel(
    n2, cot, hits, router, wg, wu, wd, hidden, cot_mine, gain,
    grad_out, low_out, small_out, out_parts, d_gate, d_up, d_down,
    stage, parts, routed, cot_rows, wg_v, wu_v, wd_v, scaled, ggate, gup, gate_sums, gates, one_hots,
    land, ringbuf, in_sems, w_sems, part_sems, wide_sems, out_sems, last_sem,
    gate_send, gate_keep, gate_land, gate_out, gate_in, gate_sems,
):
    seq, group = Ring("seq"), Ring("expert")
    groups, toks, width = n2.shape
    experts, rows, _ = routed.shape
    slots = rows // groups
    ff = wg_v.shape[1]
    n_total = experts * groups
    order = group_order(group)
    pairs = len(order)
    wide_at = pl.ds(0, width)

    def two(k):
        return pl.ds(group.at(order[k]) * 2, 2)

    def stage_copy(k):
        return pltpu.make_async_copy(n2.at[two(k)], stage.at[pl.ds(2 * k, 2)], in_sems.at[0, k])

    def cot_copy(k):
        return pltpu.make_async_copy(cot.at[two(k)], parts.at[two(k), :, wide_at], in_sems.at[1, k])

    def weight_copy(i, j):
        src, dst = ((wg, wg_v), (wu, wu_v), (wd, wd_v))[i]
        return pltpu.make_async_copy(src.at[j], dst, w_sems.at[i])

    def each(count, body):
        lax.fori_loop(0, count, lambda i, _: (body(i), 0)[1], 0)

    for k in range(pairs):
        stage_copy(k).start()
    for i in range(3):
        weight_copy(i, 0).start()
    for k in range(pairs):
        cot_copy(k).start()
    greet(seq.partners() + group.partners())

    lanes = lax.broadcasted_iota(jnp.int32, (toks, 128), 1)
    first_half = lanes < slots
    slot_of = jnp.where(first_half, lanes, lanes - slots).astype(F32)
    earlier = jnp.where(
        lax.broadcasted_iota(jnp.int32, (toks, toks), 0)
        > lax.broadcasted_iota(jnp.int32, (toks, toks), 1), 1.0, 0.0
    ).astype(BF)

    def softmax(logits):
        known = lax.broadcasted_iota(jnp.int32, logits.shape, 1) < n_total
        logits = jnp.where(known, logits, masked_score)
        weights = jnp.exp(logits - jnp.max(logits, axis=-1, keepdims=True))
        return weights / jnp.sum(weights, axis=-1, keepdims=True)

    def of_mine(values):
        first, second = [
            jnp.sum(jnp.where(lanes == group.me * experts + j, values, 0.0), axis=1, keepdims=True)
            for j in range(experts)
        ]
        return jnp.where(first_half, first, second)

    one_hots[...] = jnp.zeros_like(one_hots)
    for k in range(pairs):
        stage_copy(k).wait()
        for b in range(2):
            p = 2 * k + b
            hit = hits[group.at(order[k]) * 2 + b]
            rank = of_mine(dot(earlier, hit))
            chosen = (of_mine(hit.astype(F32)) > 0.0) & (rank == slot_of)
            one_hot = jnp.where(chosen, 1.0, 0.0)
            gate = of_mine(softmax(dot(stage[p], router[...])))
            row = jnp.sum(one_hot * gate, axis=0, keepdims=True)
            column = jnp.broadcast_to(row, (128, 128)).T
            for j in range(experts):
                gates[j, p * slots : (p + 1) * slots] = column[j * slots : (j + 1) * slots]
            one_hots[k, b * toks : (b + 1) * toks, b * 128 : (b + 1) * 128] = one_hot.astype(BF)

    def pick(k, values, dst):
        got = dot(one_hots[k], values.reshape(2 * toks, width), 0, 0).astype(BF)
        for b in range(2):
            at = slice((2 * k + b) * slots, (2 * k + b + 1) * slots)
            for j in range(experts):
                start = b * 128 + j * slots
                dst[j, at] = got[start : start + slots]

    for k in range(pairs):
        pick(k, stage[2 * k : 2 * k + 2], routed)
    for k in range(pairs):
        cot_copy(k).wait()
        pick(k, parts[two(k), :, wide_at], cot_rows)

    def hidden_tiles(j, start, count):
        span = slice(start, start + count)

        def tile(f):
            at = pl.ds(pl.multiple_of(f * TILE, TILE), TILE)
            gate_pre = dot(routed[j, span], wg_v[:, at])
            up_pre = dot(routed[j, span], wu_v[:, at])
            unit = dot(cot_rows[j, span], wd_v[at, :], 1, 1)
            gate = gates[j, span][:, :1]
            sig = 1.0 / (1.0 + jnp.exp(-gate_pre))
            silu = gate_pre * sig
            active = silu * up_pre
            low = active.astype(BF).astype(F32)
            gate_sums[j, span] += jnp.sum(unit * low, axis=-1, keepdims=True)
            scaled[j, span, at] = (low * gate).astype(BF)
            grad_active = unit * gate
            ggate[j, span, at] = (
                grad_active * up_pre * sig * (1.0 + gate_pre * (1.0 - sig))
            ).astype(BF)
            gup[j, span, at] = (grad_active * silu).astype(BF)

        each(ff // TILE, tile)

    def row_tiles(j, start, count):
        span = slice(start, start + count)
        blocks = slice(start // slots, (start + count) // slots)

        def tile(d):
            at = pl.ds(pl.multiple_of(d * TILE, TILE), TILE)
            grad = dot(ggate[j, span], wg_v[at, :], 1, 1) + dot(gup[j, span], wu_v[at, :], 1, 1)
            stage[blocks, j * slots : (j + 1) * slots, at] = grad.astype(BF).reshape(
                count // slots, slots, TILE
            )

        each(width // TILE, tile)

    scatter = PlaceScatter(group, parts, GRAD_CHUNKS, land, ringbuf, part_sems)
    row_lanes = lanes[:slots]

    def place(k):
        value = dot(one_hots[k], stage[2 * k : 2 * k + 2].reshape(2 * toks, width))
        parts[two(k), :, wide_at] = value.astype(BF).reshape(2, toks, width)
        sums = []
        for p in (2 * k, 2 * k + 1):
            for j in range(experts):
                value = gate_sums[j, p * slots : (p + 1) * slots]
                first = value.astype(BF).astype(F32)
                mine = group.me * experts + j
                sums.append(jnp.where(row_lanes == mine, first,
                                      jnp.where(row_lanes == mine + n_total, value - first, 0.0)))
        value = dot(one_hots[k], jnp.concatenate(sums, axis=0).astype(BF))
        parts[two(k), :, pl.ds(width, 128)] = value.astype(BF).reshape(2, toks, 128)
        scatter.start_place(order[k])

    side, short = width // seq.size, ff // seq.size

    def wide_grad(right, s, j):
        at = pl.ds(pl.multiple_of(s * side, side), side)
        return dot(routed[j, :, at], right[j], 0, 0).astype(BF)

    def rows_of(j):
        return pl.ds(j * side, side)

    def gate_pair(t, j):
        return remote(gate_send, gate_land.at[t, rows_of(j)], gate_sems.at[0, t, j],
                      gate_sems.at[1, t, j], seq.pair)

    def gate_cross(j):
        return remote(gate_out.at[rows_of(j)], gate_in.at[rows_of(j)], gate_sems.at[2, 0, j],
                      gate_sems.at[3, 0, j], seq.next)

    def gate_part(j):
        for t in (1, 0):
            if t == 0:
                gate_pair(1, j).wait_send()
            elif j:
                gate_pair(0, j - 1).wait_send()
            gate_send[...] = wide_grad(ggate, seq.at(t) * 2 + 1 - seq.inner, j)
            gate_pair(t, j).start()
            mine = wide_grad(ggate, seq.at(t) * 2 + seq.inner, j)
            if t:
                gate_pair(t, j).wait_recv()
                total = mine.astype(F32) + gate_land[t, rows_of(j)].astype(F32)
                gate_out[rows_of(j)] = total.astype(BF)
                gate_cross(j).start()
            else:
                gate_keep[rows_of(j)] = mine

    gate_sums[...] = jnp.zeros_like(gate_sums)
    half = rows // 2
    for j in range(experts):
        for i in range(3):
            weight_copy(i, j).wait()
        if j + 1 < experts:
            hidden_tiles(j, 0, rows)
            weight_copy(2, j + 1).start()
            row_tiles(j, 0, rows)
            weight_copy(0, j + 1).start()
            weight_copy(1, j + 1).start()
            gate_part(j)
        else:
            hidden_tiles(j, 0, half)
            row_tiles(j, 0, half)
            for k in range(pairs // 2):
                place(k)
            hidden_tiles(j, half, half)
            weight_copy(2, 0).start()
            row_tiles(j, half, half)
            for k in range(pairs // 2, pairs):
                place(k)

    def grad_step(t):
        for c in range(GRAD_CHUNKS):
            total = scatter.step(t, c)
            if not t:
                finish_rows(c, total)

    def finish_rows(c, total):
        cut = scatter.cut(c)
        value = hidden[cut]
        inv = lax.rsqrt(jnp.mean(value * value, axis=-1, keepdims=True) + norm_eps)
        unit = value * inv
        normed2 = (unit * gain[...]).astype(BF)
        probs = softmax(dot(normed2, router[...]))
        both = total[:, width:]
        grad_probs = jnp.where(
            lax.broadcasted_iota(jnp.int32, both.shape, 1) < n_total,
            both + pltpu.roll(both, 128 - n_total, 1), 0.0,
        )
        grad_logits = probs * (grad_probs - jnp.sum(probs * grad_probs, axis=-1, keepdims=True))
        grad_logits = grad_logits.astype(BF)
        grad = total[:, :width] + dot(grad_logits, router[...], 1, 1)
        gained = grad * gain[...]
        mean = jnp.mean(gained * unit, axis=-1, keepdims=True)
        result = cot_mine[cut].astype(F32) + inv * (gained - unit * mean)
        grad_out[cut] = result
        low_out[cut] = result.astype(BF)
        count = small_out.shape[0]
        sums = dot(grad_logits, normed2, 0, 0)[:count]
        line = lax.broadcasted_iota(jnp.int32, sums.shape, 0)
        sums = jnp.where(line == n_total, jnp.sum(grad * unit, axis=0, keepdims=True), sums)
        small_out[...] = sums if c == 0 else small_out[...] + sums

    def send_wide(right, out, s):
        copies = [
            pltpu.make_async_copy(
                wg_v.at[pl.ds(j * side, side)], out.at[s, pl.ds(j * side, side)], wide_sems.at[j]
            )
            for j in range(experts)
        ]
        for j in range(experts):
            wg_v[pl.ds(j * side, side)] = wide_grad(right, s, j)
            copies[j].start()
        for copy in copies:
            copy.wait()

    def send_tall(s):
        at = pl.ds(pl.multiple_of(s * short, short), short)
        per = short // toks
        copies = []
        for j in range(experts):
            value = dot(scaled[j, :, at], cot_rows[j], 0, 0).astype(BF)
            for i in range(per):
                place_at = j * per + i
                stage[place_at] = value[i * toks : (i + 1) * toks]
                copies.append(pltpu.make_async_copy(
                    stage.at[place_at], d_down.at[s, pl.ds(place_at * toks, toks)],
                    out_sems.at[place_at]))
                copies[-1].start()
        for copy in copies:
            copy.wait()

    for j in range(1, experts):
        gate_part(j)
    grad_step(scatter.order[0])
    if len(scatter.order) > 2:
        grad_step(scatter.order[1])
    each(seq.size, lambda s: send_wide(gup, d_up, s))
    for t in scatter.order[2:-1]:
        grad_step(t)
    each(seq.size, send_tall)

    for j in range(experts):
        weight_copy(2, j).wait()

        def out_tile(d, j=j):
            at = pl.ds(pl.multiple_of(d * TILE, TILE), TILE)
            value = dot(scaled[j], wd_v[:, at])
            stage[:, j * slots : (j + 1) * slots, at] = value.astype(BF).reshape(groups, slots, TILE)

        each(width // TILE, out_tile)
        if j + 1 < experts:
            weight_copy(2, j + 1).start()

    def out_copy(k):
        return pltpu.make_async_copy(stage.at[pl.ds(2 * k, 2)], out_parts.at[two(k)], out_sems.at[k])

    for k in range(pairs):
        value = dot(one_hots[k], stage[2 * k : 2 * k + 2].reshape(2 * toks, width))
        stage[2 * k : 2 * k + 2] = value.astype(BF).reshape(2, toks, width)
        out_copy(k).start()
    grad_step(0)
    for j in range(experts):
        gate_pair(0, j).wait_recv()
        gate_cross(j).wait_recv()
        at = rows_of(j)
        total = gate_keep[at].astype(F32) + gate_land[0, at].astype(F32) + gate_in[at].astype(F32)
        gate_keep[at] = total.astype(BF)
    gate_copy = pltpu.make_async_copy(gate_keep, d_gate, last_sem.at[0])
    gate_copy.start()
    for k in range(pairs):
        out_copy(k).wait()
    gate_copy.wait()
    scatter.finish()
    gate_pair(0, experts - 1).wait_send()
    for j in range(experts):
        gate_cross(j).wait_send()


def run_experts(n2, cot, hits, router, wg, wu, wd, hidden, cot_mine, gain):
    seq_count, group_count = lax.axis_size("seq"), lax.axis_size("expert")
    experts, width, ff = wg.shape
    toks = n2.shape[1]
    rows = group_count * MOST
    outer_count = group_count // 2
    columns = width + 128
    small_rows = -(-(experts * group_count + 1) // 8) * 8
    dma = pltpu.SemaphoreType.DMA
    side, short = width // seq_count, ff // seq_count

    low = lambda *shape: pltpu.VMEM(shape, BF)
    out = jax.ShapeDtypeStruct
    return call(
        expert_kernel, 6, 100,
        (out((toks, width), F32), out((toks, width), BF), out((small_rows, width), F32),
         out((group_count, toks, width), BF),
         out((experts * side, ff), BF),
         out((seq_count, experts * side, ff), BF), out((seq_count, experts * short, width), BF)),
        [low(group_count, toks, width), low(group_count, toks, columns),
         low(experts, rows, width), low(experts, rows, width),
         low(width, ff), low(width, ff), low(ff, width),
         low(experts, rows, ff), low(experts, rows, ff), low(experts, rows, ff),
         pltpu.VMEM((experts, rows, 128), F32), pltpu.VMEM((experts, rows, 128), F32),
         low(outer_count, 2 * toks, 256),
         low(outer_count, toks, columns), low(outer_count - 1, toks, columns),
         dma((2, outer_count)), dma((3,)), dma((4, outer_count, GRAD_CHUNKS)), dma((experts,)),
         dma((group_count,)), dma((1,)),
         low(side, ff), low(experts * side, ff), low(2, experts * side, ff),
         low(experts * side, ff), low(experts * side, ff), dma((4, 2, experts))],
        n2, cot, hits, router, wg, wu, wd, hidden, cot_mine, gain,
        specs=[ANY, ANY, IN_VMEM, IN_VMEM, ANY, ANY, ANY, IN_VMEM, IN_VMEM, IN_VMEM],
        out_specs=(IN_VMEM, IN_VMEM, IN_VMEM, ANY, ANY, ANY, ANY),
    )


NORMED_CHUNKS = 2
CROSS_CHUNKS = 8


class AllSum:
    def __init__(self, steps, sums, land, sems):
        self.steps, self.sums, self.land, self.sems = steps, sums, land, sems
        self.at = 0

    def copy(self, i):
        return remote(self.sums.at[i], self.land.at[i], self.sems.at[0, i], self.sems.at[1, i], self.steps[i])

    def start(self):
        self.copy(0).start()

    def hop(self):
        i = self.at
        if i == len(self.steps):
            return
        self.at += 1
        self.copy(i).wait_recv()
        self.sums[i + 1] = self.sums[i] + self.land[i]
        if self.at < len(self.steps):
            self.copy(self.at).start()

    def result(self):
        while self.at < len(self.steps):
            self.hop()
        for i in range(len(self.steps)):
            self.copy(i).wait_send()
        return self.sums[len(self.steps)]


class Cross:
    def __init__(self, seq, parts, land, crossed, bufs, stage, sems):
        self.seq, self.parts, self.land, self.crossed = seq, parts, land, crossed
        self.bufs, self.stage, self.sems = bufs, stage, sems
        self.rows = parts.shape[1] // CROSS_CHUNKS

    def swap(self, t):
        src = self.parts.at[self.seq.at(t) * 2 + 1 - self.seq.inner]
        return remote(src, self.land.at[t], self.sems.at[0, t], self.sems.at[1, t], self.seq.pair)

    def loads(self, i):
        cut = pl.ds(i * self.rows, self.rows)
        own = self.parts.at[self.seq.at(1) * 2 + self.seq.inner, cut]
        return [
            pltpu.make_async_copy(own, self.bufs.at[i % 2, 0], self.sems.at[2, i % 2]),
            pltpu.make_async_copy(self.land.at[1, cut], self.bufs.at[i % 2, 1], self.sems.at[3, i % 2]),
        ]

    def load(self, i):
        if i == 0:
            self.swap(1).wait_recv()
        if i < CROSS_CHUNKS:
            for copy in self.loads(i):
                copy.start()

    def send(self, i):
        cut = pl.ds(i * self.rows, self.rows)
        return remote(self.stage.at[i % 2], self.crossed.at[cut], self.sems.at[4, i % 2],
                      self.sems.at[5, i], self.seq.next)

    def tick(self, i):
        if i == 0:
            self.load(0)
        for copy in self.loads(i):
            copy.wait()
        self.load(i + 1)
        if i >= 2:
            self.send(i - 2).wait_send()
        total = self.bufs[i % 2, 0].astype(F32) + self.bufs[i % 2, 1].astype(F32)
        self.stage[i % 2] = total.astype(BF)
        self.send(i).start()

    def finish(self):
        self.send(CROSS_CHUNKS - 2).wait_send()
        self.send(CROSS_CHUNKS - 1).wait_send()
        for c in range(CROSS_CHUNKS):
            self.send(c).wait_recv()
        self.swap(0).wait_recv()
        self.swap(0).wait_send()
        self.swap(1).wait_send()


def cross_scratch(parts):
    rows, columns = parts.shape[1] // CROSS_CHUNKS, parts.shape[2]
    return [pltpu.VMEM((2, 2, rows, columns), BF), pltpu.VMEM((2, rows, columns), BF),
            pltpu.SemaphoreType.DMA((6, CROSS_CHUNKS))]


def place_scratch(axis, size, rows, columns, chunks):
    outer_count = lax.axis_size(axis) // 2
    return [pltpu.VMEM((size, rows, columns), BF), pltpu.VMEM((outer_count, rows, columns), BF),
            pltpu.VMEM((max(outer_count - 1, 1), rows, columns), BF),
            pltpu.SemaphoreType.DMA((4, outer_count, chunks))]


Q_BLOCK = 256
LATE = ("w_rows", "normed", "probs", "q_unit", "k_unit", "wq", "wk", "wv")
LATE_AT = (4, 17, 9, 10, 11, 18, 19, 20)


def last_kernel(
    grad_low, grad_hidden, tokens, gain, w_rows, q_low, k_low, v_low, attended, probs,
    q_unit, k_unit, scales, gain_q, gain_k, cosine, sine, normed, wq, wk, wv, small, *refs,
    crossings,
):
    expert_parts, refs = refs[:crossings], refs[crossings:]
    late = {}
    refs, copies, load_sems = refs[: -len(LATE) - 1], refs[-len(LATE) - 1 : -1], refs[-1]
    arrays = dict(w_rows=w_rows, probs=probs, q_unit=q_unit, k_unit=k_unit, normed=normed,
                  wq=wq, wk=wk, wv=wv)
    for i, name in enumerate(LATE):
        late[name] = pltpu.make_async_copy(arrays[name], copies[i], load_sems.at[i])
    w_rows, normed, probs, q_unit, k_unit, wq, wk, wv = copies
    d_tokens, d_q, d_k, d_v, d_out, small_out = refs[:6]
    refs = refs[6:]
    cross_out, refs = refs[: 2 * crossings], refs[2 * crossings :]
    cross_bufs, refs = refs[: 3 * crossings], refs[3 * crossings :]
    place = [refs[4 * i : 4 * i + 4] for i in range(5)]
    (grad_all, normed_t, grad_att, grad_g, grad_three, dk_sum, row_send, row_land,
     low_send, low_land, early_buf, early_land, late_buf, late_land,
     own_sem, pack_send, pack_recv, row_sems, swap_sems, early_sems, late_sems) = refs[20:]
    seq, group = Ring("seq"), Ring("expert")
    others = [{"seq": seq.me ^ d} for d in range(1, seq.size)]
    known = [{"expert": group.me ^ (1 << i)} for i in range((group.size - 1).bit_length())]
    across = [{"seq": seq.me ^ (1 << i)} for i in range((seq.size - 1).bit_length())]
    early_sums = AllSum(known[::-1] + across, early_buf, early_land, early_sems)
    late_sums = AllSum(across[:1] + known[::-1] + across[1:], late_buf, late_land, late_sems)
    early_rows = small.shape[0]
    for name in LATE:
        late[name].start()
    greet(others + known + [group.next, group.last])
    length, cols = q_low.shape
    width = tokens.shape[1]
    toks = tokens.shape[0]
    head_dim = cosine.shape[1]
    heads = cols // head_dim
    wrows = d_out.shape[0]
    scale = head_dim**-0.5

    crosses = [
        Cross(seq, expert_parts[i], *cross_out[2 * i : 2 * i + 2], *cross_bufs[3 * i : 3 * i + 3])
        for i in range(crossings)
    ]
    ticks = [(cross, i) for i in range(CROSS_CHUNKS) for cross in crosses]

    def tick(count=1):
        for _ in range(count):
            if ticks:
                cross, i = ticks.pop(0)
                cross.tick(i)

    own = pltpu.make_async_copy(grad_low, grad_all.at[seq.me], own_sem.at[0])
    own.start()
    pack = Gather(seq, lambda s: grad_all.at[s], pack_send, pack_recv)
    pack.start(grad_low)
    early_buf[0] = small[...]
    early_sums.start()
    late_buf[0] = jnp.zeros_like(late_buf[0])
    for t in (1, 0):
        for cross in crosses:
            cross.swap(t).start()
    size = width // seq.size
    late["normed"].wait()
    for s in range(seq.size):
        normed_t[pl.ds(s * size, size)] = normed[:, s * size : (s + 1) * size].T
        if s % 2:
            early_sums.hop()
    for back in range(1, seq.outer_count):
        pack.relay(back)
    tick(2)
    own.wait()
    pack.finish()

    late["w_rows"].wait()
    for c in range(0, cols, Q_BLOCK):
        at = slice(c, c + Q_BLOCK)
        grad_att[:, at] = dot(
            grad_all[...].reshape(length, width), w_rows[at, :], 1, 1
        ).astype(BF)

    query_sums, key_sums, value_sums = [
        PlaceScatter(group, p[0], 1, p[1], p[2], p[3]) for p in place[:3]
    ]
    out_sums = RingFirst(group, *place[3])
    normed_sums = PlaceScatter(seq, place[4][0], NORMED_CHUNKS, *place[4][1:])

    def head(h):
        return slice(h * head_dim, (h + 1) * head_dim)

    early_sums.hop()
    late["probs"].wait()
    for h in range(heads):
        grad_three[2, :, head(h)] = dot(
            probs[h].astype(BF), grad_att[:, head(h)], 0, 0
        ).astype(BF)

    def weight_grad(i, sums):
        for s in range(seq.size):
            value = dot(normed_t[pl.ds(s * size, size)], grad_three[i])
            sums.x_ref[:, pl.ds(s * wrows, wrows)] = value.astype(BF).reshape(
                group.size, wrows, cols
            )
        sums.start()

    tick()
    weight_grad(2, value_sums)
    early_sums.hop()
    for c in range(0, width, 512):
        at = slice(c, c + 512)
        value = dot(attended[...], grad_all[:, :, at].reshape(length, 512), 0, 0)
        out_sums.parts[:, :, at] = value.astype(BF).reshape(group.size, wrows, 512)
    out_sums.start()
    tick()
    out_order, value_order = list(out_sums.order[1:]), list(value_sums.order)

    def out_step():
        if len(out_order) > 1:
            out_sums.step(out_order.pop(0))

    def value_step():
        if len(value_order) > 1:
            value_sums.step(value_order.pop(0), 0)

    row_sums = [jnp.zeros((length, 1), F32), jnp.zeros((length, 1), F32)]
    gain_row = 0
    cos_rows, sin_rows = cosine[...], sine[...]

    def through_rope(i, h, grad, unit, gains):
        turned = turn(grad, cos_rows, sin_rows)
        late_buf[0, pl.ds(i, 1), pl.ds(pl.multiple_of(seq.me * cols, 128) + h * head_dim, head_dim)] = (
            jnp.sum(turned * unit, axis=0, keepdims=True)
        )
        gained = turned * gains
        grad_g[i, :, head(h)] = gained
        row_sums[i] = row_sums[i] + jnp.sum(gained * unit, axis=1, keepdims=True)

    late["q_unit"].wait()
    late["k_unit"].wait()
    early_sums.hop()
    for h in range(heads):
        queries = []
        for b in range(0, length, Q_BLOCK):
            rows = slice(b, b + Q_BLOCK)
            prob = probs[h, rows]
            grad = dot(grad_att[rows, head(h)], v_low[:, head(h)], 1, 1)
            row_dot = jnp.sum(prob * grad, axis=-1, keepdims=True)
            grad_scores = (prob * (grad - row_dot)).astype(BF)
            queries.append(dot(grad_scores, k_low[:, head(h)]) * scale)
            keys = dot(grad_scores, q_low[rows, head(h)], 0, 0)
            dk_sum[...] = keys if b == 0 else dk_sum[...] + keys
        at = pl.ds(pl.multiple_of(seq.me * cols + h * head_dim, head_dim), head_dim)
        through_rope(0, h, jnp.concatenate(queries, axis=0), q_unit[:, head(h)], gain_q[:, at])
        through_rope(1, h, dk_sum[...] * scale, k_unit[:, head(h)], gain_k[:, at])
        if h == 1:
            value_step()

    lanes = lax.broadcasted_iota(jnp.int32, (length, 128), 1)
    table = jnp.where(lanes == 0, row_sums[0], jnp.where(lanes == 1, row_sums[1], 0.0))
    row_send[...] = table.T[:8]

    def row_copy(d):
        return remote(row_send, row_land.at[d], row_sems.at[0, d], row_sems.at[1, d], others[d - 1])

    for d in range(1, seq.size):
        row_copy(d).start()
    out_step()
    total = row_send[...]
    for d in range(1, seq.size):
        row_copy(d).wait_recv()
        total = total + row_land[d]
    for d in range(1, seq.size):
        row_copy(d).wait_send()
    tick(3)
    means = jnp.concatenate([total / width, jnp.zeros((120, length), F32)], axis=0).T
    for i, (unit, sums) in enumerate(((q_unit, query_sums), (k_unit, key_sums))):
        for h in range(heads):
            value = grad_g[i, :, head(h)] - unit[:, head(h)] * means[:, i : i + 1]
            grad_three[i, :, head(h)] = (value * scales[:, i : i + 1]).astype(BF)
        weight_grad(i, sums)
        value_step()
    for name in ("wq", "wk", "wv"):
        late[name].wait()
    for c in range(0, width, 512):
        at = slice(c, c + 512)
        value = dot(grad_three[0], wq[at, :], 1, 1) + dot(grad_three[1], wk[at, :], 1, 1)
        value = value + dot(grad_three[2], wv[at, :], 1, 1)
        normed_sums.x_ref[:, :, at] = value.astype(BF).reshape(seq.size, toks, 512)
    normed_sums.start()
    out_step()
    tick(2)

    swaps = {}

    def swap_copy(i, d):
        src = low_send.at[i, pl.ds((seq.me ^ d) * wrows, wrows)]
        return remote(src, low_land.at[i, seq.me], swap_sems.at[0, i, d], swap_sems.at[1, i, d], others[d - 1])

    def send_columns(i, sums):
        low_send[i] = sums.step(0, 0).astype(BF)
        for d in range(1, seq.size):
            swap_copy(i, d).start()

    while len(value_order) > 1:
        value_step()
    for t in normed_sums.order[:-1]:
        for c in range(NORMED_CHUNKS):
            normed_sums.step(t, c)
    first, *middle = group_order(group)[:-1]
    query_sums.step(first, 0)
    tick()
    key_sums.step(first, 0)
    tick()
    while len(out_order) > 1:
        out_step()
    gain_sum = jnp.zeros((1, width), F32)
    for c in range(NORMED_CHUNKS):
        cut = normed_sums.cut(c)
        grad = normed_sums.step(0, c)
        value = tokens[cut].astype(F32)
        inv = lax.rsqrt(jnp.mean(value * value, axis=-1, keepdims=True) + norm_eps)
        unit = value * inv
        gained = grad * gain[...]
        mean = jnp.mean(gained * unit, axis=-1, keepdims=True)
        d_tokens[cut] = grad_hidden[cut] + inv * (gained - unit * mean)
        gain_sum = gain_sum + jnp.sum(grad * unit, axis=0, keepdims=True)
    late_buf[0, pl.ds(2, 1)] = gain_sum

    late_sums.start()
    tick()
    send_columns(2, value_sums)
    out_sums.step(0)
    for t in middle:
        query_sums.step(t, 0)
        tick(2)
        key_sums.step(t, 0)
        tick(2)
        late_sums.hop()
    d_out[...] = out_sums.last()
    tick()
    send_columns(0, query_sums)
    late_sums.hop()
    send_columns(1, key_sums)
    late_sums.hop()

    tick(len(ticks))
    for i, out in ((2, d_v), (0, d_q), (1, d_k)):
        for d in range(1, seq.size):
            there = low_land.at[i, seq.me ^ d]
            remote(there, there, swap_sems.at[0, i, d], swap_sems.at[1, i, d], others[d - 1]).wait_recv()
            swap_copy(i, d).wait_send()
        low_land[i, seq.me] = low_send[i, pl.ds(pl.multiple_of(seq.me * wrows, wrows), wrows)]
        for s in range(seq.size):
            out[:, s * cols : (s + 1) * cols] = low_land[i, s].astype(F32)
    small_out[pl.ds(0, early_rows)] = early_sums.result()
    small_out[pl.ds(early_rows, 8)] = late_sums.result()
    for cross in crosses:
        cross.finish()
    for sums in (query_sums, key_sums, value_sums, out_sums, normed_sums):
        sums.finish()


def group_order(ring):
    return list(range(1, ring.outer_count)) + [0]


def finish_all(ins, expert_parts):
    seq_count, group_count = lax.axis_size("seq"), lax.axis_size("expert")
    (grad_low, grad_hidden, tokens, gain, w_rows, q_low, *_) = ins
    small = ins[-1]
    rows, width = tokens.shape
    length, cols = q_low.shape
    head_dim = width // HEADS
    wrows = cols // group_count
    side = seq_count * wrows
    count = (seq_count - 1).bit_length() + (group_count - 1).bit_length()
    dma = pltpu.SemaphoreType.DMA
    low = lambda *shape: pltpu.VMEM(shape, BF)
    full = lambda *shape: pltpu.VMEM(shape, F32)
    shape = lambda *dims: jax.ShapeDtypeStruct(dims, F32)
    outs = [shape(rows, width)] + [shape(wrows, width)] * 4 + [shape(small.shape[0] + 8, width)]
    cross_outs, scratch = [], []
    for parts in expert_parts:
        size = parts.shape[1:]
        cross_outs += [jax.ShapeDtypeStruct((2,) + size, BF), jax.ShapeDtypeStruct(size, BF)]
        scratch += cross_scratch(parts)
    for _ in range(3):
        scratch += place_scratch("expert", group_count, side, cols, 1)
    scratch += ring_first_scratch("expert", wrows, width)
    scratch += place_scratch("seq", seq_count, rows, width, NORMED_CHUNKS)
    scratch += [
        low(seq_count, rows, width), low(width, length), low(length, cols),
        full(2, length, cols), low(3, length, cols), full(length, head_dim),
        full(8, length), full(seq_count, 8, length),
        low(3, side, cols), low(3, seq_count, wrows, cols),
        full(count + 1, *small.shape), full(count, *small.shape),
        full(count + 1, 8, width), full(count, 8, width),
        dma((1,)), dma((seq_count // 2, 2)), dma((seq_count // 2, 2)), dma((2, seq_count)),
        dma((2, 3, seq_count)), dma((2, count)), dma((2, count)),
    ]
    scratch += [pltpu.VMEM(ins[i].shape, ins[i].dtype) for i in LATE_AT] + [dma((len(LATE),))]
    return call(
        partial(last_kernel, crossings=len(expert_parts)), 5, 150,
        tuple(outs + cross_outs), scratch, *ins, *expert_parts,
        specs=[ANY if i in (0, *LATE_AT) else IN_VMEM for i in range(len(ins))]
        + [ANY] * len(expert_parts),
        out_specs=tuple([IN_VMEM] * len(outs) + [ANY] * len(cross_outs)),
    )


ADD_STEPS = 8


def add_kernel(
    place, gate, up, up_land, up_in, down, down_land, down_in, hidden, out_sum, *refs
):
    copies, refs = refs[:5], refs[5:]
    d_gate, d_up, d_down, mixed = refs[:4]
    d_gate[...] = gate[...].astype(F32)
    d_up[...] = up[0].astype(F32) + up_land[0].astype(F32) + up_in[...].astype(F32)
    d_down[...] = down[0].astype(F32) + down_land[0].astype(F32) + down_in[...].astype(F32)
    mixed[...] = (hidden[...] + out_sum[...].astype(F32)).astype(BF)
    for src, dst in zip(copies, refs[4:]):
        dst[...] = src[...]


def add_up(place, gate, up, up_land, up_in, down, down_land, down_in, hidden, out_sum, *copies):
    def flat(array):
        rows, columns = array.shape
        return pl.BlockSpec((rows // ADD_STEPS, columns), lambda i, s: (i, 0))

    def first(array):
        _, rows, columns = array.shape
        return pl.BlockSpec((1, rows // ADD_STEPS, columns), lambda i, s: (0, i, 0))

    def own(array):
        _, rows, columns = array.shape
        return pl.BlockSpec((1, rows // ADD_STEPS, columns), lambda i, s: (s[0], i, 0))

    outs = [jax.ShapeDtypeStruct(a.shape, F32) for a in (gate, up_in, down_in)]
    outs += [jax.ShapeDtypeStruct(hidden.shape, BF)]
    outs += [jax.ShapeDtypeStruct(c.shape, c.dtype) for c in copies]
    return pl.pallas_call(
        add_kernel,
        out_shape=outs,
        grid_spec=pltpu.PrefetchScalarGridSpec(
            num_scalar_prefetch=1,
            grid=(ADD_STEPS,),
            in_specs=[flat(gate), own(up), first(up_land), flat(up_in),
                      own(down), first(down_land), flat(down_in), flat(hidden), flat(out_sum)]
            + [flat(c) for c in copies],
            out_specs=[flat(o) for o in outs],
        ),
    )(place, gate, up, up_land, up_in, down, down_land, down_in, hidden, out_sum, *copies)


def each(left, right, how):
    return jnp.einsum(how, left, right, preferred_element_type=F32)


def plain_experts(normed2_all, cot_all, chosen, gate_rows, w_gate, w_up, w_down):
    seq_count, group_count = lax.axis_size("seq"), lax.axis_size("expert")
    experts_local, tok_rows = w_gate.shape[0], chosen.shape[-1]
    total_experts = experts_local * group_count
    chosen_low = chosen.astype(BF)

    def pick_rows(values):
        return jnp.einsum("ejmt,etd->jemd", chosen_low, values, preferred_element_type=F32).astype(BF)

    def place_rows(values):
        return jnp.einsum("ejmt,jemd->etd", chosen_low, values, preferred_element_type=F32).astype(BF)

    routed = pick_rows(normed2_all)
    cot_rows = pick_rows(cot_all)

    gate_pre = each(routed, w_gate, "jemd,jdf->jemf")
    up_pre = each(routed, w_up, "jemd,jdf->jemf")
    sigmoid_gate = jax.nn.sigmoid(gate_pre)
    silu_gate = gate_pre * sigmoid_gate
    active = silu_gate * up_pre
    active_low = active.astype(BF)
    grad_unit = each(cot_rows, w_down, "jemd,jfd->jemf")
    grad_gate_rows = jnp.sum(grad_unit * active_low.astype(F32), axis=-1)
    grad_active = grad_unit * gate_rows
    grad_gate_low = (
        grad_active * up_pre * sigmoid_gate * (1.0 + gate_pre * (1.0 - sigmoid_gate))
    ).astype(BF)
    grad_up_low = (grad_active * silu_gate).astype(BF)
    grad_routed = each(grad_gate_low, w_gate, "jemf,jdf->jemd")
    grad_routed = (grad_routed + each(grad_up_low, w_up, "jemf,jdf->jemd")).astype(BF)
    grad_parts = place_rows(grad_routed)
    grad_normed2 = sum_rows(grad_parts)
    grad_probs_parts = jnp.einsum(
        "ejmt,jem->etj", chosen.astype(F32), grad_gate_rows, precision=lax.Precision.HIGHEST
    )
    grad_probs = lax.all_to_all(grad_probs_parts, "expert", split_axis=0, concat_axis=0, tiled=True)
    grad_probs = grad_probs.transpose(1, 0, 2).reshape(tok_rows, total_experts)

    expert_out = each(active_low, w_down, "jemf,jfd->jemd") * gate_rows
    out_parts = place_rows(expert_out.astype(BF))

    active_scaled = (active_low.astype(F32) * gate_rows).astype(BF)

    def expert_grad(left, right):
        grad = jnp.einsum("jemd,jemf->jdf", left, right, preferred_element_type=F32).astype(BF)
        rows = grad.shape[1] // seq_count
        grad = grad.reshape(experts_local, seq_count, rows, grad.shape[2])
        return scatter_sum(
            [lax.dynamic_index_in_dim(grad, o, 1, keepdims=False) for o in owners("seq")], "seq"
        )

    d_w_gate = expert_grad(routed, grad_gate_low)
    d_w_up = expert_grad(routed, grad_up_low)
    d_w_down = expert_grad(active_scaled, cot_rows)
    return grad_normed2, grad_probs, out_parts, d_w_gate, d_w_up, d_w_down


def local(
    tokens,
    lengths,
    routes,
    gain_attn,
    w_query,
    w_key,
    w_value,
    gain_query,
    gain_key,
    w_out,
    gain_mlp,
    router,
    w_gate,
    w_up,
    w_down,
    cotangent,
):
    seq_count = lax.axis_size("seq")
    group_count = lax.axis_size("expert")
    seq_me = lax.axis_index("seq")
    group_me = lax.axis_index("expert")
    tok_rows, width = tokens.shape[1], tokens.shape[2]
    head_dim = width // HEADS
    heads = HEADS // seq_count
    cols = width // seq_count
    wrows = w_query.shape[0]
    length = tok_rows * seq_count
    experts_local = w_gate.shape[0]
    total_experts = experts_local * group_count
    slots = MOST
    score_scale = head_dim ** (-0.5)
    half = head_dim // 2
    inverse = 10000.0 ** (-jnp.arange(half, dtype=F32) / half)
    frequency = jnp.concatenate([inverse, inverse])[None]

    cot_all = lax.all_gather(cotangent[0], "expert", axis=0)
    w_rows = lax.all_gather(w_out, "expert", axis=0, tiled=True)
    wq_cols, wk_cols, wv_cols, normed_all, hits_all, cosine, sine, bias = gather_weights(
        w_query, w_key, w_value, tokens[0], gain_attn[None], routes[0], lengths, frequency
    )
    normed_all = normed_all.reshape(length, width)
    w_cols = [w.reshape(width, cols) for w in (wq_cols, wk_cols, wv_cols)]
    (hidden, normed2_all, query_low, key_low, value_low, attended_low, probs, query_unit, key_unit,
     scales) = attend(normed_all, *w_cols, w_rows, bias, cosine, sine, gain_query[None], gain_key[None],
                      tokens[0], gain_mlp[None])
    roomy = group_count * slots <= 512 and seq_count == 4
    if roomy:
        router_wide = jnp.concatenate(
            [router, jnp.zeros((width, 128 - total_experts), BF)], axis=1
        )
        grad_hidden, grad_low, small, out_parts, gate_sum, up_parts, down_parts = run_experts(
            normed2_all, cot_all, hits_all, router_wide, w_gate, w_up, w_down, hidden,
            cotangent[0], gain_mlp[None]
        )
        expert_parts = (up_parts, down_parts)
    else:
        normed2, mlp_norm_back = jax.vjp(rms_norm, hidden, gain_mlp)
        normed2_low = normed2.astype(BF)

        first_expert = group_me * experts_local
        hit = lax.dynamic_slice_in_dim(hits_all, first_expert, experts_local, axis=2)
        hit = hit.transpose(0, 2, 1)
        before = (jnp.arange(tok_rows)[:, None] < jnp.arange(tok_rows)[None, :]).astype(BF)
        rank = jnp.einsum("ejt,tu->eju", hit, before, preferred_element_type=F32)
        slot_ids = jnp.arange(slots, dtype=jnp.int32)
        chosen = (hit[:, :, None, :] > 0) & (rank.astype(jnp.int32)[:, :, None, :] == slot_ids[None, None, :, None])
        chosen_low = chosen.astype(BF)

        logits_all = jnp.einsum("etd,dn->etn", normed2_all, router, preferred_element_type=F32)
        probs_all = jax.nn.softmax(logits_all, axis=-1)
        mine = lax.dynamic_slice_in_dim(probs_all, first_expert, experts_local, axis=2)
        gate_rows = jnp.einsum(
            "ejmt,etj->jem", chosen.astype(F32), mine, precision=lax.Precision.HIGHEST
        )[..., None]

        grad_normed2, grad_probs, out_parts, d_w_gate, d_w_up, d_w_down = plain_experts(
            normed2_all, cot_all, chosen, gate_rows, w_gate, w_up, w_down
        )
        expert_parts = ()
        router_probs, softmax_back = jax.vjp(
            partial(jax.nn.softmax, axis=-1), product(normed2_low, router)
        )
        (grad_logits,) = softmax_back(grad_probs)
        grad_logits_low = grad_logits.astype(BF)
        grad_router = jnp.einsum("td,te->ed", normed2_low, grad_logits_low, preferred_element_type=F32)
        grad_normed2 = grad_normed2 + jnp.einsum(
            "te,de->td", grad_logits_low, router, preferred_element_type=F32
        )
        grad_hidden_part, grad_gain_mlp = mlp_norm_back(grad_normed2)
        grad_hidden = cotangent[0].astype(F32) + grad_hidden_part
        grad_low = grad_hidden.astype(BF)
        spare = -(total_experts + 1) % 8
        small = jnp.concatenate([grad_router, grad_gain_mlp[None], jnp.zeros((spare, width), F32)])

    out_sum = lax.psum_scatter(out_parts, "expert", scatter_dimension=0, tiled=False)

    d_tokens, d_w_query, d_w_key, d_w_value, d_w_out, small, *crossed = finish_all(
        (grad_low, grad_hidden, tokens[0], gain_attn[None], w_rows, query_low,
         key_low, value_low, attended_low, probs, query_unit, key_unit, scales,
         gain_query[None], gain_key[None], cosine, sine, normed_all, *w_cols, small),
        expert_parts,
    )
    out_sum = after(out_sum, d_w_out)
    if roomy:
        (d_w_gate, d_w_up, d_w_down, mixed, d_tokens, d_w_query, d_w_key, d_w_value,
         d_w_out) = add_up(
            seq_me.astype(jnp.int32)[None], gate_sum,
            up_parts, crossed[0], crossed[1], down_parts, crossed[2], crossed[3],
            hidden, out_sum, d_tokens, d_w_query, d_w_key, d_w_value, d_w_out,
        )
        d_w_gate = d_w_gate.reshape(experts_local, width // seq_count, -1)
        d_w_up = d_w_up.reshape(d_w_gate.shape)
        d_w_down = d_w_down.reshape(experts_local, -1, width)
    else:
        mixed = (hidden + out_sum.astype(F32)).astype(BF)
    return (
        mixed[None],
        d_tokens[None],
        small[-6],
        d_w_query,
        d_w_key,
        d_w_value,
        small[-8],
        small[-7],
        d_w_out,
        small[total_experts],
        small[:total_experts].T,
        d_w_gate,
        d_w_up,
        d_w_down,
    )


def solution(mesh):
    return jax.shard_map(
        local,
        mesh=mesh,
        in_specs=(
            P("expert", "seq", None),
            P("expert", None),
            P("expert", "seq", None),
            P(),
            P(("seq", "expert"), None),
            P(("seq", "expert"), None),
            P(("seq", "expert"), None),
            P(),
            P(),
            P(("seq", "expert"), None),
            P(),
            P(),
            P("expert", None, None),
            P("expert", None, None),
            P("expert", None, None),
            P("expert", "seq", None),
        ),
        out_specs=(
            P("expert", "seq", None),
            P("expert", "seq", None),
            P(),
            P(("seq", "expert"), None),
            P(("seq", "expert"), None),
            P(("seq", "expert"), None),
            P(),
            P(),
            P(("seq", "expert"), None),
            P(),
            P(),
            P("expert", "seq", None),
            P("expert", "seq", None),
            P("expert", "seq", None),
        ),
        check_vma=False,
    )
```
